32 devices in a mesh: face: 1, tile: 32 (over z, y, x, core).
Axes of the slice: x: 2, y: 2, z: 4, core: 2. Of those that a mesh axis runs over, the one named last changes fastest.
Arguments:
- atmos_state: bfloat16 [32, 12, 256, 256], P(None, 'face', 'tile'), may hold values from -6 to 6
- land_sea: int32 [12, 256, 256], P('face', 'tile'), may hold values 0 or 1
- owners: int32 [3072, 1], P(('face', 'tile')), may hold values from 0 to 31; in each aligned block of 96 rows (0 to 95, 96 to 191, ...) at most 6 rows name the same one
- seam_table: int32 [48, 2], replicated, may hold values from 0 to 47, as said below
- ocean_state: float32 [1, 32, 192, 2, 256], P('face', 'tile'), may hold values from -6 to 6
- conv_input: bfloat16 [3, 64, 96], replicated, may hold values from -0.375 to 0.375
- conv_encode: bfloat16 [3, 64, 192], replicated, may hold values from -0.25 to 0.25
- conv_coarse: bfloat16 [3, 64, 192], replicated, may hold values from -0.25 to 0.25
- conv_decode: bfloat16 [3, 64, 384], replicated, may hold values from -0.1875 to 0.1875
- output_head: bfloat16 [12, 64], replicated, may hold values from -0.75 to 0.75
- ocean_in: float32 [64, 6], replicated, may hold values from -2.5 to 2.5
- ocean_out: float32 [64], replicated, may hold values from -0.75 to 0.75
Outputs:
- atmos_next: bfloat16 [8, 12, 256, 256], P(None, 'face', 'tile')
- ocean_next: float32 [1, 32, 192, 2, 256], P('face', 'tile')
The draws below stay inside these ranges and needn't reach their ends.
Inputs may be any that keep to these rules, and one draw needn't show every extreme that they name: `owners`: among the 96 tiles of one face group and stripe (an aligned block of rows) no owner appears more than 6 times, and that bound is reached in some block. `seam_table`: row 4 g + s describes side s of face g. Column 0 names the partner side 4 h + u; the pairing is an involution with no fixed points, and paired sides carry the same reversal flag in column 1 (0 or 1).
All inputs are finite; a program needn't handle non-finite values. No bound on the sum of `land_sea` on one device may be relied on, other than what follows from the above.
Results may differ from the reference program's by a relative error of at most 0.0028.
Values may be sent and summed in bfloat16 or wider, within the bound.
No kernel may reach another device: no remote copies, remote signals or barrier semaphores. Data moves between devices by JAX's collectives and lax.ppermute only.
A program may use at most 128 MiB of HBM per device.

```python
import math
import jax
import jax.numpy as jnp
import numpy as np
from jax import lax

WIDTH = 64
IN_CH = 32
OUT_VARS = 8
FLUX_CH = 4
OCEAN_CH = 2
OCEAN_HID = 64
FACES = 12
GROUPS = 1
STRIPES = 32
SIDE = 256
TILES_DEV = 96
SEND_CAP = 6
SLOTS = 192
ROUTE_ROWS = 3072


def draw_seam_table(key, part):
    base_key = jax.random.fold_in(key, 7)
    key_order, key_flip = jax.random.split(base_key)
    side_count = 4 * FACES
    shuffled = jax.random.permutation(key_order, side_count).astype(jnp.int32)
    paired = shuffled.reshape(side_count // 2, 2)
    flip_bits = jax.random.randint(key_flip, (side_count // 2,), 0, 2).astype(jnp.int32)
    partner = jnp.zeros((side_count,), jnp.int32).at[paired[:, 0]].set(paired[:, 1]).at[paired[:, 1]].set(paired[:, 0])
    reverse = jnp.zeros((side_count,), jnp.int32).at[paired[:, 0]].set(flip_bits).at[paired[:, 1]].set(flip_bits)
    return jnp.stack([partner, reverse], axis=1)


def set_ends(drawn, stream_key, least, largest):
    dims = drawn.shape
    index_at = [jax.random.randint(jax.random.fold_in(stream_key, axis), (), 0, dims[axis]) for axis in range(len(dims))]
    drawn = drawn.at[tuple(index_at)].set(least)
    longest = dims.index(max(dims))
    index_at[longest] = (index_at[longest] + 1) % dims[longest]
    return drawn.at[tuple(index_at)].set(largest)


def steps_of(own_key, shape, cuts, least, high):
    factor_of, own = 1.0, jax.random.fold_in(own_key, 6)
    for position, parts in cuts:
        draws = jnp.exp(jax.random.uniform(jax.random.fold_in(own, position), (parts,), jnp.float32, least / len(cuts), high / len(cuts)))
        factor_of = factor_of * jnp.repeat(draws, shape[position] // parts).reshape([-1 if axis == position else 1 for axis in range(len(shape))])
    return factor_of


def assign_block(stream_key, own, number, rows, count, top, bound, skew):
    ranking = jax.random.permutation(stream_key, count)
    heavy_load, common = portions_of(count, rows * top, bound, skew, True), portions_of(count, rows * top, bound, skew, False)
    places = jnp.arange(count)

    def named(tallies, offset_by):
        used = int((tallies > 0).sum())
        fixed = max(1, used // 4)
        passed = fixed + (places - fixed + offset_by * (used - fixed)) % max(1, count - fixed)
        return jnp.zeros((count,), jnp.int32).at[ranking[jnp.where(places < fixed, places, passed)]].set(jnp.asarray(tallies, jnp.int32))

    tallies = jnp.where(number % 4 == 0, named(heavy_load, number // 4), named(common, number - number // 4 - 1))
    mixed = jax.random.permutation(jax.random.fold_in(own, 3), count)
    giver, receiver = mixed[0:count // 2 * 2:2], mixed[1:count // 2 * 2:2]
    slack = jnp.minimum(tallies[giver] - 1, bound - tallies[receiver]) // 2
    slack = jnp.where((giver == ranking[0]) | (receiver == ranking[0]) | (tallies[receiver] == 0), 0, jnp.maximum(slack, 0))
    passed = jax.random.randint(jax.random.fold_in(own, 4), (count // 2,), 0, 1 << 20) % (slack + 1)
    tallies = tallies.at[giver].add(-passed).at[receiver].add(passed)
    items = jnp.searchsorted(jnp.cumsum(tallies), jnp.arange(rows * top), side="right").astype(jnp.int32)
    listing = items.reshape(top, rows).T
    listing = listing[jax.random.permutation(jax.random.fold_in(own, 1), rows)]
    offset_by = jax.random.randint(jax.random.fold_in(own, 2), (rows, 1), 0, top)
    return jnp.take_along_axis(listing, (jnp.arange(top)[None, :] + offset_by) % top, axis=1)


def portions_of(count, total, bound, lean, full):
    portions = [(1 << 20) // math.isqrt(standing ** lean) + 1 for standing in range(1, count + 1)]
    largest = bound if full else min(bound, max(-(-total // count), total * portions[0] // sum(portions)))
    least = 1 if total - largest >= count - 1 else 0
    given, surplus = [largest] + [least] * (count - 1), total - largest - least * (count - 1)
    while surplus > 0:
        candidates = [i for i in range(1, count) if given[i] < largest] or [i for i in range(1, count) if given[i] < bound]
        whole, left = sum([portions[i] for i in candidates]), surplus
        for i in candidates:
            addition = min(bound - given[i], max(1, left * portions[i] // whole), surplus)
            given[i] = given[i] + addition
            surplus = surplus - addition
    return np.array(given)


def noise(own_key, extent, width, reach, cuts=(), held_as=jnp.bfloat16):
    factor_of = steps_of(own_key, extent, cuts, -0.22, 0.18) if cuts else 1.0
    result = jax.random.normal(own_key, extent, jnp.float32) * width * factor_of
    return jnp.minimum(jnp.maximum(result, -reach), reach).astype(held_as)


def setup_inputs(seed: int = 0) -> dict:
    key_of = jax.random.split(jax.random.key(seed), 13)
    atmos_state = noise(key_of[0], (IN_CH, FACES, SIDE, SIDE), 1.0, 6.0, ((2, 32),))
    land_sea = set_ends((jax.random.randint(key_of[1], (FACES, SIDE, SIDE), 0, 10) < 7).astype(jnp.int32), jax.random.fold_in(key_of[1], 1), 0, 1)
    owners_keys = jax.random.split(jax.random.fold_in(key_of[2], 1), ROUTE_ROWS // TILES_DEV)
    owners_turns = jax.random.permutation(jax.random.fold_in(key_of[2], 3), ROUTE_ROWS // TILES_DEV)
    owners = jax.vmap(lambda own, number: assign_block(jax.random.fold_in(key_of[2], 2), own, number, TILES_DEV, STRIPES, 1, SEND_CAP, 2))(owners_keys, owners_turns).reshape((ROUTE_ROWS, 1))
    seam_table = draw_seam_table(jax.random.fold_in(key_of[12], 71), 0)
    ocean_state = noise(key_of[4], (GROUPS, STRIPES, SLOTS, OCEAN_CH, SIDE), 1.0, 6.0, ((1, 32),), jnp.float32)
    conv_input = noise(key_of[5], (3, WIDTH, 3 * IN_CH), (9 * IN_CH) ** -0.5, 0.375)
    conv_encode = noise(key_of[6], (3, WIDTH, 3 * WIDTH), (9 * WIDTH) ** -0.5, 0.25)
    conv_coarse = noise(key_of[7], (3, WIDTH, 3 * WIDTH), (9 * WIDTH) ** -0.5, 0.25)
    conv_decode = noise(key_of[8], (3, WIDTH, 6 * WIDTH), (18 * WIDTH) ** -0.5, 0.1875)
    output_head = noise(key_of[9], (OUT_VARS + FLUX_CH, WIDTH), WIDTH ** -0.5, 0.75)
    ocean_in = noise(key_of[10], (OCEAN_HID, OCEAN_CH + FLUX_CH), (OCEAN_CH + FLUX_CH) ** -0.5, 2.5, (), jnp.float32)
    ocean_out = noise(key_of[11], (OCEAN_HID,), OCEAN_HID ** -0.5, 0.75, (), jnp.float32)
    return {"atmos_state": atmos_state, "land_sea": land_sea, "owners": owners, "seam_table": seam_table, "ocean_state": ocean_state, "conv_input": conv_input, "conv_encode": conv_encode, "conv_coarse": conv_coarse, "conv_decode": conv_decode, "output_head": output_head, "ocean_in": ocean_in, "ocean_out": ocean_out}


def seam_pad(values, seam_table):
    channels, faces, face_side, _ = values.shape
    face_edges = jnp.stack([values[:, :, 0, :], values[:, :, face_side - 1, :], values[:, :, :, 0], values[:, :, :, face_side - 1]], axis=2)
    face_edges = face_edges.reshape(channels, faces * 4, face_side)
    strips = jnp.take(face_edges, seam_table[:, 0], axis=1)
    strips = jnp.where(seam_table[:, 1][None, :, None] == 1, strips[:, :, ::-1], strips)
    strips = strips.reshape(channels, faces, 4, face_side)
    padded = jnp.pad(values, ((0, 0), (0, 0), (1, 1), (1, 1)))
    padded = padded.at[:, :, 0, 1:face_side + 1].set(strips[:, :, 0])
    padded = padded.at[:, :, face_side + 1, 1:face_side + 1].set(strips[:, :, 1])
    padded = padded.at[:, :, 1:face_side + 1, 0].set(strips[:, :, 2])
    padded = padded.at[:, :, 1:face_side + 1, face_side + 1].set(strips[:, :, 3])
    return padded


def conv_layer(padded, weight):
    channels = padded.shape[0]
    face_side = padded.shape[2] - 2

    def one_face(face_index):
        face_plane = lax.dynamic_index_in_dim(padded, face_index, 1, keepdims=False)
        summed = jnp.zeros((weight.shape[1], face_side * face_side), jnp.float32)
        for row_shift in range(3):
            tap_rows = jnp.concatenate([face_plane[:, row_shift:row_shift + face_side, col_shift:col_shift + face_side] for col_shift in range(3)], axis=0)
            summed = summed + jnp.dot(weight[row_shift], tap_rows.reshape(3 * channels, face_side * face_side), preferred_element_type=jnp.float32)
        return jax.nn.gelu(summed).astype(jnp.bfloat16).reshape(-1, face_side, face_side)

    stacked = lax.map(one_face, jnp.arange(padded.shape[1]))
    return jnp.transpose(stacked, (1, 0, 2, 3))


def ocean_update(held_state, arrived_flux, ocean_in, ocean_out):
    stacked = jnp.concatenate([held_state, arrived_flux.astype(jnp.float32)], axis=1)
    hidden = jax.nn.gelu(jnp.einsum('hc,ncs->nhs', ocean_in, stacked, precision=lax.Precision.HIGHEST))
    sea_now = held_state[:, 0] + jnp.einsum('h,nhs->ns', ocean_out, hidden, precision=lax.Precision.HIGHEST)
    return jnp.stack([sea_now, held_state[:, 0]], axis=1)


def reference(atmos_state, land_sea, owners, seam_table, ocean_state, conv_input, conv_encode, conv_coarse, conv_decode, output_head, ocean_in, ocean_out):
    encoded = conv_layer(seam_pad(atmos_state, seam_table), conv_input)
    skip_level = conv_layer(seam_pad(encoded, seam_table), conv_encode)
    channels, faces, face_side, _ = skip_level.shape
    pooled = skip_level.astype(jnp.float32).reshape(channels, faces, face_side // 2, 2, face_side // 2, 2).mean(axis=(3, 5)).astype(jnp.bfloat16)
    coarse_out = conv_layer(seam_pad(pooled, seam_table), conv_coarse)
    widened = jnp.repeat(jnp.repeat(coarse_out, 2, axis=2), 2, axis=3)
    decoded = conv_layer(seam_pad(jnp.concatenate([skip_level, widened], axis=0), seam_table), conv_decode)
    head_out = jnp.dot(output_head, decoded.reshape(channels, -1), preferred_element_type=jnp.float32).reshape(-1, faces, face_side, face_side)
    predicted = atmos_state[:OUT_VARS].astype(jnp.float32) + head_out[:OUT_VARS]
    is_ocean = land_sea == 1
    fluxes = jnp.where(is_ocean[None], head_out[OUT_VARS:], 0.0).astype(jnp.bfloat16)
    faces_dev = faces // GROUPS
    stripe_rows = face_side // STRIPES
    tiles_dev = faces_dev * stripe_rows
    flux_tiles = fluxes.reshape(FLUX_CH, GROUPS, faces_dev, STRIPES, stripe_rows, face_side)
    flux_tiles = jnp.transpose(flux_tiles, (1, 3, 2, 4, 0, 5)).reshape(GROUPS, STRIPES, tiles_dev, FLUX_CH * face_side)
    owner_ids = owners.reshape(GROUPS, STRIPES, tiles_dev)
    slot_count = ocean_state.shape[2]
    capacity = slot_count // STRIPES
    owner_hits = (owner_ids[..., None] == jnp.arange(STRIPES)[None, None, None, :]).astype(jnp.int32)
    slot_rank = jnp.sum((jnp.cumsum(owner_hits, axis=2) - 1) * owner_hits, axis=3)
    slot_index = owner_ids * capacity + slot_rank
    selector = (slot_index[:, :, None, :] == jnp.arange(slot_count)[None, None, :, None]).astype(jnp.float32)
    outgoing = jnp.einsum('gtnk,gtkc->gtnc', selector, flux_tiles.astype(jnp.float32))
    outgoing = outgoing.reshape(GROUPS, STRIPES, STRIPES, capacity, FLUX_CH, face_side)
    arrived = jnp.transpose(outgoing, (0, 2, 1, 3, 4, 5)).reshape(GROUPS * STRIPES, slot_count, FLUX_CH, face_side).astype(jnp.bfloat16)
    held_blocks = ocean_state.reshape(GROUPS * STRIPES, slot_count, OCEAN_CH, face_side)
    renewed = lax.map(lambda pair: ocean_update(pair[0], pair[1], ocean_in, ocean_out), (held_blocks, arrived))
    renewed = renewed.reshape(GROUPS, STRIPES, slot_count, OCEAN_CH, face_side)
    sea_slots = renewed[:, :, :, 0, :].astype(jnp.bfloat16).reshape(GROUPS, STRIPES, STRIPES, capacity, face_side)
    returned = jnp.transpose(sea_slots, (0, 2, 1, 3, 4)).reshape(GROUPS, STRIPES, slot_count, face_side)
    sea_tiles = jnp.einsum('gtnk,gtns->gtks', selector, returned.astype(jnp.float32))
    sea_temp = sea_tiles.reshape(GROUPS, STRIPES, faces_dev, stripe_rows, face_side)
    sea_temp = jnp.transpose(sea_temp, (0, 2, 1, 3, 4)).reshape(faces, face_side, face_side)
    surface = jnp.where(is_ocean, sea_temp, predicted[0])
    atmos_next = jnp.concatenate([surface[None], predicted[1:]], axis=0).astype(jnp.bfloat16)
    return atmos_next, renewed
```

```python
import functools

import jax
import jax.numpy as jnp
import numpy as np
from jax import lax
from jax.experimental import pallas as pl
from jax.experimental.pallas import tpu as pltpu
from jax.sharding import PartitionSpec as P

OUT_VARS = 8
FLUX_CH = 4
OCEAN_CH = 2


def extended(shard, sides, width):
    for axis, dim in sides:
        size, length = (lax.axis_size(axis), shard.shape[dim])
        up = [(i, (i + 1) % size) for i in range(size)]
        down = [(j, i) for i, j in up]
        last = lax.slice_in_dim(shard, length - width, length, axis=dim)
        initial = lax.slice_in_dim(shard, 0, width, axis=dim)
        before = lax.ppermute(last, axis, up)
        after = lax.ppermute(initial, axis, down)
        shard = jnp.concatenate([before, shard, after], axis=dim)
    return shard


def pad_field(values, seam_table):
    channels, faces_dev, stripe_rows, face_side = values.shape
    tile_count = lax.axis_size("tile")
    stripe = lax.axis_index("tile")
    face_group = lax.axis_index("face")
    rimmed = extended(values, (("tile", 2),), 1)
    edge_rows = jnp.stack([values[:, :, 0, :], rimmed[:, :, 0, :]], axis=2)
    edge_pieces = edge_rows.reshape(channels, faces_dev, 2, tile_count, stripe_rows)
    received = lax.all_to_all(edge_pieces, "tile", split_axis=3, concat_axis=3, tiled=True)
    row_part = received[:, :, :, 0, :]
    row_start = stripe * stripe_rows
    col_part = jnp.stack([values[:, :, :, 0], values[:, :, :, face_side - 1]], axis=2)
    seam_piece = jnp.concatenate([row_part, col_part], axis=2)
    seam_piece = jnp.transpose(seam_piece, (1, 2, 0, 3)).reshape(
        1, faces_dev, 4, channels * stripe_rows
    )
    own_sides = lax.dynamic_slice_in_dim(seam_table, face_group * (faces_dev * 4), faces_dev * 4, 0)
    gathered = lax.all_gather(seam_piece, ("face", "tile"), axis=0, tiled=True)
    group_count = gathered.shape[0] // tile_count
    strip_table = gathered.reshape(group_count, tile_count, faces_dev, 4, channels, stripe_rows)
    strip_table = jnp.transpose(strip_table, (0, 2, 3, 4, 1, 5)).reshape(
        group_count * faces_dev * 4, channels, face_side
    )
    strips = jnp.take(strip_table, own_sides[:, 0], axis=0)
    strips = jnp.where(own_sides[:, 1][:, None, None] == 1, strips[:, :, ::-1], strips)
    strips = jnp.transpose(strips.reshape(faces_dev, 4, channels, face_side), (2, 0, 1, 3))
    upper_row = jnp.where(stripe == 0, strips[:, :, 0, :], rimmed[:, :, 0, :])
    bottom = jnp.where(
        stripe == tile_count - 1, strips[:, :, 1, :], rimmed[:, :, stripe_rows + 1, :]
    )
    middle = jnp.concatenate([upper_row[:, :, None, :], values, bottom[:, :, None, :]], axis=2)
    zero_cells = jnp.zeros((channels, faces_dev, 2, 1), values.dtype)
    columns = jnp.concatenate([zero_cells, strips[:, :, 2:, :], zero_cells], axis=3)
    columns = lax.dynamic_slice_in_dim(columns, row_start, stripe_rows + 2, 3)
    return jnp.concatenate([columns[:, :, 0, :, None], middle, columns[:, :, 1, :, None]], axis=3)


def convolve(padded, weight):
    channels, faces_dev, rows_two, side_two = padded.shape
    stripe_rows = rows_two - 2
    face_side = side_two - 2
    planes = []
    for face_index in range(faces_dev):
        summed = jnp.zeros((weight.shape[1], stripe_rows * face_side), jnp.float32)
        for row_shift in range(3):
            tap_rows = jnp.concatenate(
                [
                    padded[
                        :,
                        face_index,
                        row_shift : row_shift + stripe_rows,
                        col_shift : col_shift + face_side,
                    ]
                    for col_shift in range(3)
                ],
                axis=0,
            )
            summed = summed + jnp.dot(
                weight[row_shift],
                tap_rows.reshape(3 * channels, stripe_rows * face_side),
                preferred_element_type=jnp.float32,
            )
        planes.append(jax.nn.gelu(summed).astype(jnp.bfloat16).reshape(-1, stripe_rows, face_side))
    return jnp.stack(planes, axis=1)


def upsample(values):
    return jnp.repeat(jnp.repeat(values, 2, axis=2), 2, axis=3)


def ocean_update(held_state, arrived_flux, ocean_in, ocean_out):
    stacked = jnp.concatenate([held_state, arrived_flux.astype(jnp.float32)], axis=1)
    hidden = jax.nn.gelu(
        jnp.einsum("hc,ncs->nhs", ocean_in, stacked, precision=lax.Precision.HIGHEST)
    )
    sea_now = held_state[:, 0] + jnp.einsum(
        "h,nhs->ns", ocean_out, hidden, precision=lax.Precision.HIGHEST
    )
    return jnp.stack([sea_now, held_state[:, 0]], axis=1)


def ocean_blocks(held_state, arrived_flux, ocean_in, ocean_out, block_count):
    slot_count, state_ch, face_side = held_state.shape
    capacity = slot_count // block_count
    held_split = held_state.reshape(block_count, capacity, state_ch, face_side)
    flux_split = arrived_flux.reshape(block_count, capacity, arrived_flux.shape[1], face_side)
    stepped = lax.map(
        lambda pair: ocean_update(pair[0], pair[1], ocean_in, ocean_out), (held_split, flux_split)
    )
    return stepped.reshape(slot_count, state_ch, face_side)


def on_device(
    atmos_state,
    land_sea,
    owners,
    seam_table,
    ocean_state,
    conv_input,
    conv_encode,
    conv_coarse,
    conv_decode,
    output_head,
    ocean_in,
    ocean_out,
):
    encoded = convolve(pad_field(atmos_state, seam_table), conv_input)
    skip_level = convolve(pad_field(encoded, seam_table), conv_encode)
    channels, faces_dev, stripe_rows, face_side = skip_level.shape
    pooled = (
        skip_level.astype(jnp.float32)
        .reshape(channels, faces_dev, stripe_rows // 2, 2, face_side // 2, 2)
        .mean(axis=(3, 5))
        .astype(jnp.bfloat16)
    )
    coarse_out = convolve(pad_field(pooled, seam_table), conv_coarse)
    coarse_pad = upsample(pad_field(coarse_out, seam_table))[
        :, :, 1 : stripe_rows + 3, 1 : face_side + 3
    ]
    padded = jnp.concatenate([pad_field(skip_level, seam_table), coarse_pad], axis=0)
    decoded = convolve(padded, conv_decode)
    head_out = jnp.dot(
        output_head, decoded.reshape(channels, -1), preferred_element_type=jnp.float32
    )
    head_out = head_out.reshape(-1, faces_dev, stripe_rows, face_side)
    predicted = atmos_state[:OUT_VARS].astype(jnp.float32) + head_out[:OUT_VARS]
    is_ocean = land_sea == 1
    fluxes = jnp.where(is_ocean[None], head_out[OUT_VARS:], 0.0).astype(jnp.bfloat16)
    flux_tiles = jnp.transpose(fluxes, (1, 2, 0, 3)).reshape(
        faces_dev * stripe_rows, FLUX_CH * face_side
    )
    tile_count = lax.axis_size("tile")
    owner_ids = owners[:, 0]
    owner_hits = (owner_ids[:, None] == jnp.arange(tile_count)[None, :]).astype(jnp.int32)
    slot_rank = jnp.sum((jnp.cumsum(owner_hits, axis=0) - 1) * owner_hits, axis=1)
    slot_count = ocean_state.shape[2]
    capacity = slot_count // tile_count
    slot_index = owner_ids * capacity + slot_rank
    selector = (jnp.arange(slot_count)[:, None] == slot_index[None, :]).astype(jnp.bfloat16)
    outgoing = jnp.dot(selector, flux_tiles, preferred_element_type=jnp.float32).astype(
        jnp.bfloat16
    )
    outgoing = outgoing.reshape(tile_count, capacity, FLUX_CH, face_side)
    held_state = ocean_state[0, 0]
    arrived = lax.all_to_all(outgoing, "tile", split_axis=0, concat_axis=0, tiled=True)
    renewed = ocean_blocks(
        held_state, arrived.reshape(slot_count, FLUX_CH, face_side), ocean_in, ocean_out, tile_count
    )
    sea_back = renewed[:, 0].astype(jnp.bfloat16).reshape(tile_count, capacity, face_side)
    sea_slots = lax.all_to_all(sea_back, "tile", split_axis=0, concat_axis=0, tiled=True)
    sea_tiles = jnp.dot(
        selector.T, sea_slots.reshape(slot_count, face_side), preferred_element_type=jnp.float32
    )
    sea_temp = sea_tiles.reshape(faces_dev, stripe_rows, face_side)
    surface = jnp.where(is_ocean, sea_temp, predicted[0])
    atmos_next = jnp.concatenate([surface[None], predicted[1:]], axis=0).astype(jnp.bfloat16)
    return (atmos_next, renewed.reshape(1, 1, slot_count, OCEAN_CH, face_side))


GROUP = 16
LANES = 128
VMEM = pltpu.VMEM
BF = jnp.bfloat16
F32 = jnp.float32
NT = (((1,), (1,)), ((), ()))


def mm(a, b):
    return jnp.dot(a, b, preferred_element_type=F32)


def mm_nt(a, b):
    return lax.dot_general(a, b, NT, preferred_element_type=F32)


def iota(shape, dim):
    return lax.broadcasted_iota(jnp.int32, shape, dim)


def smooth(x):
    inner = x * (0.7978845608028654 + 0.03567740813636141 * (x * x))
    half = 0.5 * x
    return half * jnp.tanh(inner) + half


class Field:
    def __init__(self, faces, rows, chans, side, tiles):
        self.faces, self.rows, self.chans, self.side, self.tiles = faces, rows, chans, side, tiles
        self.per = LANES // chans
        self.groups = faces // self.per
        self.span = rows + 2
        used = self.groups * self.span
        self.chunk = used + (-used) % 16

    def main(self):
        return jax.ShapeDtypeStruct((self.faces, self.rows, self.chans, self.side), BF)

    def outs(self):
        edge = jax.ShapeDtypeStruct((self.faces, self.chans, self.side), BF)
        return [
            edge,
            edge,
            jax.ShapeDtypeStruct((2 * self.faces * 8, self.chans), BF),
            jax.ShapeDtypeStruct((self.tiles, self.chunk, LANES), BF),
        ]

    def send_scratch(self):
        return [
            pltpu.VMEM((2, self.faces, 8, self.chans), F32),
            pltpu.VMEM((self.tiles, self.chunk, LANES), F32),
            pltpu.VMEM((self.side + 8, LANES), F32),
        ]

    def halo_scratch(self):
        return [
            pltpu.VMEM((6, self.faces, GROUP, self.chans), F32),
            pltpu.VMEM((2, GROUP * GROUP, self.chans), F32),
            pltpu.VMEM((self.faces, self.chans, self.side), BF),
            pltpu.VMEM((self.faces, self.chans, self.side), BF),
            pltpu.VMEM((2, self.faces, self.chans, self.side), BF),
            pltpu.VMEM((self.tiles, self.chunk, LANES), F32),
        ]


def flip_matrix(size, flag):
    row, col = iota((size, size), 0), iota((size, size), 1)
    return (row == jnp.where(flag == 1, size - 1 - col, col)).astype(F32).astype(BF)


def edge_columns(fld, face_rows):
    row, col = iota((16, fld.side), 0), iota((16, fld.side), 1)
    total = jnp.zeros((16, fld.chans), F32)
    for r, cells in enumerate(face_rows):
        pick = ((row == r) & (col == 0)) | ((row == 8 + r) & (col == fld.side - 1))
        total = total + mm_nt(pick.astype(F32).astype(BF), cells)
    return total


def pack_sends(fld, stripe, tab, top, bot, ec_out, send_out, cols, stage, strip):
    last = fld.tiles - 1
    ec_out[...] = cols[...].reshape(2 * fld.faces * 8, fld.chans).astype(BF)
    stage[...] = jnp.zeros_like(stage)
    for q in range(2):
        for g in range(fld.faces):
            p = tab[4 * g + q, 0]
            kind, h = p % 4, p // 4
            piece = cols[jnp.maximum(kind - 2, 0), h]
            i, j = g // fld.per, g % fld.per
            stage[
                q * last,
                i * fld.span + 1 : i * fld.span + 1 + fld.rows,
                j * fld.chans : (j + 1) * fld.chans,
            ] = piece[: fld.rows]

    @pl.when((stripe == 0) | (stripe == last))
    def _():
        q = jnp.where(stripe == 0, 0, 1)
        for i in range(fld.groups):
            strip[...] = jnp.zeros_like(strip)
            for j in range(fld.per):
                h = i * fld.per + j
                cells = jnp.where(q == 0, top[h].astype(F32), bot[h].astype(F32)).astype(BF)
                turned = mm_nt(flip_matrix(fld.side, tab[4 * h + q, 1]), cells)
                strip[1 : fld.side + 1, j * fld.chans : (j + 1) * fld.chans] = turned
            for d in range(1, last):
                stage[d, i * fld.span : (i + 1) * fld.span, :] = strip[
                    d * fld.rows : d * fld.rows + fld.span, :
                ]

    send_out[...] = stage[...].astype(BF)


def gather_halos(fld, stripe, tab, x, up, dn, ec, ecm, ecf, ecl, recv, cand, cols, above, below, pair, got):
    faces, rows, chans, side, tiles = fld.faces, fld.rows, fld.chans, fld.side, fld.tiles
    last = tiles - 1
    got[...] = recv[...].astype(F32)
    own = ec[...].astype(F32).reshape(2, faces, 8, chans)
    row, col = iota((faces * 8, faces * 8), 0), iota((faces * 8, faces * 8), 1)
    turn = ((row // 8 == col // 8) & (row % 8 + col % 8 == rows - 1)).astype(F32).astype(BF)
    first = ecf[...].astype(F32).reshape(2, faces, 8, chans)
    final = ecl[...].astype(F32).reshape(2, faces, 8, chans)
    prow, pcol = iota((16, side), 0), iota((16, side), 1)
    ends = ((prow == 0) & (pcol == 0)) | ((prow == 1) & (pcol == side - 1))
    ends = ends.astype(F32).astype(BF)
    for h in range(faces):
        over, under = mm_nt(ends, up[h]), mm_nt(ends, dn[h])
        for s in range(2):
            cand[2 + s, h, 0:1] = over[s : s + 1]
            cand[2 + s, h, rows + 1 : rows + 2] = under[s : s + 1]
            cand[2 + s, h, 1 : rows + 1] = own[s, h, :rows]
    for s in range(2):
        turned = mm(turn, ecm[s * faces * 8 : (s + 1) * faces * 8, :]).reshape(faces, 8, chans)
        for h in range(faces):
            cand[4 + s, h, 0:1] = first[s, h, 0:1]
            cand[4 + s, h, rows + 1 : rows + 2] = final[s, h, rows - 1 : rows]
            cand[4 + s, h, 1 : rows + 1] = turned[h, :rows]
    above[...] = up[...]
    below[...] = dn[...]
    at_edge = (stripe == 0) | (stripe == last)

    @pl.when(jnp.logical_not(at_edge))
    def _():
        for q in range(2):
            for h in range(faces):
                i, j = h // fld.per, h % fld.per
                cand[q, h, 0 : fld.span] = got[
                    q * last,
                    i * fld.span : (i + 1) * fld.span,
                    j * chans : (j + 1) * chans,
                ]

    @pl.when(at_edge)
    def _():
        q = jnp.where(stripe == 0, 0, 1)
        for h in range(faces):
            pair[0, h] = jnp.where(q == 0, x[h, 0].astype(F32), dn[h].astype(F32)).astype(BF)
            pair[1, h] = jnp.where(q == 0, up[h].astype(F32), x[h, rows - 1].astype(F32)).astype(BF)
        place = stripe * rows - 1 + prow
        inside = (place >= 0) & (place < side)
        for s in range(2):
            for h in range(faces):
                want = jnp.where(tab[4 * h + s, 1] == 1, side - 1 - place, place)
                window = ((pcol == want) & inside).astype(F32).astype(BF)
                cand[s, h] = mm_nt(window, pair[s, h])
        for i in range(fld.groups):
            lined = jnp.concatenate(
                [got[d, i * fld.span + 1 : i * fld.span + 1 + rows, :] for d in range(tiles)], axis=0
            )
            lined = jnp.transpose(lined)
            for j in range(fld.per):
                g = i * fld.per + j
                p = tab[4 * g + q, 0]
                kind, h = p % 4, p // 4
                near = pair[jnp.minimum(kind, 1), h].astype(F32)
                far = lined[j * chans : (j + 1) * chans]
                cells = jnp.where(kind < 2, near, far).astype(BF)
                placed = mm(cells, flip_matrix(side, tab[4 * g + q, 1])).astype(BF)

                @pl.when(q == 0)
                def _():
                    above[g] = placed

                @pl.when(q == 1)
                def _():
                    below[g] = placed

    cols[...] = jnp.zeros_like(cols)
    slot = iota((GROUP, chans), 0)
    live = (slot < fld.span) & jnp.logical_not(
        ((slot == 0) & (stripe == 0)) | ((slot == rows + 1) & (stripe == last))
    )
    for s in range(2):
        for g in range(faces):
            p = tab[4 * g + 2 + s, 0]
            kind, h = p % 4, p // 4
            which = jnp.where((kind >= 2) & (tab[4 * g + 2 + s, 1] == 1), kind + 2, kind)
            cols[s, g * GROUP : (g + 1) * GROUP] = jnp.where(live, cand[which, h], 0.0)


def column_terms(side_weight, cols, out_ch):
    terms = []
    for s in range(2):
        part = mm_nt(side_weight[s], cols[s])
        size = part.shape[1]
        terms.append(
            part[out_ch : 2 * out_ch]
            + pltpu.roll(part[:out_ch], 1, 1)
            + pltpu.roll(part[2 * out_ch :], size - 1, 1)
        )
    return terms


def face_terms(terms, face_index):
    size = terms[0].shape[1]
    shift = lax.rem(2 * size - GROUP * face_index - 1, size)
    return [pltpu.roll(term, shift, 1)[:, :LANES] for term in terms]


def conv_row(weight, stacked, terms, r, out_ch):
    z = mm(weight, stacked)
    side = z.shape[1]
    left, right = pltpu.roll(z[:out_ch], 1, 1), pltpu.roll(z[2 * out_ch :], side - 1, 1)
    lane = iota((out_ch, LANES), 1)
    first = terms[0] if r == 0 else pltpu.roll(terms[0], LANES - r, 1)
    final = pltpu.roll(terms[1], LANES - 1 - r, 1)
    head = jnp.where(lane == 0, first, left[:, :LANES])
    tail = jnp.where(lane == LANES - 1, final, right[:, side - LANES :])
    if side > LANES:
        left = jnp.concatenate([head, left[:, LANES:]], axis=1)
        right = jnp.concatenate([right[:, : side - LANES], tail], axis=1)
    else:
        left, right = head, tail
    return smooth(z[out_ch : 2 * out_ch] + left + right).astype(BF)


def row_stack(x, above, below, f, rows):
    lines = [above[f]] + [x[f, r] for r in range(rows)] + [below[f]]
    return lambda r: lines[r : r + 3]


def prep_kernel(fld, stripe_ref, tab, atmos, perm, x_out, top, bot, ec_out, send_out, cols, stage, strip):
    stripe = stripe_ref[0]

    def one_face(f, carry):
        block = atmos[:, f].astype(F32).reshape(fld.chans * fld.rows, fld.side).astype(BF)
        moved = mm(perm[...], block).astype(BF)
        lines = [moved[r * fld.chans : (r + 1) * fld.chans] for r in range(fld.rows)]
        for r in range(fld.rows):
            x_out[f, r] = lines[r]
        top[f] = lines[0]
        bot[f] = lines[-1]
        edges = edge_columns(fld, lines)
        cols[0, f] = edges[:8]
        cols[1, f] = edges[8:]
        return carry

    lax.fori_loop(0, fld.faces, one_face, 0)
    pack_sends(fld, stripe, tab, top, bot, ec_out, send_out, cols, stage, strip)


def level_kernel(fld, out_fld, stripe_ref, tab, x, up, dn, ec, ecm, ecf, ecl, recv, weight, side_weight, *refs):
    outs, sends, halos = refs[:5], refs[5:8], refs[8:]
    x_out, top, bot, ec_out, send_out = outs
    stripe = stripe_ref[0]
    gather_halos(fld, stripe, tab, x, up, dn, ec, ecm, ecf, ecl, recv, *halos)
    _, cols, above, below = halos[:4]
    terms = column_terms(side_weight, [cols[0].astype(BF), cols[1].astype(BF)], out_fld.chans)

    def one_face(f, carry):
        lines = row_stack(x, above, below, f, fld.rows)
        ends = face_terms(terms, f)
        made = []
        for r in range(fld.rows):
            cells = conv_row(
                weight[...], jnp.concatenate(lines(r), axis=0), ends, r, out_fld.chans
            )
            x_out[f, r] = cells
            made.append(cells)
        top[f] = made[0]
        bot[f] = made[-1]
        edges = edge_columns(out_fld, made)
        sends[0][0, f] = edges[:8]
        sends[0][1, f] = edges[8:]
        return carry

    lax.fori_loop(0, fld.faces, one_face, 0)
    pack_sends(out_fld, stripe, tab, top, bot, ec_out, send_out, *sends)


def encode_kernel(fld, out_fld, low, stripe_ref, tab, x, up, dn, ec, ecm, ecf, ecl, recv, weight, side_weight, pool, *refs):
    outs, low_outs, sends, low_sends, halos = refs[:5], refs[5:10], refs[10:13], refs[13:16], refs[16:]
    x_out, top, bot, ec_out, send_out = outs
    y_out, low_top, low_bot, low_ec, low_send = low_outs
    stripe = stripe_ref[0]
    gather_halos(fld, stripe, tab, x, up, dn, ec, ecm, ecf, ecl, recv, *halos)
    _, cols, above, below = halos[:4]
    terms = column_terms(side_weight, [cols[0].astype(BF), cols[1].astype(BF)], out_fld.chans)

    def one_face(f, carry):
        lines = row_stack(x, above, below, f, fld.rows)
        ends = face_terms(terms, f)
        made, pooled = [], []
        for r in range(fld.rows):
            cells = conv_row(
                weight[...], jnp.concatenate(lines(r), axis=0), ends, r, out_fld.chans
            )
            x_out[f, r] = cells
            made.append(cells)
            if r % 2 == 1:
                mean = (mm(made[r - 1], pool[...]) + mm(cells, pool[...])).astype(BF)
                y_out[f, r // 2] = mean
                pooled.append(mean)
        top[f] = made[0]
        bot[f] = made[-1]
        edges = edge_columns(out_fld, made)
        sends[0][0, f] = edges[:8]
        sends[0][1, f] = edges[8:]
        low_top[f] = pooled[0]
        low_bot[f] = pooled[-1]
        edges = edge_columns(low, pooled)
        low_sends[0][0, f] = edges[:8]
        low_sends[0][1, f] = edges[8:]
        return carry

    lax.fori_loop(0, fld.faces, one_face, 0)
    pack_sends(low, stripe, tab, low_top, low_bot, low_ec, low_send, *low_sends)
    pack_sends(out_fld, stripe, tab, top, bot, ec_out, send_out, *sends)


def decode_kernel(fld, low, out_ch, vars_out, stripe_ref, tab, x, up, dn, ec, ecm, ecf, ecl, recv, y, yup, ydn, yec, yecm, yecf, yecl, yrecv, weight, side_weight, spread, head, atmos, land, row_key, col_key, pred_out, flux_out, *refs):
    halos, low_halos, flux = refs[:6], refs[6:12], refs[12]
    stripe = stripe_ref[0]
    gather_halos(low, stripe, tab, y, yup, ydn, yec, yecm, yecf, yecl, yrecv, *low_halos)
    gather_halos(fld, stripe, tab, x, up, dn, ec, ecm, ecf, ecl, recv, *halos)
    _, cols, above, below = halos[:4]
    _, low_cols, low_above, low_below = low_halos[:4]
    size = GROUP * GROUP
    row, col = iota((size, size), 0), iota((size, size), 1)
    widen = (col == (row // GROUP) * GROUP + (row % GROUP + 1) // 2).astype(F32).astype(BF)
    joined = []
    for s in range(2):
        wide = mm(widen, low_cols[s].astype(BF))
        joined.append(jnp.concatenate([cols[s], wide], axis=1).astype(BF))
    terms = column_terms(side_weight, joined, out_ch)

    def one_face(f, carry):
        lines = row_stack(x, above, below, f, fld.rows)
        ends = face_terms(terms, f)
        low_lines = [low_above[f]] + [y[f, r] for r in range(low.rows)] + [low_below[f]]
        wide = [mm(cells, spread[...]).astype(BF) for cells in low_lines]
        made = []
        for r in range(fld.rows):
            picked = [wide[(r + a + 1) // 2] for a in range(3)]
            made.append(
                conv_row(weight[...], jnp.concatenate(lines(r) + picked, axis=0), ends, r, out_ch)
            )
        result = mm(head[...], jnp.concatenate(made, axis=0)).reshape(-1, fld.rows, fld.side)
        pred_out[:, f] = (atmos[:, f].astype(F32) + result[:vars_out]).astype(BF)
        sea = land[f] == 1
        flux[:, f] = jnp.where(sea[None], result[vars_out:], 0.0)
        return carry

    lax.fori_loop(0, fld.faces, one_face, 0)
    chosen = (row_key[...] == col_key[...]).astype(F32).astype(BF)
    tiles = flux[...].reshape(-1, fld.side).astype(BF)
    flux_out[...] = mm(chosen, tiles).astype(BF).reshape(flux_out.shape)


def ocean_kernel(cap, recv, state, into, out_weight, sea_out, back_out):
    tiles, _, side = recv.shape

    def one_source(t, carry):
        flux = recv[t].astype(F32)
        pad = (-flux.shape[0]) % 16
        flux = jnp.concatenate([flux, jnp.zeros((pad, side), F32)], axis=0).astype(BF)
        held = state[t]
        high = held.astype(BF)
        low = (held - high.astype(F32)).astype(BF)
        hidden = smooth(mm(into[...], jnp.concatenate([flux, flux, high, high, low], axis=0)))
        width = out_weight[...]
        wide = jnp.concatenate([width] * (side // LANES), axis=1)
        drift = (hidden * wide).reshape(cap, -1, side).sum(axis=1)
        drift = jnp.concatenate([drift, jnp.zeros((8 - cap, side), F32)], axis=0)
        sea = held[:8] + drift
        sea_out[t] = sea
        back_out[t] = sea.astype(BF)
        return carry

    lax.fori_loop(0, tiles, one_source, 0)


def surface_kernel(back, key, land, pred, out):
    faces, rows, side = land.shape
    slots = back[...].astype(F32).reshape(-1, side).astype(BF)
    chosen = (key[...] == iota((faces * rows, slots.shape[0]), 1)).astype(F32).astype(BF)
    sea = mm(chosen, slots).reshape(faces, rows, side)
    out[0] = jnp.where(land[...] == 1, sea, pred[0].astype(F32)).astype(BF)


def call(kernel, outs, ins, scratch, flops, smem=0, specs=None, aliases=None, out_specs=None, name=None):
    whole = pl.BlockSpec(memory_space=pltpu.VMEM)
    in_specs = [pl.BlockSpec(memory_space=pltpu.SMEM)] * smem + [whole] * (len(ins) - smem)
    for position, spec in (specs or {}).items():
        in_specs[position] = spec
    grid = {"grid": (1,)} if specs else {}
    moved = sum(int(np.prod(a.shape)) * a.dtype.itemsize for a in list(ins) + list(outs))
    return pl.pallas_call(
        kernel,
        out_shape=outs,
        **grid,
        in_specs=in_specs,
        out_specs=out_specs or [whole] * len(outs),
        scratch_shapes=scratch,
        input_output_aliases=aliases or {},
        compiler_params=pltpu.CompilerParams(vmem_limit_bytes=56 * 1024 * 1024),
        cost_estimate=pl.CostEstimate(flops=int(flops), bytes_accessed=int(moved), transcendentals=0),
        name=name,
    )(*ins)


def exchange(fld, top, bot, ec, send):
    tiles = fld.tiles

    def move(values, to):
        return lax.ppermute(values, "tile", [(i, to(i) % tiles) for i in range(tiles)])

    return (
        move(bot, lambda i: i + 1),
        move(top, lambda i: i - 1),
        ec,
        move(ec, lambda i: tiles - 1 - i),
        move(ec, lambda i: tiles - i),
        move(ec, lambda i: tiles - 2 - i),
        lax.all_to_all(send, "tile", split_axis=0, concat_axis=0, tiled=True),
    )


def packed_weight(weight, chans):
    taps, out_ch, _ = weight.shape
    split = weight.reshape(taps, out_ch, taps, chans)
    body = jnp.transpose(split, (2, 1, 0, 3)).reshape(taps * out_ch, taps * chans)
    sides = jnp.stack([split[:, :, 0], split[:, :, 2]]).reshape(2, taps * out_ch, chans)
    return body, sides


def on_one_group(
    atmos_state,
    land_sea,
    owners,
    seam_table,
    ocean_state,
    conv_input,
    conv_encode,
    conv_coarse,
    conv_decode,
    output_head,
    ocean_in,
    ocean_out,
):
    in_ch, faces, rows, side = atmos_state.shape
    tiles = lax.axis_size("tile")
    width = conv_input.shape[1]
    stripe = lax.axis_index("tile").astype(jnp.int32).reshape(1)
    entry = Field(faces, rows, in_ch, side, tiles)
    full = Field(faces, rows, width, side, tiles)
    low = Field(faces, rows // 2, width, side // 2, tiles)
    cells = faces * rows * side

    order = np.arange(in_ch * rows)
    perm = np.zeros((in_ch * rows, in_ch * rows), np.float32)
    perm[order, (order % in_ch) * rows + order // in_ch] = 1.0
    spread = np.zeros((side // 2, side), np.float32)
    spread[np.arange(side) // 2, np.arange(side)] = 1.0
    perm, pool = jnp.asarray(perm, BF), jnp.asarray(0.25 * spread.T, BF)
    spread = jnp.asarray(spread, BF)

    x0, *edges = call(
        functools.partial(prep_kernel, entry),
        [entry.main()] + entry.outs(),
        (stripe, seam_table, atmos_state, perm),
        entry.send_scratch(),
        2 * cells * in_ch * in_ch * rows,
        smem=2,
        name="prep",
    )
    moved = exchange(entry, *edges)
    body, sides = packed_weight(conv_input, in_ch)
    x1, *edges = call(
        functools.partial(level_kernel, entry, full),
        [full.main()] + full.outs(),
        (stripe, seam_table, x0) + moved + (body, sides),
        full.send_scratch() + entry.halo_scratch(),
        2 * cells * 9 * in_ch * width,
        smem=2,
        name="conv_in",
    )
    moved = exchange(full, *edges)
    body, sides = packed_weight(conv_encode, width)
    made = call(
        functools.partial(encode_kernel, full, full, low),
        [full.main()] + full.outs() + [low.main()] + low.outs(),
        (stripe, seam_table, x1) + moved + (body, sides, pool),
        full.send_scratch() + low.send_scratch() + full.halo_scratch(),
        2 * cells * 9 * width * width,
        smem=2,
        name="encode",
    )
    x2, *edges = made[:5]
    y0, *low_edges = made[5:]
    low_moved = exchange(low, *low_edges)
    moved = exchange(full, *edges)
    body, sides = packed_weight(conv_coarse, width)
    y1, *low_edges = call(
        functools.partial(level_kernel, low, low),
        [low.main()] + low.outs(),
        (stripe, seam_table, y0) + low_moved + (body, sides),
        low.send_scratch() + low.halo_scratch(),
        2 * cells * 9 * width * width // 4,
        smem=2,
        name="coarse",
    )
    low_moved = exchange(low, *low_edges)

    taps = conv_decode.shape[0]
    split = conv_decode.reshape(taps, width, taps, 2, width)
    body = jnp.transpose(split, (2, 1, 3, 0, 4)).reshape(taps * width, 2 * taps * width)
    sides = jnp.stack([split[:, :, 0], split[:, :, 2]]).reshape(2, taps * width, 2 * width)
    heads = output_head.shape[0]
    flux_ch = heads - OUT_VARS
    eye = jnp.eye(rows, dtype=output_head.dtype)
    head = (output_head[:, None, None, :] * eye[None, :, :, None]).reshape(heads * rows, rows * width)

    slot_count = ocean_state.shape[2]
    cap = slot_count // tiles
    owner_ids = owners[:, 0]
    count = owner_ids.shape[0]
    earlier = np.tril(np.ones((count, count), bool), -1)
    rank = jnp.sum((owner_ids[:, None] == owner_ids[None, :]) & earlier, axis=1).astype(jnp.int32)
    slot_index = owner_ids * cap + rank
    col_key = (np.arange(flux_ch, dtype=np.int32)[:, None] * slot_count + slot_index[None, :]).reshape(1, -1)
    row_key = (
        np.arange(flux_ch, dtype=np.int32)[None, :, None] * slot_count
        + np.arange(slot_count, dtype=np.int32).reshape(tiles, 1, cap)
    ).reshape(-1, 1)
    row_key = jnp.asarray(row_key)
    pred, outgoing = call(
        functools.partial(decode_kernel, full, low, width, OUT_VARS),
        [
            jax.ShapeDtypeStruct((OUT_VARS, faces, rows, side), BF),
            jax.ShapeDtypeStruct((tiles, flux_ch * cap, side), BF),
        ],
        (stripe, seam_table, x2)
        + moved
        + (y1,)
        + low_moved
        + (body, sides, spread, head, atmos_state, land_sea, row_key, col_key),
        full.halo_scratch() + low.halo_scratch() + [pltpu.VMEM((flux_ch, faces, rows, side), F32)],
        2 * cells * 18 * width * width,
        smem=2,
        specs={22: pl.BlockSpec((OUT_VARS, faces, rows, side), lambda i: (0, 0, 0, 0))},
        name="decode",
    )
    arrived = lax.all_to_all(outgoing, "tile", split_axis=0, concat_axis=0, tiled=True)

    held = jnp.transpose(ocean_state[0, 0].reshape(tiles, cap, OCEAN_CH, side), (0, 2, 1, 3))
    state = jnp.pad(held, ((0, 0), (0, 0), (0, 8 - cap), (0, 0))).reshape(tiles, OCEAN_CH * 8, side)
    hidden = ocean_in.shape[0]
    high = ocean_in.astype(BF)
    rest = (ocean_in - high.astype(F32)).astype(BF)
    flux_pad = (-flux_ch * cap) % 16
    each = jnp.eye(cap, dtype=BF)
    slot8 = jnp.eye(cap, 8, dtype=BF)

    def flux_part(weights):
        part = each[:, None, None, :] * weights[None, :, OCEAN_CH:, None]
        return jnp.pad(part.reshape(cap * hidden, flux_ch * cap), ((0, 0), (0, flux_pad)))

    def state_part(weights):
        part = slot8[:, None, None, :] * weights[None, :, :OCEAN_CH, None]
        return part.reshape(cap * hidden, OCEAN_CH * 8)

    into = jnp.concatenate(
        [flux_part(high), flux_part(rest), state_part(high), state_part(rest), state_part(high)], axis=1
    )
    out_weight = jnp.broadcast_to(ocean_out[None, :, None], (cap, hidden, LANES)).reshape(-1, LANES)
    sea, back = call(
        functools.partial(ocean_kernel, cap),
        [jax.ShapeDtypeStruct((tiles, 8, side), F32), jax.ShapeDtypeStruct((tiles, 8, side), BF)],
        (arrived, state, into, out_weight),
        [],
        2 * slot_count * side * hidden * 8,
        name="ocean",
    )
    returned = lax.all_to_all(back, "tile", split_axis=0, concat_axis=0, tiled=True)
    key = (owner_ids * 8 + rank)[:, None]
    first = pl.BlockSpec((1, faces, rows, side), lambda i: (0, 0, 0, 0))
    (atmos_next,) = call(
        surface_kernel,
        [jax.ShapeDtypeStruct(pred.shape, BF)],
        (returned, key, land_sea, pred),
        [],
        2 * count * tiles * 8 * side,
        specs={3: first},
        out_specs=[first],
        aliases={3: 0},
        name="surface",
    )
    renewed = jnp.stack([sea[:, :cap], held[:, 0]], axis=2)
    return atmos_next, renewed.reshape(1, 1, slot_count, OCEAN_CH, side)


def fits(mesh):
    return mesh.shape["face"] == 1


def solution(mesh):
    in_specs = (
        P(None, "face", "tile", None),
        P("face", "tile", None),
        P(("face", "tile"), None),
        P(),
        P("face", "tile", None, None, None),
        P(),
        P(),
        P(),
        P(),
        P(),
        P(),
        P(),
    )
    out_specs = (P(None, "face", "tile", None), P("face", "tile", None, None, None))
    return jax.shard_map(
        on_one_group if fits(mesh) else on_device,
        mesh=mesh,
        in_specs=in_specs,
        out_specs=out_specs,
        check_vma=False,
    )
```

```python
import functools

import jax
import jax.numpy as jnp
import numpy as np
from jax import lax
from jax.experimental import pallas as pl
from jax.experimental.pallas import tpu as pltpu
from jax.sharding import PartitionSpec as P

OUT_VARS = 8
FLUX_CH = 4
OCEAN_CH = 2


def extended(shard, sides, width):
    for axis, dim in sides:
        size, length = (lax.axis_size(axis), shard.shape[dim])
        up = [(i, (i + 1) % size) for i in range(size)]
        down = [(j, i) for i, j in up]
        last = lax.slice_in_dim(shard, length - width, length, axis=dim)
        initial = lax.slice_in_dim(shard, 0, width, axis=dim)
        before = lax.ppermute(last, axis, up)
        after = lax.ppermute(initial, axis, down)
        shard = jnp.concatenate([before, shard, after], axis=dim)
    return shard


def pad_field(values, seam_table):
    channels, faces_dev, stripe_rows, face_side = values.shape
    tile_count = lax.axis_size("tile")
    stripe = lax.axis_index("tile")
    face_group = lax.axis_index("face")
    rimmed = extended(values, (("tile", 2),), 1)
    edge_rows = jnp.stack([values[:, :, 0, :], rimmed[:, :, 0, :]], axis=2)
    edge_pieces = edge_rows.reshape(channels, faces_dev, 2, tile_count, stripe_rows)
    received = lax.all_to_all(edge_pieces, "tile", split_axis=3, concat_axis=3, tiled=True)
    row_part = received[:, :, :, 0, :]
    row_start = stripe * stripe_rows
    col_part = jnp.stack([values[:, :, :, 0], values[:, :, :, face_side - 1]], axis=2)
    seam_piece = jnp.concatenate([row_part, col_part], axis=2)
    seam_piece = jnp.transpose(seam_piece, (1, 2, 0, 3)).reshape(
        1, faces_dev, 4, channels * stripe_rows
    )
    own_sides = lax.dynamic_slice_in_dim(seam_table, face_group * (faces_dev * 4), faces_dev * 4, 0)
    gathered = lax.all_gather(seam_piece, ("face", "tile"), axis=0, tiled=True)
    group_count = gathered.shape[0] // tile_count
    strip_table = gathered.reshape(group_count, tile_count, faces_dev, 4, channels, stripe_rows)
    strip_table = jnp.transpose(strip_table, (0, 2, 3, 4, 1, 5)).reshape(
        group_count * faces_dev * 4, channels, face_side
    )
    strips = jnp.take(strip_table, own_sides[:, 0], axis=0)
    strips = jnp.where(own_sides[:, 1][:, None, None] == 1, strips[:, :, ::-1], strips)
    strips = jnp.transpose(strips.reshape(faces_dev, 4, channels, face_side), (2, 0, 1, 3))
    upper_row = jnp.where(stripe == 0, strips[:, :, 0, :], rimmed[:, :, 0, :])
    bottom = jnp.where(
        stripe == tile_count - 1, strips[:, :, 1, :], rimmed[:, :, stripe_rows + 1, :]
    )
    middle = jnp.concatenate([upper_row[:, :, None, :], values, bottom[:, :, None, :]], axis=2)
    zero_cells = jnp.zeros((channels, faces_dev, 2, 1), values.dtype)
    columns = jnp.concatenate([zero_cells, strips[:, :, 2:, :], zero_cells], axis=3)
    columns = lax.dynamic_slice_in_dim(columns, row_start, stripe_rows + 2, 3)
    return jnp.concatenate([columns[:, :, 0, :, None], middle, columns[:, :, 1, :, None]], axis=3)


def convolve(padded, weight):
    channels, faces_dev, rows_two, side_two = padded.shape
    stripe_rows = rows_two - 2
    face_side = side_two - 2
    planes = []
    for face_index in range(faces_dev):
        summed = jnp.zeros((weight.shape[1], stripe_rows * face_side), jnp.float32)
        for row_shift in range(3):
            tap_rows = jnp.concatenate(
                [
                    padded[
                        :,
                        face_index,
                        row_shift : row_shift + stripe_rows,
                        col_shift : col_shift + face_side,
                    ]
                    for col_shift in range(3)
                ],
                axis=0,
            )
            summed = summed + jnp.dot(
                weight[row_shift],
                tap_rows.reshape(3 * channels, stripe_rows * face_side),
                preferred_element_type=jnp.float32,
            )
        planes.append(jax.nn.gelu(summed).astype(jnp.bfloat16).reshape(-1, stripe_rows, face_side))
    return jnp.stack(planes, axis=1)


def upsample(values):
    return jnp.repeat(jnp.repeat(values, 2, axis=2), 2, axis=3)


def ocean_update(held_state, arrived_flux, ocean_in, ocean_out):
    stacked = jnp.concatenate([held_state, arrived_flux.astype(jnp.float32)], axis=1)
    hidden = jax.nn.gelu(
        jnp.einsum("hc,ncs->nhs", ocean_in, stacked, precision=lax.Precision.HIGHEST)
    )
    sea_now = held_state[:, 0] + jnp.einsum(
        "h,nhs->ns", ocean_out, hidden, precision=lax.Precision.HIGHEST
    )
    return jnp.stack([sea_now, held_state[:, 0]], axis=1)


def ocean_blocks(held_state, arrived_flux, ocean_in, ocean_out, block_count):
    slot_count, state_ch, face_side = held_state.shape
    capacity = slot_count // block_count
    held_split = held_state.reshape(block_count, capacity, state_ch, face_side)
    flux_split = arrived_flux.reshape(block_count, capacity, arrived_flux.shape[1], face_side)
    stepped = lax.map(
        lambda pair: ocean_update(pair[0], pair[1], ocean_in, ocean_out), (held_split, flux_split)
    )
    return stepped.reshape(slot_count, state_ch, face_side)


def on_device(
    atmos_state,
    land_sea,
    owners,
    seam_table,
    ocean_state,
    conv_input,
    conv_encode,
    conv_coarse,
    conv_decode,
    output_head,
    ocean_in,
    ocean_out,
):
    encoded = convolve(pad_field(atmos_state, seam_table), conv_input)
    skip_level = convolve(pad_field(encoded, seam_table), conv_encode)
    channels, faces_dev, stripe_rows, face_side = skip_level.shape
    pooled = (
        skip_level.astype(jnp.float32)
        .reshape(channels, faces_dev, stripe_rows // 2, 2, face_side // 2, 2)
        .mean(axis=(3, 5))
        .astype(jnp.bfloat16)
    )
    coarse_out = convolve(pad_field(pooled, seam_table), conv_coarse)
    coarse_pad = upsample(pad_field(coarse_out, seam_table))[
        :, :, 1 : stripe_rows + 3, 1 : face_side + 3
    ]
    padded = jnp.concatenate([pad_field(skip_level, seam_table), coarse_pad], axis=0)
    decoded = convolve(padded, conv_decode)
    head_out = jnp.dot(
        output_head, decoded.reshape(channels, -1), preferred_element_type=jnp.float32
    )
    head_out = head_out.reshape(-1, faces_dev, stripe_rows, face_side)
    predicted = atmos_state[:OUT_VARS].astype(jnp.float32) + head_out[:OUT_VARS]
    is_ocean = land_sea == 1
    fluxes = jnp.where(is_ocean[None], head_out[OUT_VARS:], 0.0).astype(jnp.bfloat16)
    flux_tiles = jnp.transpose(fluxes, (1, 2, 0, 3)).reshape(
        faces_dev * stripe_rows, FLUX_CH * face_side
    )
    tile_count = lax.axis_size("tile")
    owner_ids = owners[:, 0]
    owner_hits = (owner_ids[:, None] == jnp.arange(tile_count)[None, :]).astype(jnp.int32)
    slot_rank = jnp.sum((jnp.cumsum(owner_hits, axis=0) - 1) * owner_hits, axis=1)
    slot_count = ocean_state.shape[2]
    capacity = slot_count // tile_count
    slot_index = owner_ids * capacity + slot_rank
    selector = (jnp.arange(slot_count)[:, None] == slot_index[None, :]).astype(jnp.bfloat16)
    outgoing = jnp.dot(selector, flux_tiles, preferred_element_type=jnp.float32).astype(
        jnp.bfloat16
    )
    outgoing = outgoing.reshape(tile_count, capacity, FLUX_CH, face_side)
    held_state = ocean_state[0, 0]
    arrived = lax.all_to_all(outgoing, "tile", split_axis=0, concat_axis=0, tiled=True)
    renewed = ocean_blocks(
        held_state, arrived.reshape(slot_count, FLUX_CH, face_side), ocean_in, ocean_out, tile_count
    )
    sea_back = renewed[:, 0].astype(jnp.bfloat16).reshape(tile_count, capacity, face_side)
    sea_slots = lax.all_to_all(sea_back, "tile", split_axis=0, concat_axis=0, tiled=True)
    sea_tiles = jnp.dot(
        selector.T, sea_slots.reshape(slot_count, face_side), preferred_element_type=jnp.float32
    )
    sea_temp = sea_tiles.reshape(faces_dev, stripe_rows, face_side)
    surface = jnp.where(is_ocean, sea_temp, predicted[0])
    atmos_next = jnp.concatenate([surface[None], predicted[1:]], axis=0).astype(jnp.bfloat16)
    return (atmos_next, renewed.reshape(1, 1, slot_count, OCEAN_CH, face_side))


GROUP = 16
LANES = 128
VMEM = pltpu.VMEM
BF = jnp.bfloat16
F32 = jnp.float32
NT = (((1,), (1,)), ((), ()))


def mm(a, b):
    return jnp.dot(a, b, preferred_element_type=F32)


def mm_nt(a, b):
    return lax.dot_general(a, b, NT, preferred_element_type=F32)


def iota(shape, dim):
    return lax.broadcasted_iota(jnp.int32, shape, dim)


def smooth(x):
    inner = x * (0.7978845608028654 + 0.03567740813636141 * (x * x))
    half = 0.5 * x
    return half * jnp.tanh(inner) + half


class Field:
    def __init__(self, faces, rows, chans, side, tiles):
        self.faces, self.rows, self.chans, self.side, self.tiles = faces, rows, chans, side, tiles
        self.per = LANES // chans
        self.groups = faces // self.per
        self.span = rows + 2
        self.extra = self.groups * self.span
        used = max(self.extra + 2 * self.groups, 2 * self.groups * rows)
        self.chunk = used + (-used) % 16

    def main(self):
        return jax.ShapeDtypeStruct((self.faces, self.rows, self.chans, self.side), BF)

    def edges(self, more=0):
        edge = jax.ShapeDtypeStruct((self.faces, self.chans, self.side + more), BF)
        return [edge, edge]

    def sends(self):
        return [
            jax.ShapeDtypeStruct((2 * self.faces * 8, self.chans), BF),
            jax.ShapeDtypeStruct((self.tiles, self.chunk, LANES), BF),
        ]

    def send_scratch(self):
        return [
            pltpu.VMEM((2, self.faces, 8, self.chans), F32),
            pltpu.VMEM((self.tiles, self.chunk, LANES), F32),
            pltpu.VMEM((self.side + 8, LANES), F32),
        ]

    def halo_scratch(self):
        return [
            pltpu.VMEM((6, self.faces, GROUP, self.chans), F32),
            pltpu.VMEM((2, GROUP * GROUP, self.chans), F32),
            pltpu.VMEM((self.faces, self.chans, self.side), BF),
            pltpu.VMEM((self.faces, self.chans, self.side), BF),
            pltpu.VMEM((2, self.faces, self.chans, self.side), BF),
            pltpu.VMEM((self.tiles, self.chunk, LANES), F32),
            pltpu.VMEM((2, self.faces, 8, self.chans), F32),
        ]


def flip_matrix(size, flag):
    row, col = iota((size, size), 0), iota((size, size), 1)
    return (row == jnp.where(flag == 1, size - 1 - col, col)).astype(F32).astype(BF)


def end_picker(side):
    row, col = iota((16, side), 0), iota((16, side), 1)
    return (((row == 0) & (col == 0)) | ((row == 1) & (col == side - 1))).astype(F32).astype(BF)


def keep_columns(fld, face_rows, f, cols):
    picked = mm_nt(end_picker(fld.side), jnp.concatenate(face_rows, axis=0))
    for s in range(2):
        for r in range(fld.rows):
            cols[s, f, r : r + 1] = picked[s : s + 1, r * fld.chans : (r + 1) * fld.chans]


def pack_sends(fld, stripe, tab, top, bot, off, ec_out, send_out, cols, stage, strip):
    last, rows, chans = fld.tiles - 1, fld.rows, fld.chans
    ec_out[...] = cols[...].reshape(2 * fld.faces * 8, chans).astype(BF)
    stage[...] = jnp.zeros_like(stage)

    def lanes(h):
        return slice((h % fld.per) * chans, (h % fld.per + 1) * chans)

    for q in range(2):
        for g in range(fld.faces):
            p = tab[4 * g + q, 0]
            kind, h = p & 3, p >> 2
            piece = cols[jnp.maximum(kind - 2, 0), h]
            at = (g // fld.per) * fld.span + 1
            stage[q * last, at : at + rows, lanes(g)] = piece[:rows]

    @pl.when((stripe == 0) | (stripe == last))
    def _():
        q = jnp.where(stripe == 0, 0, 1)
        for i in range(fld.groups):
            strip[...] = jnp.zeros_like(strip)
            for j in range(fld.per):
                h = i * fld.per + j
                upper = top[h, :, off : off + fld.side].astype(F32)
                lower = bot[h, :, off : off + fld.side].astype(F32)
                cells = jnp.where(q == 0, upper, lower).astype(BF)
                turned = mm_nt(flip_matrix(fld.side, tab[4 * h + q, 1]), cells)
                strip[1 : fld.side + 1, lanes(h)] = turned
            for d in range(1, last):
                stage[d, i * fld.span : (i + 1) * fld.span, :] = strip[d * rows : d * rows + fld.span, :]

    for s in range(2):
        for h in range(fld.faces):
            at = (s * fld.groups + h // fld.per) * rows
            stage[last - stripe, at : at + rows, lanes(h)] = cols[s, h, :rows]

    @pl.when(stripe < last)
    def _():
        for s in range(2):
            for h in range(fld.faces):
                at = fld.extra + s * fld.groups + h // fld.per
                stage[last - 1 - stripe, at : at + 1, lanes(h)] = cols[s, h, rows - 1 : rows]

    @pl.when(stripe > 0)
    def _():
        for s in range(2):
            for h in range(fld.faces):
                at = fld.extra + s * fld.groups + h // fld.per
                stage[last + 1 - stripe, at : at + 1, lanes(h)] = cols[s, h, 0:1]

    send_out[...] = stage[...].astype(BF)


def gather_halos(fld, stripe, tab, x, up, dn, off, ec, recv, cand, cols, above, below, pair, got, mirror):
    faces, rows, chans, side, tiles = fld.faces, fld.rows, fld.chans, fld.side, fld.tiles
    last = tiles - 1
    groups = fld.groups
    got[...] = recv[...].astype(F32)
    own = ec[...].astype(F32).reshape(2, faces, 8, chans)
    row, col = iota((groups * rows, groups * rows), 0), iota((groups * rows, groups * rows), 1)
    turn = ((row // rows == col // rows) & (row % rows + col % rows == rows - 1)).astype(F32).astype(BF)
    prow, pcol = iota((16, side), 0), iota((16, side), 1)

    def lanes(h):
        return slice((h % fld.per) * chans, (h % fld.per + 1) * chans)

    above[...] = up[:, :, off : off + side]
    below[...] = dn[:, :, off : off + side]
    over = mm_nt(end_picker(side), above[...].reshape(faces * chans, side))
    under = mm_nt(end_picker(side), below[...].reshape(faces * chans, side))
    before = got[jnp.minimum(last + 1 - stripe, last), fld.extra : fld.extra + 2 * groups, :]
    after = got[jnp.maximum(last - 1 - stripe, 0), fld.extra : fld.extra + 2 * groups, :]
    for s in range(2):
        across = got[last - stripe, s * groups * rows : (s + 1) * groups * rows, :]
        turned = mm(turn, across.astype(BF))
        for h in range(faces):
            i = h // fld.per
            cand[2 + s, h, 0:1] = over[s : s + 1, h * chans : (h + 1) * chans]
            cand[2 + s, h, rows + 1 : rows + 2] = under[s : s + 1, h * chans : (h + 1) * chans]
            cand[2 + s, h, 1 : rows + 1] = own[s, h, :rows]
            mirror[s, h, :rows] = across[i * rows : (i + 1) * rows, lanes(h)]
            cand[4 + s, h, 0:1] = before[s * groups + i : s * groups + i + 1, lanes(h)]
            cand[4 + s, h, rows + 1 : rows + 2] = after[s * groups + i : s * groups + i + 1, lanes(h)]
            cand[4 + s, h, 1 : rows + 1] = turned[i * rows : (i + 1) * rows, lanes(h)]
    at_edge = (stripe == 0) | (stripe == last)

    @pl.when(jnp.logical_not(at_edge))
    def _():
        for q in range(2):
            for h in range(faces):
                i = h // fld.per
                cand[q, h, 0 : fld.span] = got[q * last, i * fld.span : (i + 1) * fld.span, lanes(h)]

    @pl.when(at_edge)
    def _():
        q = jnp.where(stripe == 0, 0, 1)
        for h in range(faces):
            pair[0, h] = jnp.where(q == 0, x[h, 0].astype(F32), below[h].astype(F32)).astype(BF)
            pair[1, h] = jnp.where(q == 0, above[h].astype(F32), x[h, rows - 1].astype(F32)).astype(BF)
        place = stripe * rows - 1 + prow
        inside = (place >= 0) & (place < side)
        for s in range(2):
            for h in range(faces):
                want = jnp.where(tab[4 * h + s, 1] == 1, side - 1 - place, place)
                window = ((pcol == want) & inside).astype(F32).astype(BF)
                cand[s, h] = mm_nt(window, pair[s, h])
        for g in range(faces):
            p = tab[4 * g + q, 0]
            at = (g // fld.per) * fld.span + 1
            piece = mirror[jnp.maximum((p & 3) - 2, 0), p >> 2]
            got[last - stripe, at : at + rows, lanes(g)] = piece[:rows]
        for i in range(groups):
            lined = jnp.concatenate(
                [got[d, i * fld.span + 1 : i * fld.span + 1 + rows, :] for d in range(tiles)], axis=0
            )
            lined = jnp.transpose(lined)
            for j in range(fld.per):
                g = i * fld.per + j
                p = tab[4 * g + q, 0]
                kind, h = p & 3, p >> 2
                near = pair[jnp.minimum(kind, 1), h].astype(F32)
                far = lined[j * chans : (j + 1) * chans]
                cells = jnp.where(kind < 2, near, far).astype(BF)
                placed = mm(cells, flip_matrix(side, tab[4 * g + q, 1])).astype(BF)

                @pl.when(q == 0)
                def _():
                    above[g] = placed

                @pl.when(q == 1)
                def _():
                    below[g] = placed

    cols[...] = jnp.zeros_like(cols)
    slot = iota((GROUP, chans), 0)
    live = (slot < fld.span) & jnp.logical_not(
        ((slot == 0) & (stripe == 0)) | ((slot == rows + 1) & (stripe == last))
    )
    for s in range(2):
        for g in range(faces):
            p = tab[4 * g + 2 + s, 0]
            kind, h = p & 3, p >> 2
            which = jnp.where((kind >= 2) & (tab[4 * g + 2 + s, 1] == 1), kind + 2, kind)
            cols[s, g * GROUP : (g + 1) * GROUP] = jnp.where(live, cand[which, h], 0.0)


def column_terms(side_weight, cols, out_ch):
    terms = []
    for s in range(2):
        part = mm_nt(side_weight[s], cols[s])
        size = part.shape[1]
        terms.append(
            part[out_ch : 2 * out_ch]
            + pltpu.roll(part[:out_ch], 1, 1)
            + pltpu.roll(part[2 * out_ch :], size - 1, 1)
        )
    return terms


def face_terms(terms, face_index):
    size = terms[0].shape[1]
    shift = lax.rem(2 * size - GROUP * face_index - 1, size)
    return [pltpu.roll(term, shift, 1)[:, :LANES] for term in terms]


def conv_row(weight, stacked, terms, r, out_ch):
    z = mm(weight, stacked)
    side = z.shape[1]
    left, right = pltpu.roll(z[:out_ch], 1, 1), pltpu.roll(z[2 * out_ch :], side - 1, 1)
    lane = iota((out_ch, LANES), 1)
    first = terms[0] if r == 0 else pltpu.roll(terms[0], LANES - r, 1)
    final = pltpu.roll(terms[1], LANES - 1 - r, 1)
    head = jnp.where(lane == 0, first, left[:, :LANES])
    tail = jnp.where(lane == LANES - 1, final, right[:, side - LANES :])
    if side > LANES:
        left = jnp.concatenate([head, left[:, LANES:]], axis=1)
        right = jnp.concatenate([right[:, : side - LANES], tail], axis=1)
    else:
        left, right = head, tail
    return smooth(z[out_ch : 2 * out_ch] + left + right).astype(BF)


def row_stack(x, above, below, f, rows):
    lines = [above[f]] + [x[f, r] for r in range(rows)] + [below[f]]
    return lambda r: lines[r : r + 3]


def prep_kernel(fld, stripe_ref, tab, atmos, perm, x_out, top, bot, ec_out, send_out, cols, stage, strip):
    stripe = stripe_ref[0]

    def one_face(f, carry):
        block = atmos[:, f].astype(F32).reshape(fld.chans * fld.rows, fld.side).astype(BF)
        moved = mm(perm[...], block).astype(BF)
        lines = [moved[r * fld.chans : (r + 1) * fld.chans] for r in range(fld.rows)]
        for r in range(fld.rows):
            x_out[f, r] = lines[r]
        top[f] = lines[0]
        bot[f] = lines[-1]
        keep_columns(fld, lines, f, cols)
        return carry

    lax.fori_loop(0, fld.faces, one_face, 0)
    pack_sends(fld, stripe, tab, top, bot, 0, ec_out, send_out, cols, stage, strip)


def level_kernel(fld, out_fld, off, stripe_ref, tab, x, up, dn, ec, recv, weight, side_weight, *refs):
    outs, sends, halos = refs[:5], refs[5:8], refs[8:]
    x_out, top, bot, ec_out, send_out = outs
    stripe = stripe_ref[0]
    gather_halos(fld, stripe, tab, x, up, dn, off, ec, recv, *halos)
    _, cols, above, below = halos[:4]
    terms = column_terms(side_weight, [cols[0].astype(BF), cols[1].astype(BF)], out_fld.chans)

    def one_face(f, carry):
        lines = row_stack(x, above, below, f, fld.rows)
        ends = face_terms(terms, f)
        made = []
        for r in range(fld.rows):
            cells = conv_row(
                weight[...], jnp.concatenate(lines(r), axis=0), ends, r, out_fld.chans
            )
            x_out[f, r] = cells
            made.append(cells)
        top[f] = made[0]
        bot[f] = made[-1]
        keep_columns(out_fld, made, f, sends[0])
        return carry

    lax.fori_loop(0, fld.faces, one_face, 0)
    pack_sends(out_fld, stripe, tab, top, bot, 0, ec_out, send_out, *sends)


def encode_kernel(fld, out_fld, low, stripe_ref, tab, x, up, dn, ec, recv, weight, side_weight, pool, *refs):
    outs, sends, low_sends, halos = refs[:8], refs[8:11], refs[11:14], refs[14:]
    x_out, y_out, top, bot, ec_out, send_out, low_ec, low_send = outs
    stripe = stripe_ref[0]
    gather_halos(fld, stripe, tab, x, up, dn, 0, ec, recv, *halos)
    _, cols, above, below = halos[:4]
    terms = column_terms(side_weight, [cols[0].astype(BF), cols[1].astype(BF)], out_fld.chans)
    side = fld.side

    def one_face(f, carry):
        lines = row_stack(x, above, below, f, fld.rows)
        ends = face_terms(terms, f)
        made, pooled = [], []
        for r in range(fld.rows):
            cells = conv_row(
                weight[...], jnp.concatenate(lines(r), axis=0), ends, r, out_fld.chans
            )
            x_out[f, r] = cells
            made.append(cells)
            if r % 2 == 1:
                mean = (mm(made[r - 1], pool[...]) + mm(cells, pool[...])).astype(BF)
                y_out[f, r // 2] = mean
                pooled.append(mean)
        top[f, :, :side] = made[0]
        bot[f, :, :side] = made[-1]
        keep_columns(out_fld, made, f, sends[0])
        top[f, :, side:] = pooled[0]
        bot[f, :, side:] = pooled[-1]
        keep_columns(low, pooled, f, low_sends[0])
        return carry

    lax.fori_loop(0, fld.faces, one_face, 0)
    pack_sends(low, stripe, tab, top, bot, side, low_ec, low_send, *low_sends)
    pack_sends(out_fld, stripe, tab, top, bot, 0, ec_out, send_out, *sends)


def decode_kernel(fld, low, out_ch, vars_out, stripe_ref, tab, x, up, dn, ec, recv, y, yup, ydn, yec, yrecv, weight, side_weight, spread, head, atmos, land, row_key, col_key, pred_out, flux_out, *refs):
    halos, low_halos, flux = refs[:7], refs[7:14], refs[14]
    stripe = stripe_ref[0]
    gather_halos(low, stripe, tab, y, yup, ydn, 0, yec, yrecv, *low_halos)
    gather_halos(fld, stripe, tab, x, up, dn, 0, ec, recv, *halos)
    _, cols, above, below = halos[:4]
    _, low_cols, low_above, low_below = low_halos[:4]
    size = GROUP * GROUP
    row, col = iota((size, size), 0), iota((size, size), 1)
    widen = (col == (row // GROUP) * GROUP + (row % GROUP + 1) // 2).astype(F32).astype(BF)
    joined = []
    for s in range(2):
        wide = mm(widen, low_cols[s].astype(BF))
        joined.append(jnp.concatenate([cols[s], wide], axis=1).astype(BF))
    terms = column_terms(side_weight, joined, out_ch)

    def one_face(f, carry):
        lines = row_stack(x, above, below, f, fld.rows)
        ends = face_terms(terms, f)
        low_lines = [low_above[f]] + [y[f, r] for r in range(low.rows)] + [low_below[f]]
        wide = [mm(cells, spread[...]).astype(BF) for cells in low_lines]
        made = []
        for r in range(fld.rows):
            picked = [wide[(r + a + 1) // 2] for a in range(3)]
            made.append(
                conv_row(weight[...], jnp.concatenate(lines(r) + picked, axis=0), ends, r, out_ch)
            )
        result = mm(head[...], jnp.concatenate(made, axis=0)).reshape(-1, fld.rows, fld.side)
        pred_out[:, f] = (atmos[:, f].astype(F32) + result[:vars_out]).astype(BF)
        sea = land[f] == 1
        flux[:, f] = jnp.where(sea[None], result[vars_out:], 0.0)
        return carry

    lax.fori_loop(0, fld.faces, one_face, 0)
    chosen = (row_key[...] == col_key[...]).astype(F32).astype(BF)
    tiles = flux[...].reshape(-1, fld.side).astype(BF)
    flux_out[...] = mm(chosen, tiles).astype(BF).reshape(flux_out.shape)


def ocean_kernel(cap, recv, state, into, out_weight, sea_out, back_out):
    tiles, _, side = recv.shape

    def one_source(t, carry):
        flux = recv[t].astype(F32)
        pad = (-flux.shape[0]) % 16
        flux = jnp.concatenate([flux, jnp.zeros((pad, side), F32)], axis=0).astype(BF)
        held = state[t]
        high = held.astype(BF)
        low = (held - high.astype(F32)).astype(BF)
        hidden = smooth(mm(into[...], jnp.concatenate([flux, flux, high, high, low], axis=0)))
        width = out_weight[...]
        wide = jnp.concatenate([width] * (side // LANES), axis=1)
        drift = (hidden * wide).reshape(cap, -1, side).sum(axis=1)
        drift = jnp.concatenate([drift, jnp.zeros((8 - cap, side), F32)], axis=0)
        sea = held[:8] + drift
        sea_out[t] = sea
        back_out[t] = sea.astype(BF)
        return carry

    lax.fori_loop(0, tiles, one_source, 0)


def surface_kernel(back, key, land, pred, out):
    faces, rows, side = land.shape
    slots = back[...].astype(F32).reshape(-1, side).astype(BF)
    chosen = (key[...] == iota((faces * rows, slots.shape[0]), 1)).astype(F32).astype(BF)
    sea = mm(chosen, slots).reshape(faces, rows, side)
    out[0] = jnp.where(land[...] == 1, sea, pred[0].astype(F32)).astype(BF)


def call(kernel, outs, ins, scratch, flops, smem=0, specs=None, aliases=None, out_specs=None, name=None):
    whole = pl.BlockSpec(memory_space=pltpu.VMEM)
    in_specs = [pl.BlockSpec(memory_space=pltpu.SMEM)] * smem + [whole] * (len(ins) - smem)
    for position, spec in (specs or {}).items():
        in_specs[position] = spec
    grid = {"grid": (1,)} if specs else {}
    moved = sum(int(np.prod(a.shape)) * a.dtype.itemsize for a in list(ins) + list(outs))
    return pl.pallas_call(
        kernel,
        out_shape=outs,
        **grid,
        in_specs=in_specs,
        out_specs=out_specs or [whole] * len(outs),
        scratch_shapes=scratch,
        input_output_aliases=aliases or {},
        compiler_params=pltpu.CompilerParams(vmem_limit_bytes=56 * 1024 * 1024),
        cost_estimate=pl.CostEstimate(flops=int(flops), bytes_accessed=int(moved), transcendentals=0),
        name=name,
    )(*ins)


def swap_rows(top, bot):
    tiles = lax.axis_size("tile")
    ring = [(i, (i + 1) % tiles) for i in range(tiles)]
    up = lax.ppermute(bot, "tile", ring)
    return up, lax.ppermute(top, "tile", [(j, i) for i, j in ring])


def swap_chunks(chunks):
    return lax.all_to_all(chunks, "tile", split_axis=0, concat_axis=0, tiled=True)


def packed_weight(weight, chans):
    taps, out_ch, _ = weight.shape
    split = weight.reshape(taps, out_ch, taps, chans)
    body = jnp.transpose(split, (2, 1, 0, 3)).reshape(taps * out_ch, taps * chans)
    sides = jnp.stack([split[:, :, 0], split[:, :, 2]]).reshape(2, taps * out_ch, chans)
    return body, sides


def on_one_group(
    atmos_state,
    land_sea,
    owners,
    seam_table,
    ocean_state,
    conv_input,
    conv_encode,
    conv_coarse,
    conv_decode,
    output_head,
    ocean_in,
    ocean_out,
):
    in_ch, faces, rows, side = atmos_state.shape
    tiles = lax.axis_size("tile")
    width = conv_input.shape[1]
    stripe = lax.axis_index("tile").astype(jnp.int32).reshape(1)
    entry = Field(faces, rows, in_ch, side, tiles)
    full = Field(faces, rows, width, side, tiles)
    low = Field(faces, rows // 2, width, side // 2, tiles)
    cells = faces * rows * side

    order = np.arange(in_ch * rows)
    perm = np.zeros((in_ch * rows, in_ch * rows), np.float32)
    perm[order, (order % in_ch) * rows + order // in_ch] = 1.0
    spread = np.zeros((side // 2, side), np.float32)
    spread[np.arange(side) // 2, np.arange(side)] = 1.0
    perm, pool = jnp.asarray(perm, BF), jnp.asarray(0.25 * spread.T, BF)
    spread = jnp.asarray(spread, BF)

    x0, top, bot, ec, send = call(
        functools.partial(prep_kernel, entry),
        [entry.main()] + entry.edges() + entry.sends(),
        (stripe, seam_table, atmos_state, perm),
        entry.send_scratch(),
        2 * cells * in_ch * in_ch * rows,
        smem=2,
        name="prep",
    )
    got = swap_chunks(send)
    up, dn = swap_rows(top, bot)
    x1, top, bot, ec, send = call(
        functools.partial(level_kernel, entry, full, 0),
        [full.main()] + full.edges() + full.sends(),
        (stripe, seam_table, x0, up, dn, ec, got) + packed_weight(conv_input, in_ch),
        full.send_scratch() + entry.halo_scratch(),
        2 * cells * 9 * in_ch * width,
        smem=2,
        name="conv_in",
    )
    got = swap_chunks(send)
    up, dn = swap_rows(top, bot)
    x2, y0, top, bot, ec, send, low_ec, low_send = call(
        functools.partial(encode_kernel, full, full, low),
        [full.main(), low.main()] + full.edges(side // 2) + full.sends() + low.sends(),
        (stripe, seam_table, x1, up, dn, ec, got) + packed_weight(conv_encode, width) + (pool,),
        full.send_scratch() + low.send_scratch() + full.halo_scratch(),
        2 * cells * 9 * width * width,
        smem=2,
        name="encode",
    )
    low_got = swap_chunks(low_send)
    up, dn = swap_rows(top, bot)
    y1, low_top, low_bot, low_ec, low_send = call(
        functools.partial(level_kernel, low, low, side),
        [low.main()] + low.edges() + low.sends(),
        (stripe, seam_table, y0, up, dn, low_ec, low_got) + packed_weight(conv_coarse, width),
        low.send_scratch() + low.halo_scratch(),
        2 * cells * 9 * width * width // 4,
        smem=2,
        name="coarse",
    )
    got = swap_chunks(send)
    low_got = swap_chunks(low_send)
    low_up, low_dn = swap_rows(low_top, low_bot)

    taps = conv_decode.shape[0]
    split = conv_decode.reshape(taps, width, taps, 2, width)
    body = jnp.transpose(split, (2, 1, 3, 0, 4)).reshape(taps * width, 2 * taps * width)
    sides = jnp.stack([split[:, :, 0], split[:, :, 2]]).reshape(2, taps * width, 2 * width)
    heads = output_head.shape[0]
    flux_ch = heads - OUT_VARS
    eye = jnp.eye(rows, dtype=output_head.dtype)
    head = (output_head[:, None, None, :] * eye[None, :, :, None]).reshape(heads * rows, rows * width)

    slot_count = ocean_state.shape[2]
    cap = slot_count // tiles
    owner_ids = owners[:, 0]
    count = owner_ids.shape[0]
    earlier = np.tril(np.ones((count, count), bool), -1)
    rank = jnp.sum((owner_ids[:, None] == owner_ids[None, :]) & earlier, axis=1).astype(jnp.int32)
    slot_index = owner_ids * cap + rank
    col_key = (np.arange(flux_ch, dtype=np.int32)[:, None] * slot_count + slot_index[None, :]).reshape(1, -1)
    row_key = (
        np.arange(flux_ch, dtype=np.int32)[None, :, None] * slot_count
        + np.arange(slot_count, dtype=np.int32).reshape(tiles, 1, cap)
    ).reshape(-1, 1)
    row_key = jnp.asarray(row_key)
    pred, outgoing = call(
        functools.partial(decode_kernel, full, low, width, OUT_VARS),
        [
            jax.ShapeDtypeStruct((OUT_VARS, faces, rows, side), BF),
            jax.ShapeDtypeStruct((tiles, flux_ch * cap, side), BF),
        ],
        (stripe, seam_table, x2, up, dn, ec, got, y1, low_up, low_dn, low_ec, low_got)
        + (body, sides, spread, head, atmos_state, land_sea, row_key, col_key),
        full.halo_scratch() + low.halo_scratch() + [pltpu.VMEM((flux_ch, faces, rows, side), F32)],
        2 * cells * 18 * width * width,
        smem=2,
        specs={16: pl.BlockSpec((OUT_VARS, faces, rows, side), lambda i: (0, 0, 0, 0))},
        name="decode",
    )
    arrived = lax.all_to_all(outgoing, "tile", split_axis=0, concat_axis=0, tiled=True)

    held = jnp.transpose(ocean_state[0, 0].reshape(tiles, cap, OCEAN_CH, side), (0, 2, 1, 3))
    state = jnp.pad(held, ((0, 0), (0, 0), (0, 8 - cap), (0, 0))).reshape(tiles, OCEAN_CH * 8, side)
    hidden = ocean_in.shape[0]
    high = ocean_in.astype(BF)
    rest = (ocean_in - high.astype(F32)).astype(BF)
    flux_pad = (-flux_ch * cap) % 16
    each = jnp.eye(cap, dtype=BF)
    slot8 = jnp.eye(cap, 8, dtype=BF)

    def flux_part(weights):
        part = each[:, None, None, :] * weights[None, :, OCEAN_CH:, None]
        return jnp.pad(part.reshape(cap * hidden, flux_ch * cap), ((0, 0), (0, flux_pad)))

    def state_part(weights):
        part = slot8[:, None, None, :] * weights[None, :, :OCEAN_CH, None]
        return part.reshape(cap * hidden, OCEAN_CH * 8)

    into = jnp.concatenate(
        [flux_part(high), flux_part(rest), state_part(high), state_part(rest), state_part(high)], axis=1
    )
    out_weight = jnp.broadcast_to(ocean_out[None, :, None], (cap, hidden, LANES)).reshape(-1, LANES)
    sea, back = call(
        functools.partial(ocean_kernel, cap),
        [jax.ShapeDtypeStruct((tiles, 8, side), F32), jax.ShapeDtypeStruct((tiles, 8, side), BF)],
        (arrived, state, into, out_weight),
        [],
        2 * slot_count * side * hidden * 8,
        name="ocean",
    )
    returned = lax.all_to_all(back, "tile", split_axis=0, concat_axis=0, tiled=True)
    key = (owner_ids * 8 + rank)[:, None]
    first = pl.BlockSpec((1, faces, rows, side), lambda i: (0, 0, 0, 0))
    (atmos_next,) = call(
        surface_kernel,
        [jax.ShapeDtypeStruct(pred.shape, BF)],
        (returned, key, land_sea, pred),
        [],
        2 * count * tiles * 8 * side,
        specs={3: first},
        out_specs=[first],
        aliases={3: 0},
        name="surface",
    )
    renewed = jnp.stack([sea[:, :cap], held[:, 0]], axis=2)
    return atmos_next, renewed.reshape(1, 1, slot_count, OCEAN_CH, side)


def fits(mesh):
    return mesh.shape["face"] == 1


def solution(mesh):
    in_specs = (
        P(None, "face", "tile", None),
        P("face", "tile", None),
        P(("face", "tile"), None),
        P(),
        P("face", "tile", None, None, None),
        P(),
        P(),
        P(),
        P(),
        P(),
        P(),
        P(),
    )
    out_specs = (P(None, "face", "tile", None), P("face", "tile", None, None, None))
    return jax.shard_map(
        on_one_group if fits(mesh) else on_device,
        mesh=mesh,
        in_specs=in_specs,
        out_specs=out_specs,
        check_vma=False,
    )
```

```python
import functools

import jax
import jax.numpy as jnp
import numpy as np
from jax import lax
from jax.experimental import pallas as pl
from jax.experimental.pallas import tpu as pltpu
from jax.sharding import PartitionSpec as P

OUT_VARS = 8
FLUX_CH = 4
OCEAN_CH = 2


def extended(shard, sides, width):
    for axis, dim in sides:
        size, length = (lax.axis_size(axis), shard.shape[dim])
        up = [(i, (i + 1) % size) for i in range(size)]
        down = [(j, i) for i, j in up]
        last = lax.slice_in_dim(shard, length - width, length, axis=dim)
        initial = lax.slice_in_dim(shard, 0, width, axis=dim)
        before = lax.ppermute(last, axis, up)
        after = lax.ppermute(initial, axis, down)
        shard = jnp.concatenate([before, shard, after], axis=dim)
    return shard


def pad_field(values, seam_table):
    channels, faces_dev, stripe_rows, face_side = values.shape
    tile_count = lax.axis_size("tile")
    stripe = lax.axis_index("tile")
    face_group = lax.axis_index("face")
    rimmed = extended(values, (("tile", 2),), 1)
    edge_rows = jnp.stack([values[:, :, 0, :], rimmed[:, :, 0, :]], axis=2)
    edge_pieces = edge_rows.reshape(channels, faces_dev, 2, tile_count, stripe_rows)
    received = lax.all_to_all(edge_pieces, "tile", split_axis=3, concat_axis=3, tiled=True)
    row_part = received[:, :, :, 0, :]
    row_start = stripe * stripe_rows
    col_part = jnp.stack([values[:, :, :, 0], values[:, :, :, face_side - 1]], axis=2)
    seam_piece = jnp.concatenate([row_part, col_part], axis=2)
    seam_piece = jnp.transpose(seam_piece, (1, 2, 0, 3)).reshape(
        1, faces_dev, 4, channels * stripe_rows
    )
    own_sides = lax.dynamic_slice_in_dim(seam_table, face_group * (faces_dev * 4), faces_dev * 4, 0)
    gathered = lax.all_gather(seam_piece, ("face", "tile"), axis=0, tiled=True)
    group_count = gathered.shape[0] // tile_count
    strip_table = gathered.reshape(group_count, tile_count, faces_dev, 4, channels, stripe_rows)
    strip_table = jnp.transpose(strip_table, (0, 2, 3, 4, 1, 5)).reshape(
        group_count * faces_dev * 4, channels, face_side
    )
    strips = jnp.take(strip_table, own_sides[:, 0], axis=0)
    strips = jnp.where(own_sides[:, 1][:, None, None] == 1, strips[:, :, ::-1], strips)
    strips = jnp.transpose(strips.reshape(faces_dev, 4, channels, face_side), (2, 0, 1, 3))
    upper_row = jnp.where(stripe == 0, strips[:, :, 0, :], rimmed[:, :, 0, :])
    bottom = jnp.where(
        stripe == tile_count - 1, strips[:, :, 1, :], rimmed[:, :, stripe_rows + 1, :]
    )
    middle = jnp.concatenate([upper_row[:, :, None, :], values, bottom[:, :, None, :]], axis=2)
    zero_cells = jnp.zeros((channels, faces_dev, 2, 1), values.dtype)
    columns = jnp.concatenate([zero_cells, strips[:, :, 2:, :], zero_cells], axis=3)
    columns = lax.dynamic_slice_in_dim(columns, row_start, stripe_rows + 2, 3)
    return jnp.concatenate([columns[:, :, 0, :, None], middle, columns[:, :, 1, :, None]], axis=3)


def convolve(padded, weight):
    channels, faces_dev, rows_two, side_two = padded.shape
    stripe_rows = rows_two - 2
    face_side = side_two - 2
    planes = []
    for face_index in range(faces_dev):
        summed = jnp.zeros((weight.shape[1], stripe_rows * face_side), jnp.float32)
        for row_shift in range(3):
            tap_rows = jnp.concatenate(
                [
                    padded[
                        :,
                        face_index,
                        row_shift : row_shift + stripe_rows,
                        col_shift : col_shift + face_side,
                    ]
                    for col_shift in range(3)
                ],
                axis=0,
            )
            summed = summed + jnp.dot(
                weight[row_shift],
                tap_rows.reshape(3 * channels, stripe_rows * face_side),
                preferred_element_type=jnp.float32,
            )
        planes.append(jax.nn.gelu(summed).astype(jnp.bfloat16).reshape(-1, stripe_rows, face_side))
    return jnp.stack(planes, axis=1)


def upsample(values):
    return jnp.repeat(jnp.repeat(values, 2, axis=2), 2, axis=3)


def ocean_update(held_state, arrived_flux, ocean_in, ocean_out):
    stacked = jnp.concatenate([held_state, arrived_flux.astype(jnp.float32)], axis=1)
    hidden = jax.nn.gelu(
        jnp.einsum("hc,ncs->nhs", ocean_in, stacked, precision=lax.Precision.HIGHEST)
    )
    sea_now = held_state[:, 0] + jnp.einsum(
        "h,nhs->ns", ocean_out, hidden, precision=lax.Precision.HIGHEST
    )
    return jnp.stack([sea_now, held_state[:, 0]], axis=1)


def ocean_blocks(held_state, arrived_flux, ocean_in, ocean_out, block_count):
    slot_count, state_ch, face_side = held_state.shape
    capacity = slot_count // block_count
    held_split = held_state.reshape(block_count, capacity, state_ch, face_side)
    flux_split = arrived_flux.reshape(block_count, capacity, arrived_flux.shape[1], face_side)
    stepped = lax.map(
        lambda pair: ocean_update(pair[0], pair[1], ocean_in, ocean_out), (held_split, flux_split)
    )
    return stepped.reshape(slot_count, state_ch, face_side)


def on_device(
    atmos_state,
    land_sea,
    owners,
    seam_table,
    ocean_state,
    conv_input,
    conv_encode,
    conv_coarse,
    conv_decode,
    output_head,
    ocean_in,
    ocean_out,
):
    encoded = convolve(pad_field(atmos_state, seam_table), conv_input)
    skip_level = convolve(pad_field(encoded, seam_table), conv_encode)
    channels, faces_dev, stripe_rows, face_side = skip_level.shape
    pooled = (
        skip_level.astype(jnp.float32)
        .reshape(channels, faces_dev, stripe_rows // 2, 2, face_side // 2, 2)
        .mean(axis=(3, 5))
        .astype(jnp.bfloat16)
    )
    coarse_out = convolve(pad_field(pooled, seam_table), conv_coarse)
    coarse_pad = upsample(pad_field(coarse_out, seam_table))[
        :, :, 1 : stripe_rows + 3, 1 : face_side + 3
    ]
    padded = jnp.concatenate([pad_field(skip_level, seam_table), coarse_pad], axis=0)
    decoded = convolve(padded, conv_decode)
    head_out = jnp.dot(
        output_head, decoded.reshape(channels, -1), preferred_element_type=jnp.float32
    )
    head_out = head_out.reshape(-1, faces_dev, stripe_rows, face_side)
    predicted = atmos_state[:OUT_VARS].astype(jnp.float32) + head_out[:OUT_VARS]
    is_ocean = land_sea == 1
    fluxes = jnp.where(is_ocean[None], head_out[OUT_VARS:], 0.0).astype(jnp.bfloat16)
    flux_tiles = jnp.transpose(fluxes, (1, 2, 0, 3)).reshape(
        faces_dev * stripe_rows, FLUX_CH * face_side
    )
    tile_count = lax.axis_size("tile")
    owner_ids = owners[:, 0]
    owner_hits = (owner_ids[:, None] == jnp.arange(tile_count)[None, :]).astype(jnp.int32)
    slot_rank = jnp.sum((jnp.cumsum(owner_hits, axis=0) - 1) * owner_hits, axis=1)
    slot_count = ocean_state.shape[2]
    capacity = slot_count // tile_count
    slot_index = owner_ids * capacity + slot_rank
    selector = (jnp.arange(slot_count)[:, None] == slot_index[None, :]).astype(jnp.bfloat16)
    outgoing = jnp.dot(selector, flux_tiles, preferred_element_type=jnp.float32).astype(
        jnp.bfloat16
    )
    outgoing = outgoing.reshape(tile_count, capacity, FLUX_CH, face_side)
    held_state = ocean_state[0, 0]
    arrived = lax.all_to_all(outgoing, "tile", split_axis=0, concat_axis=0, tiled=True)
    renewed = ocean_blocks(
        held_state, arrived.reshape(slot_count, FLUX_CH, face_side), ocean_in, ocean_out, tile_count
    )
    sea_back = renewed[:, 0].astype(jnp.bfloat16).reshape(tile_count, capacity, face_side)
    sea_slots = lax.all_to_all(sea_back, "tile", split_axis=0, concat_axis=0, tiled=True)
    sea_tiles = jnp.dot(
        selector.T, sea_slots.reshape(slot_count, face_side), preferred_element_type=jnp.float32
    )
    sea_temp = sea_tiles.reshape(faces_dev, stripe_rows, face_side)
    surface = jnp.where(is_ocean, sea_temp, predicted[0])
    atmos_next = jnp.concatenate([surface[None], predicted[1:]], axis=0).astype(jnp.bfloat16)
    return (atmos_next, renewed.reshape(1, 1, slot_count, OCEAN_CH, face_side))


GROUP = 16
LANES = 128
VMEM = pltpu.VMEM
BF = jnp.bfloat16
F32 = jnp.float32
NT = (((1,), (1,)), ((), ()))


def mm(a, b):
    return jnp.dot(a, b, preferred_element_type=F32)


def mm_nt(a, b):
    return lax.dot_general(a, b, NT, preferred_element_type=F32)


def iota(shape, dim):
    return lax.broadcasted_iota(jnp.int32, shape, dim)


def smooth(x):
    inner = x * (0.7978845608028654 + 0.03567740813636141 * (x * x))
    half = 0.5 * x
    return half * jnp.tanh(inner) + half


class Field:
    def __init__(self, faces, rows, chans, side, tiles):
        self.faces, self.rows, self.chans, self.side, self.tiles = faces, rows, chans, side, tiles
        self.per = LANES // chans
        self.groups = faces // self.per
        self.span = rows + 2
        self.extra = self.groups * self.span
        used = max(self.extra + 2 * self.groups, 2 * self.groups * rows)
        self.chunk = used + (-used) % 16

    def main(self):
        return jax.ShapeDtypeStruct((self.faces, self.rows, self.chans, self.side), BF)

    def edges(self, more=0):
        edge = jax.ShapeDtypeStruct((self.faces, self.chans, self.side + more), BF)
        return [edge, edge]

    def sends(self):
        return [
            jax.ShapeDtypeStruct((2 * self.faces * 8, self.chans), BF),
            jax.ShapeDtypeStruct((self.tiles, self.chunk, LANES), BF),
        ]

    def send_scratch(self):
        return [
            pltpu.VMEM((2, self.faces, 8, self.chans), F32),
            pltpu.VMEM((self.tiles, self.chunk, LANES), F32),
            pltpu.VMEM((self.side + 8, LANES), F32),
        ]

    def halo_scratch(self):
        return [
            pltpu.VMEM((6, self.faces, GROUP, self.chans), F32),
            pltpu.VMEM((2, GROUP * GROUP, self.chans), F32),
            pltpu.VMEM((self.faces, self.chans, self.side), BF),
            pltpu.VMEM((self.faces, self.chans, self.side), BF),
            pltpu.VMEM((2, self.faces, self.chans, self.side), BF),
            pltpu.VMEM((self.tiles, self.chunk, LANES), F32),
            pltpu.VMEM((2, self.faces, 8, self.chans), F32),
        ]


def flip_matrix(size, flag):
    row, col = iota((size, size), 0), iota((size, size), 1)
    return (row == jnp.where(flag == 1, size - 1 - col, col)).astype(F32).astype(BF)


def end_picker(side):
    row, col = iota((16, side), 0), iota((16, side), 1)
    return (((row == 0) & (col == 0)) | ((row == 1) & (col == side - 1))).astype(F32).astype(BF)


def column_picker(fld):
    length = fld.rows * fld.side
    row, col = iota((16, length), 0), iota((16, length), 1)
    want = (row & 7) * fld.side + (row >> 3) * (fld.side - 1)
    return (col == want).astype(F32).astype(BF)


def keep_columns(picker, face_rows, f, cols):
    picked = mm_nt(picker, jnp.concatenate(face_rows, axis=1))
    cols[0, f] = picked[:8]
    cols[1, f] = picked[8:]


def pack_sends(fld, stripe, tab, top, bot, off, ec_out, send_out, cols, stage, strip):
    last, rows, chans, groups, per = fld.tiles - 1, fld.rows, fld.chans, fld.groups, fld.per
    held = cols[...]
    ec_out[...] = held.reshape(2 * fld.faces * 8, chans).astype(BF)
    paired = held.reshape(2, groups, per, 8, chans)
    packed = jnp.concatenate([paired[:, :, j] for j in range(per)], axis=3)
    across = packed[:, :, :rows].reshape(2 * groups * rows, LANES)
    initial = packed[:, :, 0].reshape(2 * groups, LANES)
    final = packed[:, :, rows - 1].reshape(2 * groups, LANES)
    pieces = []
    for q in range(2):
        for g in range(fld.faces):
            p = tab[4 * g + q, 0]
            pieces.append(cols[jnp.maximum((p & 3) - 2, 0), p >> 2][:rows])
    merged = [jnp.concatenate(pieces[n : n + per], axis=1) for n in range(0, len(pieces), per)]
    stage[...] = jnp.zeros_like(stage)
    for q in range(2):
        for i in range(groups):
            stage[q * last, i * fld.span + 1 : i * fld.span + 1 + rows, :] = merged[q * groups + i]

    def lanes(h):
        return slice((h % per) * chans, (h % per + 1) * chans)

    @pl.when((stripe == 0) | (stripe == last))
    def _():
        q = jnp.where(stripe == 0, 0, 1)
        for i in range(groups):
            turned = []
            for h in range(i * per, (i + 1) * per):
                upper = top[h, :, off : off + fld.side].astype(F32)
                lower = bot[h, :, off : off + fld.side].astype(F32)
                cells = jnp.where(q == 0, upper, lower).astype(BF)
                turned.append(mm_nt(flip_matrix(fld.side, tab[4 * h + q, 1]), cells))
            strip[0:8] = jnp.zeros((8, LANES), F32)
            strip[fld.side : fld.side + 8] = jnp.zeros((8, LANES), F32)
            strip[1 : fld.side + 1, :] = jnp.concatenate(turned, axis=1)
            for d in range(1, last, 10):
                here = range(d, min(d + 10, last))
                taken = [strip[e * rows : e * rows + fld.span, :] for e in here]
                for e, piece in zip(here, taken):
                    stage[e, i * fld.span : (i + 1) * fld.span, :] = piece

    stage[last - stripe, : 2 * groups * rows, :] = across

    @pl.when(stripe < last)
    def _():
        stage[last - 1 - stripe, fld.extra : fld.extra + 2 * groups, :] = final

    @pl.when(stripe > 0)
    def _():
        stage[last + 1 - stripe, fld.extra : fld.extra + 2 * groups, :] = initial

    send_out[...] = stage[...].astype(BF)


def gather_halos(fld, stripe, tab, x, up, dn, off, ec, recv, cand, cols, above, below, pair, got, mirror):
    faces, rows, chans, side, tiles = fld.faces, fld.rows, fld.chans, fld.side, fld.tiles
    last = tiles - 1
    groups = fld.groups
    got[...] = recv[...].astype(F32)
    own = ec[...].astype(F32).reshape(2, faces, 8, chans)
    row, col = iota((groups * rows, groups * rows), 0), iota((groups * rows, groups * rows), 1)
    turn = ((row // rows == col // rows) & (row % rows + col % rows == rows - 1)).astype(F32).astype(BF)
    prow, pcol = iota((16, side), 0), iota((16, side), 1)

    def lanes(h):
        return slice((h % fld.per) * chans, (h % fld.per + 1) * chans)

    above[...] = up[:, :, off : off + side]
    below[...] = dn[:, :, off : off + side]
    over = mm_nt(end_picker(side), above[...].reshape(faces * chans, side))
    under = mm_nt(end_picker(side), below[...].reshape(faces * chans, side))
    heads = [got[q * last, : fld.extra, :] for q in range(2)]
    before = got[jnp.minimum(last + 1 - stripe, last), fld.extra : fld.extra + 2 * groups, :]
    after = got[jnp.maximum(last - 1 - stripe, 0), fld.extra : fld.extra + 2 * groups, :]
    for s in range(2):
        across = got[last - stripe, s * groups * rows : (s + 1) * groups * rows, :]
        turned = mm(turn, across.astype(BF))
        for h in range(faces):
            i = h // fld.per
            cand[2 + s, h, 0:1] = over[s : s + 1, h * chans : (h + 1) * chans]
            cand[2 + s, h, rows + 1 : rows + 2] = under[s : s + 1, h * chans : (h + 1) * chans]
            cand[2 + s, h, 1 : rows + 1] = own[s, h, :rows]
            mirror[s, h, :rows] = across[i * rows : (i + 1) * rows, lanes(h)]
            cand[4 + s, h, 0:1] = before[s * groups + i : s * groups + i + 1, lanes(h)]
            cand[4 + s, h, rows + 1 : rows + 2] = after[s * groups + i : s * groups + i + 1, lanes(h)]
            cand[4 + s, h, 1 : rows + 1] = turned[i * rows : (i + 1) * rows, lanes(h)]
    at_edge = (stripe == 0) | (stripe == last)

    @pl.when(jnp.logical_not(at_edge))
    def _():
        for q in range(2):
            for h in range(faces):
                i = h // fld.per
                cand[q, h, 0 : fld.span] = heads[q][i * fld.span : (i + 1) * fld.span, lanes(h)]

    @pl.when(at_edge)
    def _():
        q = jnp.where(stripe == 0, 0, 1)
        for h in range(faces):
            pair[0, h] = jnp.where(q == 0, x[h, 0].astype(F32), below[h].astype(F32)).astype(BF)
            pair[1, h] = jnp.where(q == 0, above[h].astype(F32), x[h, rows - 1].astype(F32)).astype(BF)
        place = stripe * rows - 1 + prow
        inside = (place >= 0) & (place < side)
        windows = []
        for s in range(2):
            for h in range(faces):
                want = jnp.where(tab[4 * h + s, 1] == 1, side - 1 - place, place)
                window = ((pcol == want) & inside).astype(F32).astype(BF)
                windows.append(mm_nt(window, pair[s, h]))
        pieces = []
        for g in range(faces):
            p = tab[4 * g + q, 0]
            pieces.append(mirror[jnp.maximum((p & 3) - 2, 0), p >> 2][:rows])
        for s in range(2):
            for h in range(faces):
                cand[s, h] = windows[s * faces + h]
        for i in range(groups):
            merged = jnp.concatenate(pieces[i * fld.per : (i + 1) * fld.per], axis=1)
            got[last - stripe, i * fld.span + 1 : i * fld.span + 1 + rows, :] = merged
        for i in range(groups):
            lined = jnp.concatenate(
                [got[d, i * fld.span + 1 : i * fld.span + 1 + rows, :] for d in range(tiles)], axis=0
            )
            lined = jnp.transpose(lined)
            for j in range(fld.per):
                g = i * fld.per + j
                p = tab[4 * g + q, 0]
                kind, h = p & 3, p >> 2
                near = pair[jnp.minimum(kind, 1), h].astype(F32)
                far = lined[j * chans : (j + 1) * chans]
                cells = jnp.where(kind < 2, near, far).astype(BF)
                placed = mm(cells, flip_matrix(side, tab[4 * g + q, 1])).astype(BF)

                @pl.when(q == 0)
                def _():
                    above[g] = placed

                @pl.when(q == 1)
                def _():
                    below[g] = placed

    slot = iota((GROUP, chans), 0)
    live = (slot < fld.span) & jnp.logical_not(
        ((slot == 0) & (stripe == 0)) | ((slot == rows + 1) & (stripe == last))
    )
    for s in range(2):
        taken = []
        for g in range(faces):
            p = tab[4 * g + 2 + s, 0]
            kind, h = p & 3, p >> 2
            which = jnp.where((kind >= 2) & (tab[4 * g + 2 + s, 1] == 1), kind + 2, kind)
            taken.append(jnp.where(live, cand[which, h], 0.0))
        taken.append(jnp.zeros(((GROUP - faces) * GROUP, chans), F32))
        cols[s] = jnp.concatenate(taken, axis=0)


def column_terms(side_weight, cols, out_ch):
    terms = []
    for s in range(2):
        part = mm_nt(side_weight[s], cols[s])
        size = part.shape[1]
        terms.append(
            part[out_ch : 2 * out_ch]
            + pltpu.roll(part[:out_ch], 1, 1)
            + pltpu.roll(part[2 * out_ch :], size - 1, 1)
        )
    return terms


def face_terms(terms, face_index):
    size = terms[0].shape[1]
    shift = lax.rem(2 * size - GROUP * face_index - 1, size)
    return [pltpu.roll(term, shift, 1)[:, :LANES] for term in terms]


def conv_row(weight, stacked, terms, r, out_ch):
    z = mm(weight, stacked)
    side = z.shape[1]
    left, right = pltpu.roll(z[:out_ch], 1, 1), pltpu.roll(z[2 * out_ch :], side - 1, 1)
    lane = iota((out_ch, LANES), 1)
    first = terms[0] if r == 0 else pltpu.roll(terms[0], LANES - r, 1)
    final = pltpu.roll(terms[1], LANES - 1 - r, 1)
    head = jnp.where(lane == 0, first, left[:, :LANES])
    tail = jnp.where(lane == LANES - 1, final, right[:, side - LANES :])
    if side > LANES:
        left = jnp.concatenate([head, left[:, LANES:]], axis=1)
        right = jnp.concatenate([right[:, : side - LANES], tail], axis=1)
    else:
        left, right = head, tail
    return smooth(z[out_ch : 2 * out_ch] + left + right).astype(BF)


def row_stack(x, above, below, f, rows):
    lines = [above[f]] + [x[f, r] for r in range(rows)] + [below[f]]
    return lambda r: lines[r : r + 3]


def prep_kernel(fld, stripe_ref, tab, atmos, perm, x_out, top, bot, ec_out, send_out, cols, stage, strip):
    stripe = stripe_ref[0]
    picker = column_picker(fld)

    def one_face(f, carry):
        block = atmos[:, f].astype(F32).reshape(fld.chans * fld.rows, fld.side).astype(BF)
        moved = mm(perm[...], block).astype(BF)
        lines = [moved[r * fld.chans : (r + 1) * fld.chans] for r in range(fld.rows)]
        for r in range(fld.rows):
            x_out[f, r] = lines[r]
        top[f] = lines[0]
        bot[f] = lines[-1]
        keep_columns(picker, lines, f, cols)
        return carry

    lax.fori_loop(0, fld.faces, one_face, 0)
    pack_sends(fld, stripe, tab, top, bot, 0, ec_out, send_out, cols, stage, strip)


def level_kernel(fld, out_fld, off, stripe_ref, tab, x, up, dn, ec, recv, weight, side_weight, *refs):
    outs, sends, halos = refs[:5], refs[5:8], refs[8:]
    x_out, top, bot, ec_out, send_out = outs
    stripe = stripe_ref[0]
    gather_halos(fld, stripe, tab, x, up, dn, off, ec, recv, *halos)
    _, cols, above, below = halos[:4]
    terms = column_terms(side_weight, [cols[0].astype(BF), cols[1].astype(BF)], out_fld.chans)
    picker = column_picker(out_fld)

    def one_face(f, carry):
        lines = row_stack(x, above, below, f, fld.rows)
        ends = face_terms(terms, f)
        made = []
        for r in range(fld.rows):
            cells = conv_row(
                weight[...], jnp.concatenate(lines(r), axis=0), ends, r, out_fld.chans
            )
            x_out[f, r] = cells
            made.append(cells)
        top[f] = made[0]
        bot[f] = made[-1]
        keep_columns(picker, made, f, sends[0])
        return carry

    lax.fori_loop(0, fld.faces, one_face, 0)
    pack_sends(out_fld, stripe, tab, top, bot, 0, ec_out, send_out, *sends)


def encode_kernel(fld, out_fld, low, stripe_ref, tab, x, up, dn, ec, recv, weight, side_weight, pool, *refs):
    outs, sends, low_sends, halos = refs[:8], refs[8:11], refs[11:14], refs[14:]
    x_out, y_out, top, bot, ec_out, send_out, low_ec, low_send = outs
    stripe = stripe_ref[0]
    gather_halos(fld, stripe, tab, x, up, dn, 0, ec, recv, *halos)
    _, cols, above, below = halos[:4]
    terms = column_terms(side_weight, [cols[0].astype(BF), cols[1].astype(BF)], out_fld.chans)
    side = fld.side
    picker, low_picker = column_picker(out_fld), column_picker(low)

    def one_face(f, carry):
        lines = row_stack(x, above, below, f, fld.rows)
        ends = face_terms(terms, f)
        made, pooled = [], []
        for r in range(fld.rows):
            cells = conv_row(
                weight[...], jnp.concatenate(lines(r), axis=0), ends, r, out_fld.chans
            )
            x_out[f, r] = cells
            made.append(cells)
            if r % 2 == 1:
                mean = (mm(made[r - 1], pool[...]) + mm(cells, pool[...])).astype(BF)
                y_out[f, r // 2] = mean
                pooled.append(mean)
        top[f, :, :side] = made[0]
        bot[f, :, :side] = made[-1]
        keep_columns(picker, made, f, sends[0])
        top[f, :, side:] = pooled[0]
        bot[f, :, side:] = pooled[-1]
        keep_columns(low_picker, pooled, f, low_sends[0])
        return carry

    lax.fori_loop(0, fld.faces, one_face, 0)
    pack_sends(low, stripe, tab, top, bot, side, low_ec, low_send, *low_sends)
    pack_sends(out_fld, stripe, tab, top, bot, 0, ec_out, send_out, *sends)


def decode_kernel(fld, low, out_ch, vars_out, stripe_ref, tab, x, up, dn, ec, recv, y, yup, ydn, yec, yrecv, weight, side_weight, spread, head, atmos, land, row_key, col_key, pred_out, flux_out, *refs):
    halos, low_halos, flux = refs[:7], refs[7:14], refs[14]
    stripe = stripe_ref[0]
    gather_halos(low, stripe, tab, y, yup, ydn, 0, yec, yrecv, *low_halos)
    gather_halos(fld, stripe, tab, x, up, dn, 0, ec, recv, *halos)
    _, cols, above, below = halos[:4]
    _, low_cols, low_above, low_below = low_halos[:4]
    size = GROUP * GROUP
    row, col = iota((size, size), 0), iota((size, size), 1)
    widen = (col == (row // GROUP) * GROUP + (row % GROUP + 1) // 2).astype(F32).astype(BF)
    joined = []
    for s in range(2):
        wide = mm(widen, low_cols[s].astype(BF))
        joined.append(jnp.concatenate([cols[s], wide], axis=1).astype(BF))
    terms = column_terms(side_weight, joined, out_ch)

    def one_face(f, carry):
        lines = row_stack(x, above, below, f, fld.rows)
        ends = face_terms(terms, f)
        low_lines = [low_above[f]] + [y[f, r] for r in range(low.rows)] + [low_below[f]]
        wide = [mm(cells, spread[...]).astype(BF) for cells in low_lines]
        made = []
        for r in range(fld.rows):
            picked = [wide[(r + a + 1) // 2] for a in range(3)]
            made.append(
                conv_row(weight[...], jnp.concatenate(lines(r) + picked, axis=0), ends, r, out_ch)
            )
        result = mm(head[...], jnp.concatenate(made, axis=0)).reshape(-1, fld.rows, fld.side)
        pred_out[:, f] = (atmos[:, f].astype(F32) + result[:vars_out]).astype(BF)
        sea = land[f] == 1
        flux[:, f] = jnp.where(sea[None], result[vars_out:], 0.0)
        return carry

    lax.fori_loop(0, fld.faces, one_face, 0)
    chosen = (row_key[...] == col_key[...]).astype(F32).astype(BF)
    tiles = flux[...].reshape(-1, fld.side).astype(BF)
    flux_out[...] = mm(chosen, tiles).astype(BF).reshape(flux_out.shape)


def ocean_kernel(cap, recv, state, into, out_weight, sea_out, back_out):
    tiles, _, side = recv.shape

    def one_source(t, carry):
        flux = recv[t].astype(F32)
        pad = (-flux.shape[0]) % 16
        flux = jnp.concatenate([flux, jnp.zeros((pad, side), F32)], axis=0).astype(BF)
        held = state[t]
        high = held.astype(BF)
        low = (held - high.astype(F32)).astype(BF)
        hidden = smooth(mm(into[...], jnp.concatenate([flux, flux, high, high, low], axis=0)))
        width = out_weight[...]
        wide = jnp.concatenate([width] * (side // LANES), axis=1)
        drift = (hidden * wide).reshape(cap, -1, side).sum(axis=1)
        drift = jnp.concatenate([drift, jnp.zeros((8 - cap, side), F32)], axis=0)
        sea = held[:8] + drift
        sea_out[t] = sea
        back_out[t] = sea.astype(BF)
        return carry

    lax.fori_loop(0, tiles, one_source, 0)


def surface_kernel(back, key, land, pred, out):
    faces, rows, side = land.shape
    slots = back[...].astype(F32).reshape(-1, side).astype(BF)
    chosen = (key[...] == iota((faces * rows, slots.shape[0]), 1)).astype(F32).astype(BF)
    sea = mm(chosen, slots).reshape(faces, rows, side)
    out[0] = jnp.where(land[...] == 1, sea, pred[0].astype(F32)).astype(BF)


def call(kernel, outs, ins, scratch, flops, smem=0, specs=None, aliases=None, out_specs=None, name=None):
    whole = pl.BlockSpec(memory_space=pltpu.VMEM)
    in_specs = [pl.BlockSpec(memory_space=pltpu.SMEM)] * smem + [whole] * (len(ins) - smem)
    for position, spec in (specs or {}).items():
        in_specs[position] = spec
    grid = {"grid": (1,)} if specs else {}
    moved = sum(int(np.prod(a.shape)) * a.dtype.itemsize for a in list(ins) + list(outs))
    return pl.pallas_call(
        kernel,
        out_shape=outs,
        **grid,
        in_specs=in_specs,
        out_specs=out_specs or [whole] * len(outs),
        scratch_shapes=scratch,
        input_output_aliases=aliases or {},
        compiler_params=pltpu.CompilerParams(vmem_limit_bytes=56 * 1024 * 1024),
        cost_estimate=pl.CostEstimate(flops=int(flops), bytes_accessed=int(moved), transcendentals=0),
        name=name,
    )(*ins)


def swap_rows(top, bot):
    tiles = lax.axis_size("tile")
    ring = [(i, (i + 1) % tiles) for i in range(tiles)]
    up = lax.ppermute(bot, "tile", ring)
    return up, lax.ppermute(top, "tile", [(j, i) for i, j in ring])


def swap_chunks(chunks):
    return lax.all_to_all(chunks, "tile", split_axis=0, concat_axis=0, tiled=True)


def packed_weight(weight, chans):
    taps, out_ch, _ = weight.shape
    split = weight.reshape(taps, out_ch, taps, chans)
    body = jnp.transpose(split, (2, 1, 0, 3)).reshape(taps * out_ch, taps * chans)
    sides = jnp.stack([split[:, :, 0], split[:, :, 2]]).reshape(2, taps * out_ch, chans)
    return body, sides


def on_one_group(
    atmos_state,
    land_sea,
    owners,
    seam_table,
    ocean_state,
    conv_input,
    conv_encode,
    conv_coarse,
    conv_decode,
    output_head,
    ocean_in,
    ocean_out,
):
    in_ch, faces, rows, side = atmos_state.shape
    tiles = lax.axis_size("tile")
    width = conv_input.shape[1]
    stripe = lax.axis_index("tile").astype(jnp.int32).reshape(1)
    entry = Field(faces, rows, in_ch, side, tiles)
    full = Field(faces, rows, width, side, tiles)
    low = Field(faces, rows // 2, width, side // 2, tiles)
    cells = faces * rows * side

    order = np.arange(in_ch * rows)
    perm = np.zeros((in_ch * rows, in_ch * rows), np.float32)
    perm[order, (order % in_ch) * rows + order // in_ch] = 1.0
    spread = np.zeros((side // 2, side), np.float32)
    spread[np.arange(side) // 2, np.arange(side)] = 1.0
    perm, pool = jnp.asarray(perm, BF), jnp.asarray(0.25 * spread.T, BF)
    spread = jnp.asarray(spread, BF)

    x0, top, bot, ec, send = call(
        functools.partial(prep_kernel, entry),
        [entry.main()] + entry.edges() + entry.sends(),
        (stripe, seam_table, atmos_state, perm),
        entry.send_scratch(),
        2 * cells * in_ch * in_ch * rows,
        smem=2,
        name="prep",
    )
    got = swap_chunks(send)
    up, dn = swap_rows(top, bot)
    x1, top, bot, ec, send = call(
        functools.partial(level_kernel, entry, full, 0),
        [full.main()] + full.edges() + full.sends(),
        (stripe, seam_table, x0, up, dn, ec, got) + packed_weight(conv_input, in_ch),
        full.send_scratch() + entry.halo_scratch(),
        2 * cells * 9 * in_ch * width,
        smem=2,
        name="conv_in",
    )
    got = swap_chunks(send)
    up, dn = swap_rows(top, bot)
    x2, y0, top, bot, ec, send, low_ec, low_send = call(
        functools.partial(encode_kernel, full, full, low),
        [full.main(), low.main()] + full.edges(side // 2) + full.sends() + low.sends(),
        (stripe, seam_table, x1, up, dn, ec, got) + packed_weight(conv_encode, width) + (pool,),
        full.send_scratch() + low.send_scratch() + full.halo_scratch(),
        2 * cells * 9 * width * width,
        smem=2,
        name="encode",
    )
    low_got = swap_chunks(low_send)
    up, dn = swap_rows(top, bot)
    y1, low_top, low_bot, low_ec, low_send = call(
        functools.partial(level_kernel, low, low, side),
        [low.main()] + low.edges() + low.sends(),
        (stripe, seam_table, y0, up, dn, low_ec, low_got) + packed_weight(conv_coarse, width),
        low.send_scratch() + low.halo_scratch(),
        10e9,
        smem=2,
        name="coarse",
    )
    got = swap_chunks(send)
    low_got = swap_chunks(low_send)
    low_up, low_dn = swap_rows(low_top, low_bot)

    taps = conv_decode.shape[0]
    split = conv_decode.reshape(taps, width, taps, 2, width)
    body = jnp.transpose(split, (2, 1, 3, 0, 4)).reshape(taps * width, 2 * taps * width)
    sides = jnp.stack([split[:, :, 0], split[:, :, 2]]).reshape(2, taps * width, 2 * width)
    heads = output_head.shape[0]
    flux_ch = heads - OUT_VARS
    eye = jnp.eye(rows, dtype=output_head.dtype)
    head = (output_head[:, None, None, :] * eye[None, :, :, None]).reshape(heads * rows, rows * width)

    slot_count = ocean_state.shape[2]
    cap = slot_count // tiles
    owner_ids = owners[:, 0]
    count = owner_ids.shape[0]
    earlier = np.tril(np.ones((count, count), bool), -1)
    rank = jnp.sum((owner_ids[:, None] == owner_ids[None, :]) & earlier, axis=1).astype(jnp.int32)
    slot_index = owner_ids * cap + rank
    col_key = (np.arange(flux_ch, dtype=np.int32)[:, None] * slot_count + slot_index[None, :]).reshape(1, -1)
    row_key = (
        np.arange(flux_ch, dtype=np.int32)[None, :, None] * slot_count
        + np.arange(slot_count, dtype=np.int32).reshape(tiles, 1, cap)
    ).reshape(-1, 1)
    row_key = jnp.asarray(row_key)
    pred, outgoing = call(
        functools.partial(decode_kernel, full, low, width, OUT_VARS),
        [
            jax.ShapeDtypeStruct((OUT_VARS, faces, rows, side), BF),
            jax.ShapeDtypeStruct((tiles, flux_ch * cap, side), BF),
        ],
        (stripe, seam_table, x2, up, dn, ec, got, y1, low_up, low_dn, low_ec, low_got)
        + (body, sides, spread, head, atmos_state, land_sea, row_key, col_key),
        full.halo_scratch() + low.halo_scratch() + [pltpu.VMEM((flux_ch, faces, rows, side), F32)],
        2 * cells * 18 * width * width,
        smem=2,
        specs={16: pl.BlockSpec((OUT_VARS, faces, rows, side), lambda i: (0, 0, 0, 0))},
        name="decode",
    )
    arrived = lax.all_to_all(outgoing, "tile", split_axis=0, concat_axis=0, tiled=True)

    held = jnp.transpose(ocean_state[0, 0].reshape(tiles, cap, OCEAN_CH, side), (0, 2, 1, 3))
    state = jnp.pad(held, ((0, 0), (0, 0), (0, 8 - cap), (0, 0))).reshape(tiles, OCEAN_CH * 8, side)
    hidden = ocean_in.shape[0]
    high = ocean_in.astype(BF)
    rest = (ocean_in - high.astype(F32)).astype(BF)
    flux_pad = (-flux_ch * cap) % 16
    each = jnp.eye(cap, dtype=BF)
    slot8 = jnp.eye(cap, 8, dtype=BF)

    def flux_part(weights):
        part = each[:, None, None, :] * weights[None, :, OCEAN_CH:, None]
        return jnp.pad(part.reshape(cap * hidden, flux_ch * cap), ((0, 0), (0, flux_pad)))

    def state_part(weights):
        part = slot8[:, None, None, :] * weights[None, :, :OCEAN_CH, None]
        return part.reshape(cap * hidden, OCEAN_CH * 8)

    into = jnp.concatenate(
        [flux_part(high), flux_part(rest), state_part(high), state_part(rest), state_part(high)], axis=1
    )
    out_weight = jnp.broadcast_to(ocean_out[None, :, None], (cap, hidden, LANES)).reshape(-1, LANES)
    sea, back = call(
        functools.partial(ocean_kernel, cap),
        [jax.ShapeDtypeStruct((tiles, 8, side), F32), jax.ShapeDtypeStruct((tiles, 8, side), BF)],
        (arrived, state, into, out_weight),
        [],
        2 * slot_count * side * hidden * 8,
        name="ocean",
    )
    returned = lax.all_to_all(back, "tile", split_axis=0, concat_axis=0, tiled=True)
    key = (owner_ids * 8 + rank)[:, None]
    first = pl.BlockSpec((1, faces, rows, side), lambda i: (0, 0, 0, 0))
    (atmos_next,) = call(
        surface_kernel,
        [jax.ShapeDtypeStruct(pred.shape, BF)],
        (returned, key, land_sea, pred),
        [],
        2 * count * tiles * 8 * side,
        specs={3: first},
        out_specs=[first],
        aliases={3: 0},
        name="surface",
    )
    renewed = jnp.stack([sea[:, :cap], held[:, 0]], axis=2)
    return atmos_next, renewed.reshape(1, 1, slot_count, OCEAN_CH, side)


def fits(mesh):
    return mesh.shape["face"] == 1


def solution(mesh):
    in_specs = (
        P(None, "face", "tile", None),
        P("face", "tile", None),
        P(("face", "tile"), None),
        P(),
        P("face", "tile", None, None, None),
        P(),
        P(),
        P(),
        P(),
        P(),
        P(),
        P(),
    )
    out_specs = (P(None, "face", "tile", None), P("face", "tile", None, None, None))
    return jax.shard_map(
        on_one_group if fits(mesh) else on_device,
        mesh=mesh,
        in_specs=in_specs,
        out_specs=out_specs,
        check_vma=False,
    )
```

```python
import functools

import jax
import jax.numpy as jnp
import numpy as np
from jax import lax
from jax.experimental import pallas as pl
from jax.experimental.pallas import tpu as pltpu
from jax.sharding import PartitionSpec as P

OUT_VARS = 8
FLUX_CH = 4
OCEAN_CH = 2


def extended(shard, sides, width):
    for axis, dim in sides:
        size, length = (lax.axis_size(axis), shard.shape[dim])
        up = [(i, (i + 1) % size) for i in range(size)]
        down = [(j, i) for i, j in up]
        last = lax.slice_in_dim(shard, length - width, length, axis=dim)
        initial = lax.slice_in_dim(shard, 0, width, axis=dim)
        before = lax.ppermute(last, axis, up)
        after = lax.ppermute(initial, axis, down)
        shard = jnp.concatenate([before, shard, after], axis=dim)
    return shard


def pad_field(values, seam_table):
    channels, faces_dev, stripe_rows, face_side = values.shape
    tile_count = lax.axis_size("tile")
    stripe = lax.axis_index("tile")
    face_group = lax.axis_index("face")
    rimmed = extended(values, (("tile", 2),), 1)
    edge_rows = jnp.stack([values[:, :, 0, :], rimmed[:, :, 0, :]], axis=2)
    edge_pieces = edge_rows.reshape(channels, faces_dev, 2, tile_count, stripe_rows)
    received = lax.all_to_all(edge_pieces, "tile", split_axis=3, concat_axis=3, tiled=True)
    row_part = received[:, :, :, 0, :]
    row_start = stripe * stripe_rows
    col_part = jnp.stack([values[:, :, :, 0], values[:, :, :, face_side - 1]], axis=2)
    seam_piece = jnp.concatenate([row_part, col_part], axis=2)
    seam_piece = jnp.transpose(seam_piece, (1, 2, 0, 3)).reshape(
        1, faces_dev, 4, channels * stripe_rows
    )
    own_sides = lax.dynamic_slice_in_dim(seam_table, face_group * (faces_dev * 4), faces_dev * 4, 0)
    gathered = lax.all_gather(seam_piece, ("face", "tile"), axis=0, tiled=True)
    group_count = gathered.shape[0] // tile_count
    strip_table = gathered.reshape(group_count, tile_count, faces_dev, 4, channels, stripe_rows)
    strip_table = jnp.transpose(strip_table, (0, 2, 3, 4, 1, 5)).reshape(
        group_count * faces_dev * 4, channels, face_side
    )
    strips = jnp.take(strip_table, own_sides[:, 0], axis=0)
    strips = jnp.where(own_sides[:, 1][:, None, None] == 1, strips[:, :, ::-1], strips)
    strips = jnp.transpose(strips.reshape(faces_dev, 4, channels, face_side), (2, 0, 1, 3))
    upper_row = jnp.where(stripe == 0, strips[:, :, 0, :], rimmed[:, :, 0, :])
    bottom = jnp.where(
        stripe == tile_count - 1, strips[:, :, 1, :], rimmed[:, :, stripe_rows + 1, :]
    )
    middle = jnp.concatenate([upper_row[:, :, None, :], values, bottom[:, :, None, :]], axis=2)
    zero_cells = jnp.zeros((channels, faces_dev, 2, 1), values.dtype)
    columns = jnp.concatenate([zero_cells, strips[:, :, 2:, :], zero_cells], axis=3)
    columns = lax.dynamic_slice_in_dim(columns, row_start, stripe_rows + 2, 3)
    return jnp.concatenate([columns[:, :, 0, :, None], middle, columns[:, :, 1, :, None]], axis=3)


def convolve(padded, weight):
    channels, faces_dev, rows_two, side_two = padded.shape
    stripe_rows = rows_two - 2
    face_side = side_two - 2
    planes = []
    for face_index in range(faces_dev):
        summed = jnp.zeros((weight.shape[1], stripe_rows * face_side), jnp.float32)
        for row_shift in range(3):
            tap_rows = jnp.concatenate(
                [
                    padded[
                        :,
                        face_index,
                        row_shift : row_shift + stripe_rows,
                        col_shift : col_shift + face_side,
                    ]
                    for col_shift in range(3)
                ],
                axis=0,
            )
            summed = summed + jnp.dot(
                weight[row_shift],
                tap_rows.reshape(3 * channels, stripe_rows * face_side),
                preferred_element_type=jnp.float32,
            )
        planes.append(jax.nn.gelu(summed).astype(jnp.bfloat16).reshape(-1, stripe_rows, face_side))
    return jnp.stack(planes, axis=1)


def upsample(values):
    return jnp.repeat(jnp.repeat(values, 2, axis=2), 2, axis=3)


def ocean_update(held_state, arrived_flux, ocean_in, ocean_out):
    stacked = jnp.concatenate([held_state, arrived_flux.astype(jnp.float32)], axis=1)
    hidden = jax.nn.gelu(
        jnp.einsum("hc,ncs->nhs", ocean_in, stacked, precision=lax.Precision.HIGHEST)
    )
    sea_now = held_state[:, 0] + jnp.einsum(
        "h,nhs->ns", ocean_out, hidden, precision=lax.Precision.HIGHEST
    )
    return jnp.stack([sea_now, held_state[:, 0]], axis=1)


def ocean_blocks(held_state, arrived_flux, ocean_in, ocean_out, block_count):
    slot_count, state_ch, face_side = held_state.shape
    capacity = slot_count // block_count
    held_split = held_state.reshape(block_count, capacity, state_ch, face_side)
    flux_split = arrived_flux.reshape(block_count, capacity, arrived_flux.shape[1], face_side)
    stepped = lax.map(
        lambda pair: ocean_update(pair[0], pair[1], ocean_in, ocean_out), (held_split, flux_split)
    )
    return stepped.reshape(slot_count, state_ch, face_side)


def on_device(
    atmos_state,
    land_sea,
    owners,
    seam_table,
    ocean_state,
    conv_input,
    conv_encode,
    conv_coarse,
    conv_decode,
    output_head,
    ocean_in,
    ocean_out,
):
    encoded = convolve(pad_field(atmos_state, seam_table), conv_input)
    skip_level = convolve(pad_field(encoded, seam_table), conv_encode)
    channels, faces_dev, stripe_rows, face_side = skip_level.shape
    pooled = (
        skip_level.astype(jnp.float32)
        .reshape(channels, faces_dev, stripe_rows // 2, 2, face_side // 2, 2)
        .mean(axis=(3, 5))
        .astype(jnp.bfloat16)
    )
    coarse_out = convolve(pad_field(pooled, seam_table), conv_coarse)
    coarse_pad = upsample(pad_field(coarse_out, seam_table))[
        :, :, 1 : stripe_rows + 3, 1 : face_side + 3
    ]
    padded = jnp.concatenate([pad_field(skip_level, seam_table), coarse_pad], axis=0)
    decoded = convolve(padded, conv_decode)
    head_out = jnp.dot(
        output_head, decoded.reshape(channels, -1), preferred_element_type=jnp.float32
    )
    head_out = head_out.reshape(-1, faces_dev, stripe_rows, face_side)
    predicted = atmos_state[:OUT_VARS].astype(jnp.float32) + head_out[:OUT_VARS]
    is_ocean = land_sea == 1
    fluxes = jnp.where(is_ocean[None], head_out[OUT_VARS:], 0.0).astype(jnp.bfloat16)
    flux_tiles = jnp.transpose(fluxes, (1, 2, 0, 3)).reshape(
        faces_dev * stripe_rows, FLUX_CH * face_side
    )
    tile_count = lax.axis_size("tile")
    owner_ids = owners[:, 0]
    owner_hits = (owner_ids[:, None] == jnp.arange(tile_count)[None, :]).astype(jnp.int32)
    slot_rank = jnp.sum((jnp.cumsum(owner_hits, axis=0) - 1) * owner_hits, axis=1)
    slot_count = ocean_state.shape[2]
    capacity = slot_count // tile_count
    slot_index = owner_ids * capacity + slot_rank
    selector = (jnp.arange(slot_count)[:, None] == slot_index[None, :]).astype(jnp.bfloat16)
    outgoing = jnp.dot(selector, flux_tiles, preferred_element_type=jnp.float32).astype(
        jnp.bfloat16
    )
    outgoing = outgoing.reshape(tile_count, capacity, FLUX_CH, face_side)
    held_state = ocean_state[0, 0]
    arrived = lax.all_to_all(outgoing, "tile", split_axis=0, concat_axis=0, tiled=True)
    renewed = ocean_blocks(
        held_state, arrived.reshape(slot_count, FLUX_CH, face_side), ocean_in, ocean_out, tile_count
    )
    sea_back = renewed[:, 0].astype(jnp.bfloat16).reshape(tile_count, capacity, face_side)
    sea_slots = lax.all_to_all(sea_back, "tile", split_axis=0, concat_axis=0, tiled=True)
    sea_tiles = jnp.dot(
        selector.T, sea_slots.reshape(slot_count, face_side), preferred_element_type=jnp.float32
    )
    sea_temp = sea_tiles.reshape(faces_dev, stripe_rows, face_side)
    surface = jnp.where(is_ocean, sea_temp, predicted[0])
    atmos_next = jnp.concatenate([surface[None], predicted[1:]], axis=0).astype(jnp.bfloat16)
    return (atmos_next, renewed.reshape(1, 1, slot_count, OCEAN_CH, face_side))


GROUP = 16
LANES = 128
VMEM = pltpu.VMEM
BF = jnp.bfloat16
F32 = jnp.float32
NT = (((1,), (1,)), ((), ()))


def mm(a, b):
    return jnp.dot(a, b, preferred_element_type=F32)


def mm_nt(a, b):
    return lax.dot_general(a, b, NT, preferred_element_type=F32)


def iota(shape, dim):
    return lax.broadcasted_iota(jnp.int32, shape, dim)


def smooth(x):
    inner = x * (0.7978845608028654 + 0.03567740813636141 * (x * x))
    half = 0.5 * x
    return half * jnp.tanh(inner) + half


class Field:
    def __init__(self, faces, rows, chans, side, tiles):
        self.faces, self.rows, self.chans, self.side, self.tiles = faces, rows, chans, side, tiles
        self.per = LANES // chans
        self.groups = faces // self.per
        self.span = rows + 2
        self.extra = self.groups * self.span
        used = max(self.extra + 2 * self.groups, 2 * self.groups * rows)
        self.chunk = used + (-used) % 16

    def main(self):
        return jax.ShapeDtypeStruct((self.faces, self.rows, self.chans, self.side), BF)

    def edges(self, more=0):
        edge = jax.ShapeDtypeStruct((self.faces, self.chans, self.side + more), BF)
        return [edge, edge]

    def sends(self):
        return [
            jax.ShapeDtypeStruct((2 * self.faces * 8, self.chans), BF),
            jax.ShapeDtypeStruct((self.tiles, self.chunk, LANES), BF),
        ]

    def send_scratch(self):
        return [
            pltpu.VMEM((2, self.faces, 8, self.chans), F32),
            pltpu.VMEM((self.tiles, self.chunk, LANES), F32),
            pltpu.VMEM((self.side + 8, LANES), F32),
            pltpu.VMEM((16, self.rows * self.side), BF),
        ]

    def halo_scratch(self):
        return [
            pltpu.VMEM((6, self.faces, GROUP, self.chans), F32),
            pltpu.VMEM((2, GROUP * GROUP, self.chans), F32),
            pltpu.VMEM((self.faces, self.chans, self.side), BF),
            pltpu.VMEM((self.faces, self.chans, self.side), BF),
            pltpu.VMEM((2, self.faces, self.chans, self.side), BF),
            pltpu.VMEM((self.tiles, self.chunk, LANES), F32),
            pltpu.VMEM((2, self.faces, 8, self.chans), F32),
        ]


def flip_matrix(size, flag):
    row, col = iota((size, size), 0), iota((size, size), 1)
    return (row == jnp.where(flag == 1, size - 1 - col, col)).astype(F32).astype(BF)


def end_picker(side):
    row, col = iota((16, side), 0), iota((16, side), 1)
    return (((row == 0) & (col == 0)) | ((row == 1) & (col == side - 1))).astype(F32).astype(BF)


def column_picker(fld):
    length = fld.rows * fld.side
    row, col = iota((16, length), 0), iota((16, length), 1)
    want = (row & 7) * fld.side + (row >> 3) * (fld.side - 1)
    return (col == want).astype(F32).astype(BF)


def keep_columns(picker, face_rows, f, cols):
    picked = mm_nt(picker, jnp.concatenate(face_rows, axis=1))
    cols[0, f] = picked[:8]
    cols[1, f] = picked[8:]


def pack_sends(fld, stripe, tab, top, bot, off, ec_out, send_out, cols, stage, strip, picker):
    last, rows, chans, groups, per = fld.tiles - 1, fld.rows, fld.chans, fld.groups, fld.per
    held = cols[...]
    ec_out[...] = held.reshape(2 * fld.faces * 8, chans).astype(BF)
    paired = held.reshape(2, groups, per, 8, chans)
    packed = jnp.concatenate([paired[:, :, j] for j in range(per)], axis=3)
    across = packed[:, :, :rows].reshape(2 * groups * rows, LANES)
    initial = packed[:, :, 0].reshape(2 * groups, LANES)
    final = packed[:, :, rows - 1].reshape(2 * groups, LANES)
    pieces = []
    for q in range(2):
        for g in range(fld.faces):
            p = tab[4 * g + q, 0]
            pieces.append(cols[jnp.maximum((p & 3) - 2, 0), p >> 2][:rows])
    merged = [jnp.concatenate(pieces[n : n + per], axis=1) for n in range(0, len(pieces), per)]
    stage[...] = jnp.zeros_like(stage)
    for q in range(2):
        for i in range(groups):
            stage[q * last, i * fld.span + 1 : i * fld.span + 1 + rows, :] = merged[q * groups + i]

    def lanes(h):
        return slice((h % per) * chans, (h % per + 1) * chans)

    @pl.when((stripe == 0) | (stripe == last))
    def _():
        q = jnp.where(stripe == 0, 0, 1)
        for i in range(groups):
            turned = []
            for h in range(i * per, (i + 1) * per):
                upper = top[h, :, off : off + fld.side].astype(F32)
                lower = bot[h, :, off : off + fld.side].astype(F32)
                cells = jnp.where(q == 0, upper, lower).astype(BF)
                turned.append(mm_nt(flip_matrix(fld.side, tab[4 * h + q, 1]), cells))
            strip[0:8] = jnp.zeros((8, LANES), F32)
            strip[fld.side : fld.side + 8] = jnp.zeros((8, LANES), F32)
            strip[1 : fld.side + 1, :] = jnp.concatenate(turned, axis=1)
            for d in range(1, last, 10):
                here = range(d, min(d + 10, last))
                taken = [strip[e * rows : e * rows + fld.span, :] for e in here]
                for e, piece in zip(here, taken):
                    stage[e, i * fld.span : (i + 1) * fld.span, :] = piece

    stage[last - stripe, : 2 * groups * rows, :] = across

    @pl.when(stripe < last)
    def _():
        stage[last - 1 - stripe, fld.extra : fld.extra + 2 * groups, :] = final

    @pl.when(stripe > 0)
    def _():
        stage[last + 1 - stripe, fld.extra : fld.extra + 2 * groups, :] = initial

    send_out[...] = stage[...].astype(BF)


def gather_halos(fld, stripe, tab, top, bot, up, dn, off, ec, recv, cand, cols, above, below, pair, got, mirror):
    faces, rows, chans, side, tiles = fld.faces, fld.rows, fld.chans, fld.side, fld.tiles
    last = tiles - 1
    groups = fld.groups
    got[...] = recv[...].astype(F32)
    own = ec[...].astype(F32).reshape(2, faces, 8, chans)
    row, col = iota((groups * rows, groups * rows), 0), iota((groups * rows, groups * rows), 1)
    turn = ((row // rows == col // rows) & (row % rows + col % rows == rows - 1)).astype(F32).astype(BF)
    prow, pcol = iota((16, side), 0), iota((16, side), 1)

    def lanes(h):
        return slice((h % fld.per) * chans, (h % fld.per + 1) * chans)

    here = slice(off, off + side)
    above[...] = up[:, :, here]
    below[...] = dn[:, :, here]
    over = mm_nt(end_picker(side), above[...].reshape(faces * chans, side))
    under = mm_nt(end_picker(side), below[...].reshape(faces * chans, side))
    heads = [got[q * last, : fld.extra, :] for q in range(2)]
    before = got[jnp.minimum(last + 1 - stripe, last), fld.extra : fld.extra + 2 * groups, :]
    after = got[jnp.maximum(last - 1 - stripe, 0), fld.extra : fld.extra + 2 * groups, :]
    for s in range(2):
        across = got[last - stripe, s * groups * rows : (s + 1) * groups * rows, :]
        turned = mm(turn, across.astype(BF))
        for h in range(faces):
            i = h // fld.per
            cand[2 + s, h, 0:1] = over[s : s + 1, h * chans : (h + 1) * chans]
            cand[2 + s, h, rows + 1 : rows + 2] = under[s : s + 1, h * chans : (h + 1) * chans]
            cand[2 + s, h, 1 : rows + 1] = own[s, h, :rows]
            mirror[s, h, :rows] = across[i * rows : (i + 1) * rows, lanes(h)]
            cand[4 + s, h, 0:1] = before[s * groups + i : s * groups + i + 1, lanes(h)]
            cand[4 + s, h, rows + 1 : rows + 2] = after[s * groups + i : s * groups + i + 1, lanes(h)]
            cand[4 + s, h, 1 : rows + 1] = turned[i * rows : (i + 1) * rows, lanes(h)]
    at_edge = (stripe == 0) | (stripe == last)

    @pl.when(jnp.logical_not(at_edge))
    def _():
        for q in range(2):
            for h in range(faces):
                i = h // fld.per
                cand[q, h, 0 : fld.span] = heads[q][i * fld.span : (i + 1) * fld.span, lanes(h)]

    @pl.when(at_edge)
    def _():
        q = jnp.where(stripe == 0, 0, 1)
        for h in range(faces):
            pair[0, h] = jnp.where(q == 0, top[h, :, here].astype(F32), below[h].astype(F32)).astype(BF)
            pair[1, h] = jnp.where(q == 0, above[h].astype(F32), bot[h, :, here].astype(F32)).astype(BF)
        place = stripe * rows - 1 + prow
        inside = (place >= 0) & (place < side)
        windows = []
        for s in range(2):
            for h in range(faces):
                want = jnp.where(tab[4 * h + s, 1] == 1, side - 1 - place, place)
                window = ((pcol == want) & inside).astype(F32).astype(BF)
                windows.append(mm_nt(window, pair[s, h]))
        pieces = []
        for g in range(faces):
            p = tab[4 * g + q, 0]
            pieces.append(mirror[jnp.maximum((p & 3) - 2, 0), p >> 2][:rows])
        for s in range(2):
            for h in range(faces):
                cand[s, h] = windows[s * faces + h]
        for i in range(groups):
            merged = jnp.concatenate(pieces[i * fld.per : (i + 1) * fld.per], axis=1)
            got[last - stripe, i * fld.span + 1 : i * fld.span + 1 + rows, :] = merged
        for i in range(groups):
            lined = jnp.concatenate(
                [got[d, i * fld.span + 1 : i * fld.span + 1 + rows, :] for d in range(tiles)], axis=0
            )
            lined = jnp.transpose(lined)
            for j in range(fld.per):
                g = i * fld.per + j
                p = tab[4 * g + q, 0]
                kind, h = p & 3, p >> 2
                near = pair[jnp.minimum(kind, 1), h].astype(F32)
                far = lined[j * chans : (j + 1) * chans]
                cells = jnp.where(kind < 2, near, far).astype(BF)
                placed = mm(cells, flip_matrix(side, tab[4 * g + q, 1])).astype(BF)

                @pl.when(q == 0)
                def _():
                    above[g] = placed

                @pl.when(q == 1)
                def _():
                    below[g] = placed

    slot = iota((GROUP, chans), 0)
    live = (slot < fld.span) & jnp.logical_not(
        ((slot == 0) & (stripe == 0)) | ((slot == rows + 1) & (stripe == last))
    )
    for s in range(2):
        taken = []
        for g in range(faces):
            p = tab[4 * g + 2 + s, 0]
            kind, h = p & 3, p >> 2
            which = jnp.where((kind >= 2) & (tab[4 * g + 2 + s, 1] == 1), kind + 2, kind)
            taken.append(jnp.where(live, cand[which, h], 0.0))
        taken.append(jnp.zeros(((GROUP - faces) * GROUP, chans), F32))
        cols[s] = jnp.concatenate(taken, axis=0)


def column_terms(side_weight, cols, out_ch):
    terms = []
    for s in range(2):
        part = mm_nt(side_weight[s], cols[s])
        size = part.shape[1]
        terms.append(
            part[out_ch : 2 * out_ch]
            + pltpu.roll(part[:out_ch], 1, 1)
            + pltpu.roll(part[2 * out_ch :], size - 1, 1)
        )
    return terms


def face_terms(terms, face_index):
    size = terms[0].shape[1]
    shift = lax.rem(2 * size - GROUP * face_index - 1, size)
    return [pltpu.roll(term, shift, 1)[:, :LANES] for term in terms]


def conv_row(weight, stacked, terms, r, out_ch):
    z = mm(weight, stacked)
    side = z.shape[1]
    left, right = pltpu.roll(z[:out_ch], 1, 1), pltpu.roll(z[2 * out_ch :], side - 1, 1)
    lane = iota((out_ch, LANES), 1)
    first = terms[0] if r == 0 else pltpu.roll(terms[0], LANES - r, 1)
    final = pltpu.roll(terms[1], LANES - 1 - r, 1)
    head = jnp.where(lane == 0, first, left[:, :LANES])
    tail = jnp.where(lane == LANES - 1, final, right[:, side - LANES :])
    if side > LANES:
        left = jnp.concatenate([head, left[:, LANES:]], axis=1)
        right = jnp.concatenate([right[:, : side - LANES], tail], axis=1)
    else:
        left, right = head, tail
    return smooth(z[out_ch : 2 * out_ch] + left + right).astype(BF)


def row_stack(x, above, below, f, rows):
    lines = [above[f]] + [x[0, r] for r in range(rows)] + [below[f]]
    return lambda r: lines[r : r + 3]


def prep_kernel(fld, stripe_ref, tab, atmos, perm, x_out, top, bot, ec_out, send_out, *sends):
    stripe, f = stripe_ref[0], pl.program_id(0)

    @pl.when(f == 0)
    def _():
        sends[3][...] = column_picker(fld)

    block = atmos[...].astype(F32).reshape(fld.chans * fld.rows, fld.side).astype(BF)
    moved = mm(perm[...], block).astype(BF)
    lines = [moved[r * fld.chans : (r + 1) * fld.chans] for r in range(fld.rows)]
    for r in range(fld.rows):
        x_out[0, r] = lines[r]
    top[f] = lines[0]
    bot[f] = lines[-1]
    keep_columns(sends[3][...], lines, f, sends[0])

    @pl.when(f == fld.faces - 1)
    def _():
        pack_sends(fld, stripe, tab, top, bot, 0, ec_out, send_out, *sends)


def level_kernel(fld, out_fld, low, off, stripe_ref, tab, x, old_top, old_bot, up, dn, ec, recv, weight, side_weight, *refs):
    stripe, f = stripe_ref[0], pl.program_id(0)
    if low is None:
        outs, sends, halos = refs[:5], refs[5:9], refs[9:]
        x_out, top, bot, ec_out, send_out = outs
    else:
        pool, outs, sends, low_sends, halos = refs[0], refs[1:9], refs[9:13], refs[13:17], refs[17:]
        x_out, y_out, top, bot, ec_out, send_out, low_ec, low_send = outs
    *halos, ends_ref = halos
    _, cols, above, below = halos[:4]
    side = fld.side

    @pl.when(f == 0)
    def _():
        gather_halos(fld, stripe, tab, old_top, old_bot, up, dn, off, ec, recv, *halos)
        terms = column_terms(side_weight, [cols[0].astype(BF), cols[1].astype(BF)], out_fld.chans)
        ends_ref[0], ends_ref[1] = terms
        sends[3][...] = column_picker(out_fld)
        if low is not None:
            low_sends[3][...] = column_picker(low)

    lines = row_stack(x, above, below, f, fld.rows)
    ends = face_terms([ends_ref[0], ends_ref[1]], f)
    made, pooled = [], []
    for r in range(fld.rows):
        cells = conv_row(weight[...], jnp.concatenate(lines(r), axis=0), ends, r, out_fld.chans)
        x_out[0, r] = cells
        made.append(cells)
        if low is not None and r % 2 == 1:
            mean = (mm(made[r - 1], pool[...]) + mm(cells, pool[...])).astype(BF)
            y_out[0, r // 2] = mean
            pooled.append(mean)
    top[f, :, :side] = made[0]
    bot[f, :, :side] = made[-1]
    keep_columns(sends[3][...], made, f, sends[0])
    if low is not None:
        top[f, :, side:] = pooled[0]
        bot[f, :, side:] = pooled[-1]
        keep_columns(low_sends[3][...], pooled, f, low_sends[0])

    @pl.when(f == fld.faces - 1)
    def _():
        if low is not None:
            pack_sends(low, stripe, tab, top, bot, side, low_ec, low_send, *low_sends)
        pack_sends(out_fld, stripe, tab, top, bot, 0, ec_out, send_out, *sends)


def decode_kernel(fld, low, out_ch, vars_out, stripe_ref, tab, x, top, bot, up, dn, ec, recv, y, low_top, low_bot, yup, ydn, yec, yrecv, weight, side_weight, spread, head, atmos, land, row_key, col_key, pred_out, flux_out, *refs):
    halos, low_halos, flux, ends_ref = refs[:7], refs[7:14], refs[14], refs[15]
    stripe, f = stripe_ref[0], pl.program_id(0)
    _, cols, above, below = halos[:4]
    _, low_cols, low_above, low_below = low_halos[:4]

    @pl.when(f == 0)
    def _():
        gather_halos(low, stripe, tab, low_top, low_bot, yup, ydn, 0, yec, yrecv, *low_halos)
        gather_halos(fld, stripe, tab, top, bot, up, dn, 0, ec, recv, *halos)
        size = GROUP * GROUP
        row, col = iota((size, size), 0), iota((size, size), 1)
        widen = (col == (row // GROUP) * GROUP + (row % GROUP + 1) // 2).astype(F32).astype(BF)
        joined = []
        for s in range(2):
            wide = mm(widen, low_cols[s].astype(BF))
            joined.append(jnp.concatenate([cols[s], wide], axis=1).astype(BF))
        ends_ref[0], ends_ref[1] = column_terms(side_weight, joined, out_ch)

    lines = row_stack(x, above, below, f, fld.rows)
    ends = face_terms([ends_ref[0], ends_ref[1]], f)
    low_lines = [low_above[f]] + [y[0, r] for r in range(low.rows)] + [low_below[f]]
    wide = [mm(cells, spread[...]).astype(BF) for cells in low_lines]
    made = []
    for r in range(fld.rows):
        picked = [wide[(r + a + 1) // 2] for a in range(3)]
        made.append(
            conv_row(weight[...], jnp.concatenate(lines(r) + picked, axis=0), ends, r, out_ch)
        )
    result = mm(head[...], jnp.concatenate(made, axis=0)).reshape(-1, fld.rows, fld.side)
    pred_out[:, 0] = (atmos[:, 0].astype(F32) + result[:vars_out]).astype(BF)
    flux[:, f] = jnp.where((land[0] == 1)[None], result[vars_out:], 0.0)

    @pl.when(f == fld.faces - 1)
    def _():
        chosen = (row_key[...] == col_key[...]).astype(F32).astype(BF)
        tiles = flux[...].reshape(-1, fld.side).astype(BF)
        flux_out[...] = mm(chosen, tiles).astype(BF).reshape(flux_out.shape)


def ocean_kernel(cap, recv, state, into, out_weight, sea_out, back_out):
    tiles, _, side = recv.shape

    def one_source(t, carry):
        flux = recv[t].astype(F32)
        pad = (-flux.shape[0]) % 16
        flux = jnp.concatenate([flux, jnp.zeros((pad, side), F32)], axis=0).astype(BF)
        held = state[t]
        high = held.astype(BF)
        low = (held - high.astype(F32)).astype(BF)
        hidden = smooth(mm(into[...], jnp.concatenate([flux, flux, high, high, low], axis=0)))
        width = out_weight[...]
        wide = jnp.concatenate([width] * (side // LANES), axis=1)
        drift = (hidden * wide).reshape(cap, -1, side).sum(axis=1)
        drift = jnp.concatenate([drift, jnp.zeros((8 - cap, side), F32)], axis=0)
        sea = held[:8] + drift
        sea_out[t] = sea
        back_out[t] = sea.astype(BF)
        return carry

    lax.fori_loop(0, tiles, one_source, 0)


def surface_kernel(back, key, land, pred, out):
    faces, rows, side = land.shape
    slots = back[...].astype(F32).reshape(-1, side).astype(BF)
    chosen = (key[...] == iota((faces * rows, slots.shape[0]), 1)).astype(F32).astype(BF)
    sea = mm(chosen, slots).reshape(faces, rows, side)
    out[0] = jnp.where(land[...] == 1, sea, pred[0].astype(F32)).astype(BF)


def call(kernel, outs, ins, scratch, flops, smem=0, steps=1, specs=None, aliases=None, out_specs=None, name=None):
    whole = pl.BlockSpec(memory_space=pltpu.VMEM)
    in_specs = [pl.BlockSpec(memory_space=pltpu.SMEM)] * smem + [whole] * (len(ins) - smem)
    for position, spec in (specs or {}).items():
        in_specs[position] = spec
    grid = {"grid": (steps,)} if specs else {}
    moved = sum(int(np.prod(a.shape)) * a.dtype.itemsize for a in list(ins) + list(outs))
    return pl.pallas_call(
        kernel,
        out_shape=outs,
        **grid,
        in_specs=in_specs,
        out_specs=[(out_specs or {}).get(n, whole) for n in range(len(outs))],
        scratch_shapes=scratch,
        input_output_aliases=aliases or {},
        compiler_params=pltpu.CompilerParams(vmem_limit_bytes=30 * 1024 * 1024),
        cost_estimate=pl.CostEstimate(flops=int(flops), bytes_accessed=int(moved), transcendentals=0),
        name=name,
    )(*ins)


def swap_rows(top, bot):
    tiles = lax.axis_size("tile")
    ring = [(i, (i + 1) % tiles) for i in range(tiles)]
    up = lax.ppermute(bot, "tile", ring)
    return up, lax.ppermute(top, "tile", [(j, i) for i, j in ring])


def swap_chunks(chunks):
    return lax.all_to_all(chunks, "tile", split_axis=0, concat_axis=0, tiled=True)


def packed_weight(weight, chans):
    taps, out_ch, _ = weight.shape
    split = weight.reshape(taps, out_ch, taps, chans)
    body = jnp.transpose(split, (2, 1, 0, 3)).reshape(taps * out_ch, taps * chans)
    sides = jnp.stack([split[:, :, 0], split[:, :, 2]]).reshape(2, taps * out_ch, chans)
    return body, sides


def on_one_group(
    atmos_state,
    land_sea,
    owners,
    seam_table,
    ocean_state,
    conv_input,
    conv_encode,
    conv_coarse,
    conv_decode,
    output_head,
    ocean_in,
    ocean_out,
):
    in_ch, faces, rows, side = atmos_state.shape
    tiles = lax.axis_size("tile")
    width = conv_input.shape[1]
    stripe = lax.axis_index("tile").astype(jnp.int32).reshape(1)
    entry = Field(faces, rows, in_ch, side, tiles)
    full = Field(faces, rows, width, side, tiles)
    low = Field(faces, rows // 2, width, side // 2, tiles)
    cells = faces * rows * side

    order = np.arange(in_ch * rows)
    perm = np.zeros((in_ch * rows, in_ch * rows), np.float32)
    perm[order, (order % in_ch) * rows + order // in_ch] = 1.0
    spread = np.zeros((side // 2, side), np.float32)
    spread[np.arange(side) // 2, np.arange(side)] = 1.0
    perm, pool = jnp.asarray(perm, BF), jnp.asarray(0.25 * spread.T, BF)
    spread = jnp.asarray(spread, BF)

    def one(shape, dim=0):
        block = tuple(1 if n == dim else size for n, size in enumerate(shape))
        return pl.BlockSpec(block, lambda i: tuple(i if n == dim else 0 for n in range(len(shape))))

    ends = [pltpu.VMEM((2, width, GROUP * GROUP), F32)]
    x0, top, bot, ec, send = call(
        functools.partial(prep_kernel, entry),
        [entry.main()] + entry.edges() + entry.sends(),
        (stripe, seam_table, atmos_state, perm),
        entry.send_scratch(),
        2 * cells * in_ch * in_ch * rows,
        smem=2,
        steps=faces,
        specs={2: one(atmos_state.shape, 1)},
        out_specs={0: one(entry.main().shape)},
        name="prep",
    )
    got = swap_chunks(send)
    up, dn = swap_rows(top, bot)
    x1, top, bot, ec, send = call(
        functools.partial(level_kernel, entry, full, None, 0),
        [full.main()] + full.edges() + full.sends(),
        (stripe, seam_table, x0, top, bot, up, dn, ec, got) + packed_weight(conv_input, in_ch),
        full.send_scratch() + entry.halo_scratch() + ends,
        2 * cells * 9 * in_ch * width,
        smem=2,
        steps=faces,
        specs={2: one(x0.shape)},
        out_specs={0: one(full.main().shape)},
        name="conv_in",
    )
    got = swap_chunks(send)
    up, dn = swap_rows(top, bot)
    x2, y0, top, bot, ec, send, low_ec, low_send = call(
        functools.partial(level_kernel, full, full, low, 0),
        [full.main(), low.main()] + full.edges(side // 2) + full.sends() + low.sends(),
        (stripe, seam_table, x1, top, bot, up, dn, ec, got) + packed_weight(conv_encode, width) + (pool,),
        full.send_scratch() + low.send_scratch() + full.halo_scratch() + ends,
        2 * cells * 9 * width * width,
        smem=2,
        steps=faces,
        specs={2: one(x1.shape)},
        out_specs={0: one(full.main().shape), 1: one(low.main().shape)},
        name="encode",
    )
    low_got = swap_chunks(low_send)
    up, dn = swap_rows(top, bot)
    y1, low_top, low_bot, low_ec, low_send = call(
        functools.partial(level_kernel, low, low, None, side),
        [low.main()] + low.edges() + low.sends(),
        (stripe, seam_table, y0, top, bot, up, dn, low_ec, low_got) + packed_weight(conv_coarse, width),
        low.send_scratch() + low.halo_scratch() + ends,
        10e9,
        smem=2,
        steps=faces,
        specs={2: one(y0.shape)},
        out_specs={0: one(low.main().shape)},
        name="coarse",
    )
    low_send, got = lax.optimization_barrier((low_send, swap_chunks(send)))
    low_got = swap_chunks(low_send)
    low_up, low_dn = swap_rows(low_top, low_bot)

    taps = conv_decode.shape[0]
    split = conv_decode.reshape(taps, width, taps, 2, width)
    body = jnp.transpose(split, (2, 1, 3, 0, 4)).reshape(taps * width, 2 * taps * width)
    sides = jnp.stack([split[:, :, 0], split[:, :, 2]]).reshape(2, taps * width, 2 * width)
    heads = output_head.shape[0]
    flux_ch = heads - OUT_VARS
    eye = jnp.eye(rows, dtype=output_head.dtype)
    head = (output_head[:, None, None, :] * eye[None, :, :, None]).reshape(heads * rows, rows * width)

    slot_count = ocean_state.shape[2]
    cap = slot_count // tiles
    owner_ids = owners[:, 0]
    count = owner_ids.shape[0]
    earlier = np.tril(np.ones((count, count), bool), -1)
    rank = jnp.sum((owner_ids[:, None] == owner_ids[None, :]) & earlier, axis=1).astype(jnp.int32)
    slot_index = owner_ids * cap + rank
    col_key = (np.arange(flux_ch, dtype=np.int32)[:, None] * slot_count + slot_index[None, :]).reshape(1, -1)
    row_key = (
        np.arange(flux_ch, dtype=np.int32)[None, :, None] * slot_count
        + np.arange(slot_count, dtype=np.int32).reshape(tiles, 1, cap)
    ).reshape(-1, 1)
    row_key = jnp.asarray(row_key)
    pred, outgoing = call(
        functools.partial(decode_kernel, full, low, width, OUT_VARS),
        [
            jax.ShapeDtypeStruct((OUT_VARS, faces, rows, side), BF),
            jax.ShapeDtypeStruct((tiles, flux_ch * cap, side), BF),
        ],
        (stripe, seam_table, x2, top, bot, up, dn, ec, got)
        + (y1, low_top, low_bot, low_up, low_dn, low_ec, low_got)
        + (body, sides, spread, head, atmos_state, land_sea, row_key, col_key),
        full.halo_scratch()
        + low.halo_scratch()
        + [pltpu.VMEM((flux_ch, faces, rows, side), F32)]
        + ends,
        2 * cells * 18 * width * width,
        smem=2,
        steps=faces,
        specs={
            2: one(x2.shape),
            9: one(y1.shape),
            20: pl.BlockSpec((OUT_VARS, 1, rows, side), lambda i: (0, i, 0, 0)),
            21: one(land_sea.shape),
        },
        out_specs={0: one((OUT_VARS, faces, rows, side), 1)},
        name="decode",
    )
    arrived = lax.all_to_all(outgoing, "tile", split_axis=0, concat_axis=0, tiled=True)

    held = jnp.transpose(ocean_state[0, 0].reshape(tiles, cap, OCEAN_CH, side), (0, 2, 1, 3))
    state = jnp.pad(held, ((0, 0), (0, 0), (0, 8 - cap), (0, 0))).reshape(tiles, OCEAN_CH * 8, side)
    hidden = ocean_in.shape[0]
    high = ocean_in.astype(BF)
    rest = (ocean_in - high.astype(F32)).astype(BF)
    flux_pad = (-flux_ch * cap) % 16
    each = jnp.eye(cap, dtype=BF)
    slot8 = jnp.eye(cap, 8, dtype=BF)

    def flux_part(weights):
        part = each[:, None, None, :] * weights[None, :, OCEAN_CH:, None]
        return jnp.pad(part.reshape(cap * hidden, flux_ch * cap), ((0, 0), (0, flux_pad)))

    def state_part(weights):
        part = slot8[:, None, None, :] * weights[None, :, :OCEAN_CH, None]
        return part.reshape(cap * hidden, OCEAN_CH * 8)

    into = jnp.concatenate(
        [flux_part(high), flux_part(rest), state_part(high), state_part(rest), state_part(high)], axis=1
    )
    out_weight = jnp.broadcast_to(ocean_out[None, :, None], (cap, hidden, LANES)).reshape(-1, LANES)
    sea, back = call(
        functools.partial(ocean_kernel, cap),
        [jax.ShapeDtypeStruct((tiles, 8, side), F32), jax.ShapeDtypeStruct((tiles, 8, side), BF)],
        (arrived, state, into, out_weight),
        [],
        2 * slot_count * side * hidden * 8,
        name="ocean",
    )
    returned = lax.all_to_all(back, "tile", split_axis=0, concat_axis=0, tiled=True)
    key = (owner_ids * 8 + rank)[:, None]
    first = pl.BlockSpec((1, faces, rows, side), lambda i: (0, 0, 0, 0))
    (atmos_next,) = call(
        surface_kernel,
        [jax.ShapeDtypeStruct(pred.shape, BF)],
        (returned, key, land_sea, pred),
        [],
        2 * count * tiles * 8 * side,
        specs={3: first},
        out_specs={0: first},
        aliases={3: 0},
        name="surface",
    )
    renewed = jnp.stack([sea[:, :cap], held[:, 0]], axis=2)
    return atmos_next, renewed.reshape(1, 1, slot_count, OCEAN_CH, side)


def fits(mesh):
    return mesh.shape["face"] == 1


def solution(mesh):
    in_specs = (
        P(None, "face", "tile", None),
        P("face", "tile", None),
        P(("face", "tile"), None),
        P(),
        P("face", "tile", None, None, None),
        P(),
        P(),
        P(),
        P(),
        P(),
        P(),
        P(),
    )
    out_specs = (P(None, "face", "tile", None), P("face", "tile", None, None, None))
    return jax.shard_map(
        on_one_group if fits(mesh) else on_device,
        mesh=mesh,
        in_specs=in_specs,
        out_specs=out_specs,
        check_vma=False,
    )
```

```python
import functools

import jax
import jax.numpy as jnp
import numpy as np
from jax import lax
from jax.experimental import pallas as pl
from jax.experimental.pallas import tpu as pltpu
from jax.sharding import PartitionSpec as P

OUT_VARS = 8
FLUX_CH = 4
OCEAN_CH = 2


def extended(shard, sides, width):
    for axis, dim in sides:
        size, length = (lax.axis_size(axis), shard.shape[dim])
        up = [(i, (i + 1) % size) for i in range(size)]
        down = [(j, i) for i, j in up]
        last = lax.slice_in_dim(shard, length - width, length, axis=dim)
        initial = lax.slice_in_dim(shard, 0, width, axis=dim)
        before = lax.ppermute(last, axis, up)
        after = lax.ppermute(initial, axis, down)
        shard = jnp.concatenate([before, shard, after], axis=dim)
    return shard


def pad_field(values, seam_table):
    channels, faces_dev, stripe_rows, face_side = values.shape
    tile_count = lax.axis_size("tile")
    stripe = lax.axis_index("tile")
    face_group = lax.axis_index("face")
    rimmed = extended(values, (("tile", 2),), 1)
    edge_rows = jnp.stack([values[:, :, 0, :], rimmed[:, :, 0, :]], axis=2)
    edge_pieces = edge_rows.reshape(channels, faces_dev, 2, tile_count, stripe_rows)
    received = lax.all_to_all(edge_pieces, "tile", split_axis=3, concat_axis=3, tiled=True)
    row_part = received[:, :, :, 0, :]
    row_start = stripe * stripe_rows
    col_part = jnp.stack([values[:, :, :, 0], values[:, :, :, face_side - 1]], axis=2)
    seam_piece = jnp.concatenate([row_part, col_part], axis=2)
    seam_piece = jnp.transpose(seam_piece, (1, 2, 0, 3)).reshape(
        1, faces_dev, 4, channels * stripe_rows
    )
    own_sides = lax.dynamic_slice_in_dim(seam_table, face_group * (faces_dev * 4), faces_dev * 4, 0)
    gathered = lax.all_gather(seam_piece, ("face", "tile"), axis=0, tiled=True)
    group_count = gathered.shape[0] // tile_count
    strip_table = gathered.reshape(group_count, tile_count, faces_dev, 4, channels, stripe_rows)
    strip_table = jnp.transpose(strip_table, (0, 2, 3, 4, 1, 5)).reshape(
        group_count * faces_dev * 4, channels, face_side
    )
    strips = jnp.take(strip_table, own_sides[:, 0], axis=0)
    strips = jnp.where(own_sides[:, 1][:, None, None] == 1, strips[:, :, ::-1], strips)
    strips = jnp.transpose(strips.reshape(faces_dev, 4, channels, face_side), (2, 0, 1, 3))
    upper_row = jnp.where(stripe == 0, strips[:, :, 0, :], rimmed[:, :, 0, :])
    bottom = jnp.where(
        stripe == tile_count - 1, strips[:, :, 1, :], rimmed[:, :, stripe_rows + 1, :]
    )
    middle = jnp.concatenate([upper_row[:, :, None, :], values, bottom[:, :, None, :]], axis=2)
    zero_cells = jnp.zeros((channels, faces_dev, 2, 1), values.dtype)
    columns = jnp.concatenate([zero_cells, strips[:, :, 2:, :], zero_cells], axis=3)
    columns = lax.dynamic_slice_in_dim(columns, row_start, stripe_rows + 2, 3)
    return jnp.concatenate([columns[:, :, 0, :, None], middle, columns[:, :, 1, :, None]], axis=3)


def convolve(padded, weight):
    channels, faces_dev, rows_two, side_two = padded.shape
    stripe_rows = rows_two - 2
    face_side = side_two - 2
    planes = []
    for face_index in range(faces_dev):
        summed = jnp.zeros((weight.shape[1], stripe_rows * face_side), jnp.float32)
        for row_shift in range(3):
            tap_rows = jnp.concatenate(
                [
                    padded[
                        :,
                        face_index,
                        row_shift : row_shift + stripe_rows,
                        col_shift : col_shift + face_side,
                    ]
                    for col_shift in range(3)
                ],
                axis=0,
            )
            summed = summed + jnp.dot(
                weight[row_shift],
                tap_rows.reshape(3 * channels, stripe_rows * face_side),
                preferred_element_type=jnp.float32,
            )
        planes.append(jax.nn.gelu(summed).astype(jnp.bfloat16).reshape(-1, stripe_rows, face_side))
    return jnp.stack(planes, axis=1)


def upsample(values):
    return jnp.repeat(jnp.repeat(values, 2, axis=2), 2, axis=3)


def ocean_update(held_state, arrived_flux, ocean_in, ocean_out):
    stacked = jnp.concatenate([held_state, arrived_flux.astype(jnp.float32)], axis=1)
    hidden = jax.nn.gelu(
        jnp.einsum("hc,ncs->nhs", ocean_in, stacked, precision=lax.Precision.HIGHEST)
    )
    sea_now = held_state[:, 0] + jnp.einsum(
        "h,nhs->ns", ocean_out, hidden, precision=lax.Precision.HIGHEST
    )
    return jnp.stack([sea_now, held_state[:, 0]], axis=1)


def ocean_blocks(held_state, arrived_flux, ocean_in, ocean_out, block_count):
    slot_count, state_ch, face_side = held_state.shape
    capacity = slot_count // block_count
    held_split = held_state.reshape(block_count, capacity, state_ch, face_side)
    flux_split = arrived_flux.reshape(block_count, capacity, arrived_flux.shape[1], face_side)
    stepped = lax.map(
        lambda pair: ocean_update(pair[0], pair[1], ocean_in, ocean_out), (held_split, flux_split)
    )
    return stepped.reshape(slot_count, state_ch, face_side)


def on_device(
    atmos_state,
    land_sea,
    owners,
    seam_table,
    ocean_state,
    conv_input,
    conv_encode,
    conv_coarse,
    conv_decode,
    output_head,
    ocean_in,
    ocean_out,
):
    encoded = convolve(pad_field(atmos_state, seam_table), conv_input)
    skip_level = convolve(pad_field(encoded, seam_table), conv_encode)
    channels, faces_dev, stripe_rows, face_side = skip_level.shape
    pooled = (
        skip_level.astype(jnp.float32)
        .reshape(channels, faces_dev, stripe_rows // 2, 2, face_side // 2, 2)
        .mean(axis=(3, 5))
        .astype(jnp.bfloat16)
    )
    coarse_out = convolve(pad_field(pooled, seam_table), conv_coarse)
    coarse_pad = upsample(pad_field(coarse_out, seam_table))[
        :, :, 1 : stripe_rows + 3, 1 : face_side + 3
    ]
    padded = jnp.concatenate([pad_field(skip_level, seam_table), coarse_pad], axis=0)
    decoded = convolve(padded, conv_decode)
    head_out = jnp.dot(
        output_head, decoded.reshape(channels, -1), preferred_element_type=jnp.float32
    )
    head_out = head_out.reshape(-1, faces_dev, stripe_rows, face_side)
    predicted = atmos_state[:OUT_VARS].astype(jnp.float32) + head_out[:OUT_VARS]
    is_ocean = land_sea == 1
    fluxes = jnp.where(is_ocean[None], head_out[OUT_VARS:], 0.0).astype(jnp.bfloat16)
    flux_tiles = jnp.transpose(fluxes, (1, 2, 0, 3)).reshape(
        faces_dev * stripe_rows, FLUX_CH * face_side
    )
    tile_count = lax.axis_size("tile")
    owner_ids = owners[:, 0]
    owner_hits = (owner_ids[:, None] == jnp.arange(tile_count)[None, :]).astype(jnp.int32)
    slot_rank = jnp.sum((jnp.cumsum(owner_hits, axis=0) - 1) * owner_hits, axis=1)
    slot_count = ocean_state.shape[2]
    capacity = slot_count // tile_count
    slot_index = owner_ids * capacity + slot_rank
    selector = (jnp.arange(slot_count)[:, None] == slot_index[None, :]).astype(jnp.bfloat16)
    outgoing = jnp.dot(selector, flux_tiles, preferred_element_type=jnp.float32).astype(
        jnp.bfloat16
    )
    outgoing = outgoing.reshape(tile_count, capacity, FLUX_CH, face_side)
    held_state = ocean_state[0, 0]
    arrived = lax.all_to_all(outgoing, "tile", split_axis=0, concat_axis=0, tiled=True)
    renewed = ocean_blocks(
        held_state, arrived.reshape(slot_count, FLUX_CH, face_side), ocean_in, ocean_out, tile_count
    )
    sea_back = renewed[:, 0].astype(jnp.bfloat16).reshape(tile_count, capacity, face_side)
    sea_slots = lax.all_to_all(sea_back, "tile", split_axis=0, concat_axis=0, tiled=True)
    sea_tiles = jnp.dot(
        selector.T, sea_slots.reshape(slot_count, face_side), preferred_element_type=jnp.float32
    )
    sea_temp = sea_tiles.reshape(faces_dev, stripe_rows, face_side)
    surface = jnp.where(is_ocean, sea_temp, predicted[0])
    atmos_next = jnp.concatenate([surface[None], predicted[1:]], axis=0).astype(jnp.bfloat16)
    return (atmos_next, renewed.reshape(1, 1, slot_count, OCEAN_CH, face_side))


GROUP = 16
LANES = 128
VMEM = pltpu.VMEM
BF = jnp.bfloat16
F32 = jnp.float32
NT = (((1,), (1,)), ((), ()))


def mm(a, b):
    return jnp.dot(a, b, preferred_element_type=F32)


def mm_nt(a, b):
    return lax.dot_general(a, b, NT, preferred_element_type=F32)


def iota(shape, dim):
    return lax.broadcasted_iota(jnp.int32, shape, dim)


def smooth(x):
    inner = x * (0.7978845608028654 + 0.03567740813636141 * (x * x))
    half = 0.5 * x
    return half * jnp.tanh(inner) + half


class Field:
    def __init__(self, faces, rows, chans, side, tiles):
        self.faces, self.rows, self.chans, self.side, self.tiles = faces, rows, chans, side, tiles
        self.per = LANES // chans
        self.groups = faces // self.per
        self.span = rows + 2
        self.extra = self.groups * self.span
        used = max(self.extra + 2 * self.groups, 2 * self.groups * rows)
        self.chunk = used + (-used) % 16

    def main(self):
        return jax.ShapeDtypeStruct((self.faces, self.rows, self.chans, self.side), BF)

    def edges(self, more=0):
        edge = jax.ShapeDtypeStruct((self.faces, self.chans, self.side + more), BF)
        return [edge, edge]

    def sends(self):
        return [
            jax.ShapeDtypeStruct((2 * self.faces * 8, self.chans), BF),
            jax.ShapeDtypeStruct((self.tiles, self.chunk, LANES), BF),
        ]

    def send_scratch(self):
        return [
            pltpu.VMEM((2, self.faces, 8, self.chans), F32),
            pltpu.VMEM((self.tiles, self.chunk, LANES), F32),
            pltpu.VMEM((self.side + 8, LANES), F32),
            pltpu.VMEM((16, self.rows * self.side), BF),
        ]

    def halo_scratch(self):
        return [
            pltpu.VMEM((6, self.faces, GROUP, self.chans), F32),
            pltpu.VMEM((2, GROUP * GROUP, self.chans), F32),
            pltpu.VMEM((self.faces, self.chans, self.side), BF),
            pltpu.VMEM((self.faces, self.chans, self.side), BF),
            pltpu.VMEM((2, self.faces, self.chans, self.side), BF),
            pltpu.VMEM((self.tiles, self.chunk, LANES), F32),
            pltpu.VMEM((2, self.faces, 8, self.chans), F32),
        ]


def flip_matrix(size, flag):
    row, col = iota((size, size), 0), iota((size, size), 1)
    return (row == jnp.where(flag == 1, size - 1 - col, col)).astype(F32).astype(BF)


def end_picker(side):
    row, col = iota((16, side), 0), iota((16, side), 1)
    return (((row == 0) & (col == 0)) | ((row == 1) & (col == side - 1))).astype(F32).astype(BF)


def column_picker(fld):
    length = fld.rows * fld.side
    row, col = iota((16, length), 0), iota((16, length), 1)
    want = (row & 7) * fld.side + (row >> 3) * (fld.side - 1)
    return (col == want).astype(F32).astype(BF)


def keep_columns(picker, face_rows, f, cols):
    picked = mm_nt(picker, jnp.concatenate(face_rows, axis=1))
    cols[0, f] = picked[:8]
    cols[1, f] = picked[8:]


def pack_sends(fld, stripe, tab, top, bot, off, ec_out, send_out, cols, stage, strip, picker):
    last, rows, chans, groups, per = fld.tiles - 1, fld.rows, fld.chans, fld.groups, fld.per
    held = cols[...]
    ec_out[...] = held.reshape(2 * fld.faces * 8, chans).astype(BF)
    paired = held.reshape(2, groups, per, 8, chans)
    packed = jnp.concatenate([paired[:, :, j] for j in range(per)], axis=3)
    across = packed[:, :, :rows].reshape(2 * groups * rows, LANES)
    initial = packed[:, :, 0].reshape(2 * groups, LANES)
    final = packed[:, :, rows - 1].reshape(2 * groups, LANES)
    pieces = []
    for q in range(2):
        for g in range(fld.faces):
            p = tab[4 * g + q, 0]
            pieces.append(cols[jnp.maximum((p & 3) - 2, 0), p >> 2][:rows])
    merged = [jnp.concatenate(pieces[n : n + per], axis=1) for n in range(0, len(pieces), per)]
    stage[...] = jnp.zeros_like(stage)
    for q in range(2):
        for i in range(groups):
            stage[q * last, i * fld.span + 1 : i * fld.span + 1 + rows, :] = merged[q * groups + i]

    def lanes(h):
        return slice((h % per) * chans, (h % per + 1) * chans)

    @pl.when((stripe == 0) | (stripe == last))
    def _():
        q = jnp.where(stripe == 0, 0, 1)
        for i in range(groups):
            turned = []
            for h in range(i * per, (i + 1) * per):
                upper = top[h, :, off : off + fld.side].astype(F32)
                lower = bot[h, :, off : off + fld.side].astype(F32)
                cells = jnp.where(q == 0, upper, lower).astype(BF)
                turned.append(mm_nt(flip_matrix(fld.side, tab[4 * h + q, 1]), cells))
            strip[0:8] = jnp.zeros((8, LANES), F32)
            strip[fld.side : fld.side + 8] = jnp.zeros((8, LANES), F32)
            strip[1 : fld.side + 1, :] = jnp.concatenate(turned, axis=1)
            for d in range(1, last, 10):
                here = range(d, min(d + 10, last))
                taken = [strip[e * rows : e * rows + fld.span, :] for e in here]
                for e, piece in zip(here, taken):
                    stage[e, i * fld.span : (i + 1) * fld.span, :] = piece

    stage[last - stripe, : 2 * groups * rows, :] = across

    @pl.when(stripe < last)
    def _():
        stage[last - 1 - stripe, fld.extra : fld.extra + 2 * groups, :] = final

    @pl.when(stripe > 0)
    def _():
        stage[last + 1 - stripe, fld.extra : fld.extra + 2 * groups, :] = initial

    send_out[...] = stage[...].astype(BF)


def gather_halos(fld, stripe, tab, top, bot, up, dn, off, ec, recv, cand, cols, above, below, pair, got, mirror):
    faces, rows, chans, side, tiles = fld.faces, fld.rows, fld.chans, fld.side, fld.tiles
    last = tiles - 1
    groups = fld.groups
    got[...] = recv[...].astype(F32)
    own = ec[...].astype(F32).reshape(2, faces, 8, chans)
    row, col = iota((groups * rows, groups * rows), 0), iota((groups * rows, groups * rows), 1)
    turn = ((row // rows == col // rows) & (row % rows + col % rows == rows - 1)).astype(F32).astype(BF)
    prow, pcol = iota((16, side), 0), iota((16, side), 1)

    def lanes(h):
        return slice((h % fld.per) * chans, (h % fld.per + 1) * chans)

    here = slice(off, off + side)
    above[...] = up[:, :, here]
    below[...] = dn[:, :, here]
    over = mm_nt(end_picker(side), above[...].reshape(faces * chans, side))
    under = mm_nt(end_picker(side), below[...].reshape(faces * chans, side))
    heads = [got[q * last, : fld.extra, :] for q in range(2)]
    before = got[jnp.minimum(last + 1 - stripe, last), fld.extra : fld.extra + 2 * groups, :]
    after = got[jnp.maximum(last - 1 - stripe, 0), fld.extra : fld.extra + 2 * groups, :]
    for s in range(2):
        across = got[last - stripe, s * groups * rows : (s + 1) * groups * rows, :]
        turned = mm(turn, across.astype(BF))
        for h in range(faces):
            i = h // fld.per
            cand[2 + s, h, 0:1] = over[s : s + 1, h * chans : (h + 1) * chans]
            cand[2 + s, h, rows + 1 : rows + 2] = under[s : s + 1, h * chans : (h + 1) * chans]
            cand[2 + s, h, 1 : rows + 1] = own[s, h, :rows]
            mirror[s, h, :rows] = across[i * rows : (i + 1) * rows, lanes(h)]
            cand[4 + s, h, 0:1] = before[s * groups + i : s * groups + i + 1, lanes(h)]
            cand[4 + s, h, rows + 1 : rows + 2] = after[s * groups + i : s * groups + i + 1, lanes(h)]
            cand[4 + s, h, 1 : rows + 1] = turned[i * rows : (i + 1) * rows, lanes(h)]
    at_edge = (stripe == 0) | (stripe == last)

    @pl.when(jnp.logical_not(at_edge))
    def _():
        for q in range(2):
            for h in range(faces):
                i = h // fld.per
                cand[q, h, 0 : fld.span] = heads[q][i * fld.span : (i + 1) * fld.span, lanes(h)]

    @pl.when(at_edge)
    def _():
        q = jnp.where(stripe == 0, 0, 1)
        for h in range(faces):
            pair[0, h] = jnp.where(q == 0, top[h, :, here].astype(F32), below[h].astype(F32)).astype(BF)
            pair[1, h] = jnp.where(q == 0, above[h].astype(F32), bot[h, :, here].astype(F32)).astype(BF)
        place = stripe * rows - 1 + prow
        inside = (place >= 0) & (place < side)
        windows = []
        for s in range(2):
            for h in range(faces):
                want = jnp.where(tab[4 * h + s, 1] == 1, side - 1 - place, place)
                window = ((pcol == want) & inside).astype(F32).astype(BF)
                windows.append(mm_nt(window, pair[s, h]))
        pieces = []
        for g in range(faces):
            p = tab[4 * g + q, 0]
            pieces.append(mirror[jnp.maximum((p & 3) - 2, 0), p >> 2][:rows])
        for s in range(2):
            for h in range(faces):
                cand[s, h] = windows[s * faces + h]
        for i in range(groups):
            merged = jnp.concatenate(pieces[i * fld.per : (i + 1) * fld.per], axis=1)
            got[last - stripe, i * fld.span + 1 : i * fld.span + 1 + rows, :] = merged
        for i in range(groups):
            lined = jnp.concatenate(
                [got[d, i * fld.span + 1 : i * fld.span + 1 + rows, :] for d in range(tiles)], axis=0
            )
            lined = jnp.transpose(lined)
            for j in range(fld.per):
                g = i * fld.per + j
                p = tab[4 * g + q, 0]
                kind, h = p & 3, p >> 2
                near = pair[jnp.minimum(kind, 1), h].astype(F32)
                far = lined[j * chans : (j + 1) * chans]
                cells = jnp.where(kind < 2, near, far).astype(BF)
                placed = mm(cells, flip_matrix(side, tab[4 * g + q, 1])).astype(BF)

                @pl.when(q == 0)
                def _():
                    above[g] = placed

                @pl.when(q == 1)
                def _():
                    below[g] = placed

    slot = iota((GROUP, chans), 0)
    live = (slot < fld.span) & jnp.logical_not(
        ((slot == 0) & (stripe == 0)) | ((slot == rows + 1) & (stripe == last))
    )
    for s in range(2):
        taken = []
        for g in range(faces):
            p = tab[4 * g + 2 + s, 0]
            kind, h = p & 3, p >> 2
            which = jnp.where((kind >= 2) & (tab[4 * g + 2 + s, 1] == 1), kind + 2, kind)
            taken.append(jnp.where(live, cand[which, h], 0.0))
        taken.append(jnp.zeros(((GROUP - faces) * GROUP, chans), F32))
        cols[s] = jnp.concatenate(taken, axis=0)


def column_terms(side_weight, cols, out_ch):
    terms = []
    for s in range(2):
        part = mm_nt(side_weight[s], cols[s])
        size = part.shape[1]
        terms.append(
            part[out_ch : 2 * out_ch]
            + pltpu.roll(part[:out_ch], 1, 1)
            + pltpu.roll(part[2 * out_ch :], size - 1, 1)
        )
    return terms


def face_terms(terms, face_index):
    size = terms[0].shape[1]
    shift = lax.rem(2 * size - GROUP * face_index - 1, size)
    return [pltpu.roll(term, shift, 1)[:, :LANES] for term in terms]


def conv_row(weight, stacked, terms, r, out_ch):
    z = mm(weight, stacked)
    side = z.shape[1]
    left, right = pltpu.roll(z[:out_ch], 1, 1), pltpu.roll(z[2 * out_ch :], side - 1, 1)
    lane = iota((out_ch, LANES), 1)
    first = terms[0] if r == 0 else pltpu.roll(terms[0], LANES - r, 1)
    final = pltpu.roll(terms[1], LANES - 1 - r, 1)
    head = jnp.where(lane == 0, first, left[:, :LANES])
    tail = jnp.where(lane == LANES - 1, final, right[:, side - LANES :])
    if side > LANES:
        left = jnp.concatenate([head, left[:, LANES:]], axis=1)
        right = jnp.concatenate([right[:, : side - LANES], tail], axis=1)
    else:
        left, right = head, tail
    return smooth(z[out_ch : 2 * out_ch] + left + right).astype(BF)


def row_stack(x, above, below, f, rows):
    lines = [above[f]] + [x[0, r] for r in range(rows)] + [below[f]]
    return lambda r: lines[r : r + 3]


def prep_kernel(fld, stripe_ref, tab, atmos, perm, x_out, top, bot, ec_out, send_out, *sends):
    stripe, f = stripe_ref[0], pl.program_id(0)

    @pl.when(f == 0)
    def _():
        sends[3][...] = column_picker(fld)

    block = atmos[...].astype(F32).reshape(fld.chans * fld.rows, fld.side).astype(BF)
    moved = mm(perm[...], block).astype(BF)
    lines = [moved[r * fld.chans : (r + 1) * fld.chans] for r in range(fld.rows)]
    for r in range(fld.rows):
        x_out[0, r] = lines[r]
    top[f] = lines[0]
    bot[f] = lines[-1]
    keep_columns(sends[3][...], lines, f, sends[0])

    @pl.when(f == fld.faces - 1)
    def _():
        pack_sends(fld, stripe, tab, top, bot, 0, ec_out, send_out, *sends)


def level_kernel(fld, out_fld, low, off, stripe_ref, tab, x, old_top, old_bot, up, dn, ec, recv, weight, side_weight, *refs):
    stripe, f = stripe_ref[0], pl.program_id(0)
    if low is None:
        outs, sends, halos = refs[:5], refs[5:9], refs[9:]
        x_out, top, bot, ec_out, send_out = outs
    else:
        pool, outs, sends, low_sends, halos = refs[0], refs[1:9], refs[9:13], refs[13:17], refs[17:]
        x_out, y_out, top, bot, ec_out, send_out, low_ec, low_send = outs
    *halos, ends_ref = halos
    _, cols, above, below = halos[:4]
    side = fld.side

    @pl.when(f == 0)
    def _():
        gather_halos(fld, stripe, tab, old_top, old_bot, up, dn, off, ec, recv, *halos)
        terms = column_terms(side_weight, [cols[0].astype(BF), cols[1].astype(BF)], out_fld.chans)
        ends_ref[0], ends_ref[1] = terms
        sends[3][...] = column_picker(out_fld)
        if low is not None:
            low_sends[3][...] = column_picker(low)

    lines = row_stack(x, above, below, f, fld.rows)
    ends = face_terms([ends_ref[0], ends_ref[1]], f)
    made, pooled = [], []
    for r in range(fld.rows):
        cells = conv_row(weight[...], jnp.concatenate(lines(r), axis=0), ends, r, out_fld.chans)
        x_out[0, r] = cells
        made.append(cells)
        if low is not None and r % 2 == 1:
            mean = (mm(made[r - 1], pool[...]) + mm(cells, pool[...])).astype(BF)
            y_out[0, r // 2] = mean
            pooled.append(mean)
    top[f, :, :side] = made[0]
    bot[f, :, :side] = made[-1]
    keep_columns(sends[3][...], made, f, sends[0])
    if low is not None:
        top[f, :, side:] = pooled[0]
        bot[f, :, side:] = pooled[-1]
        keep_columns(low_sends[3][...], pooled, f, low_sends[0])

    @pl.when(f == fld.faces - 1)
    def _():
        if low is not None:
            pack_sends(low, stripe, tab, top, bot, side, low_ec, low_send, *low_sends)
        pack_sends(out_fld, stripe, tab, top, bot, 0, ec_out, send_out, *sends)


def decode_kernel(fld, low, out_ch, vars_out, stripe_ref, tab, x, top, bot, up, dn, ec, recv, y, low_top, low_bot, yup, ydn, yec, yrecv, weight, side_weight, spread, head, atmos, land, row_key, col_key, pred_out, flux_out, *refs):
    halos, low_halos, flux, ends_ref = refs[:7], refs[7:14], refs[14], refs[15]
    stripe, f = stripe_ref[0], pl.program_id(0)
    _, cols, above, below = halos[:4]
    _, low_cols, low_above, low_below = low_halos[:4]

    @pl.when(f == 0)
    def _():
        gather_halos(low, stripe, tab, low_top, low_bot, yup, ydn, 0, yec, yrecv, *low_halos)
        gather_halos(fld, stripe, tab, top, bot, up, dn, 0, ec, recv, *halos)
        size = GROUP * GROUP
        row, col = iota((size, size), 0), iota((size, size), 1)
        widen = (col == (row // GROUP) * GROUP + (row % GROUP + 1) // 2).astype(F32).astype(BF)
        joined = []
        for s in range(2):
            wide = mm(widen, low_cols[s].astype(BF))
            joined.append(jnp.concatenate([cols[s], wide], axis=1).astype(BF))
        ends_ref[0], ends_ref[1] = column_terms(side_weight, joined, out_ch)

    lines = row_stack(x, above, below, f, fld.rows)
    ends = face_terms([ends_ref[0], ends_ref[1]], f)
    low_lines = [low_above[f]] + [y[0, r] for r in range(low.rows)] + [low_below[f]]
    wide = [mm(cells, spread[...]).astype(BF) for cells in low_lines]
    made = []
    for r in range(fld.rows):
        picked = [wide[(r + a + 1) // 2] for a in range(3)]
        made.append(
            conv_row(weight[...], jnp.concatenate(lines(r) + picked, axis=0), ends, r, out_ch)
        )
    result = mm(head[...], jnp.concatenate(made, axis=0)).reshape(-1, fld.rows, fld.side)
    pred_out[:, 0] = (atmos[:, 0].astype(F32) + result[:vars_out]).astype(BF)
    flux[:, f] = jnp.where((land[0] == 1)[None], result[vars_out:], 0.0)

    @pl.when(f == fld.faces - 1)
    def _():
        chosen = (row_key[...] == col_key[...]).astype(F32).astype(BF)
        tiles = flux[...].reshape(-1, fld.side).astype(BF)
        flux_out[...] = mm(chosen, tiles).astype(BF).reshape(flux_out.shape)


def ocean_kernel(cap, recv, state, into, out_weight, sea_out, back_out):
    tiles, _, side = recv.shape

    def one_source(t, carry):
        flux = recv[t].astype(F32)
        pad = (-flux.shape[0]) % 16
        flux = jnp.concatenate([flux, jnp.zeros((pad, side), F32)], axis=0).astype(BF)
        held = state[t]
        high = held.astype(BF)
        low = (held - high.astype(F32)).astype(BF)
        hidden = smooth(mm(into[...], jnp.concatenate([flux, flux, high, high, low], axis=0)))
        width = out_weight[...]
        wide = jnp.concatenate([width] * (side // LANES), axis=1)
        drift = (hidden * wide).reshape(cap, -1, side).sum(axis=1)
        drift = jnp.concatenate([drift, jnp.zeros((8 - cap, side), F32)], axis=0)
        sea = held[:8] + drift
        sea_out[t] = sea
        back_out[t] = sea.astype(BF)
        return carry

    lax.fori_loop(0, tiles, one_source, 0)


def surface_kernel(back, key, land, pred, out):
    faces, rows, side = land.shape
    slots = back[...].astype(F32).reshape(-1, side).astype(BF)
    chosen = (key[...] == iota((faces * rows, slots.shape[0]), 1)).astype(F32).astype(BF)
    sea = mm(chosen, slots).reshape(faces, rows, side)
    out[0] = jnp.where(land[...] == 1, sea, pred[0].astype(F32)).astype(BF)


def call(kernel, outs, ins, scratch, flops, smem=0, steps=1, specs=None, aliases=None, out_specs=None, name=None):
    whole = pl.BlockSpec(memory_space=pltpu.VMEM)
    in_specs = [pl.BlockSpec(memory_space=pltpu.SMEM)] * smem + [whole] * (len(ins) - smem)
    for position, spec in (specs or {}).items():
        in_specs[position] = spec
    grid = {"grid": (steps,)} if specs else {}
    moved = sum(int(np.prod(a.shape)) * a.dtype.itemsize for a in list(ins) + list(outs))
    return pl.pallas_call(
        kernel,
        out_shape=outs,
        **grid,
        in_specs=in_specs,
        out_specs=[(out_specs or {}).get(n, whole) for n in range(len(outs))],
        scratch_shapes=scratch,
        input_output_aliases=aliases or {},
        compiler_params=pltpu.CompilerParams(vmem_limit_bytes=56 * 1024 * 1024),
        cost_estimate=pl.CostEstimate(flops=int(flops), bytes_accessed=int(moved), transcendentals=0),
        name=name,
    )(*ins)


def swap_rows(top, bot):
    tiles = lax.axis_size("tile")
    ring = [(i, (i + 1) % tiles) for i in range(tiles)]
    up = lax.ppermute(bot, "tile", ring)
    return up, lax.ppermute(top, "tile", [(j, i) for i, j in ring])


def swap_chunks(chunks):
    return lax.all_to_all(chunks, "tile", split_axis=0, concat_axis=0, tiled=True)


def packed_weight(weight, chans):
    taps, out_ch, _ = weight.shape
    split = weight.reshape(taps, out_ch, taps, chans)
    body = jnp.transpose(split, (2, 1, 0, 3)).reshape(taps * out_ch, taps * chans)
    sides = jnp.stack([split[:, :, 0], split[:, :, 2]]).reshape(2, taps * out_ch, chans)
    return body, sides


def on_one_group(
    atmos_state,
    land_sea,
    owners,
    seam_table,
    ocean_state,
    conv_input,
    conv_encode,
    conv_coarse,
    conv_decode,
    output_head,
    ocean_in,
    ocean_out,
):
    in_ch, faces, rows, side = atmos_state.shape
    tiles = lax.axis_size("tile")
    width = conv_input.shape[1]
    stripe = lax.axis_index("tile").astype(jnp.int32).reshape(1)
    entry = Field(faces, rows, in_ch, side, tiles)
    full = Field(faces, rows, width, side, tiles)
    low = Field(faces, rows // 2, width, side // 2, tiles)
    cells = faces * rows * side

    order = np.arange(in_ch * rows)
    perm = np.zeros((in_ch * rows, in_ch * rows), np.float32)
    perm[order, (order % in_ch) * rows + order // in_ch] = 1.0
    spread = np.zeros((side // 2, side), np.float32)
    spread[np.arange(side) // 2, np.arange(side)] = 1.0
    perm, pool = jnp.asarray(perm, BF), jnp.asarray(0.25 * spread.T, BF)
    spread = jnp.asarray(spread, BF)

    def one(shape, dim=0):
        block = tuple(1 if n == dim else size for n, size in enumerate(shape))
        return pl.BlockSpec(block, lambda i: tuple(i if n == dim else 0 for n in range(len(shape))))

    ends = [pltpu.VMEM((2, width, GROUP * GROUP), F32)]
    x0, top, bot, ec, send = call(
        functools.partial(prep_kernel, entry),
        [entry.main()] + entry.edges() + entry.sends(),
        (stripe, seam_table, atmos_state, perm),
        entry.send_scratch(),
        2 * cells * in_ch * in_ch * rows,
        smem=2,
        steps=faces,
        specs={2: one(atmos_state.shape, 1)},
        out_specs={0: one(entry.main().shape)},
        name="prep",
    )
    got = swap_chunks(send)
    up, dn = swap_rows(top, bot)
    x1, top, bot, ec, send = call(
        functools.partial(level_kernel, entry, full, None, 0),
        [full.main()] + full.edges() + full.sends(),
        (stripe, seam_table, x0, top, bot, up, dn, ec, got) + packed_weight(conv_input, in_ch),
        full.send_scratch() + entry.halo_scratch() + ends,
        2 * cells * 9 * in_ch * width,
        smem=2,
        steps=faces,
        specs={2: one(x0.shape)},
        out_specs={0: one(full.main().shape)},
        name="conv_in",
    )
    got = swap_chunks(send)
    up, dn = swap_rows(top, bot)
    x2, y0, top, bot, ec, send, low_ec, low_send = call(
        functools.partial(level_kernel, full, full, low, 0),
        [full.main(), low.main()] + full.edges(side // 2) + full.sends() + low.sends(),
        (stripe, seam_table, x1, top, bot, up, dn, ec, got) + packed_weight(conv_encode, width) + (pool,),
        full.send_scratch() + low.send_scratch() + full.halo_scratch() + ends,
        2 * cells * 9 * width * width,
        smem=2,
        steps=faces,
        specs={2: one(x1.shape)},
        out_specs={0: one(full.main().shape), 1: one(low.main().shape)},
        name="encode",
    )
    low_got = swap_chunks(low_send)
    up, dn = swap_rows(top, bot)
    y1, low_top, low_bot, low_ec, low_send = call(
        functools.partial(level_kernel, low, low, None, side),
        [low.main()] + low.edges() + low.sends(),
        (stripe, seam_table, y0, top, bot, up, dn, low_ec, low_got) + packed_weight(conv_coarse, width),
        low.send_scratch() + low.halo_scratch() + ends,
        10e9,
        smem=2,
        steps=faces,
        specs={2: one(y0.shape)},
        out_specs={0: one(low.main().shape)},
        name="coarse",
    )
    low_send, got = lax.optimization_barrier((low_send, swap_chunks(send)))
    low_got = swap_chunks(low_send)
    low_up, low_dn = swap_rows(low_top, low_bot)

    taps = conv_decode.shape[0]
    split = conv_decode.reshape(taps, width, taps, 2, width)
    body = jnp.transpose(split, (2, 1, 3, 0, 4)).reshape(taps * width, 2 * taps * width)
    sides = jnp.stack([split[:, :, 0], split[:, :, 2]]).reshape(2, taps * width, 2 * width)
    heads = output_head.shape[0]
    flux_ch = heads - OUT_VARS
    eye = jnp.eye(rows, dtype=output_head.dtype)
    head = (output_head[:, None, None, :] * eye[None, :, :, None]).reshape(heads * rows, rows * width)

    slot_count = ocean_state.shape[2]
    cap = slot_count // tiles
    owner_ids = owners[:, 0]
    count = owner_ids.shape[0]
    earlier = np.tril(np.ones((count, count), bool), -1)
    rank = jnp.sum((owner_ids[:, None] == owner_ids[None, :]) & earlier, axis=1).astype(jnp.int32)
    slot_index = owner_ids * cap + rank
    col_key = (np.arange(flux_ch, dtype=np.int32)[:, None] * slot_count + slot_index[None, :]).reshape(1, -1)
    row_key = (
        np.arange(flux_ch, dtype=np.int32)[None, :, None] * slot_count
        + np.arange(slot_count, dtype=np.int32).reshape(tiles, 1, cap)
    ).reshape(-1, 1)
    row_key = jnp.asarray(row_key)
    pred, outgoing = call(
        functools.partial(decode_kernel, full, low, width, OUT_VARS),
        [
            jax.ShapeDtypeStruct((OUT_VARS, faces, rows, side), BF),
            jax.ShapeDtypeStruct((tiles, flux_ch * cap, side), BF),
        ],
        (stripe, seam_table, x2, top, bot, up, dn, ec, got)
        + (y1, low_top, low_bot, low_up, low_dn, low_ec, low_got)
        + (body, sides, spread, head, atmos_state, land_sea, row_key, col_key),
        full.halo_scratch()
        + low.halo_scratch()
        + [pltpu.VMEM((flux_ch, faces, rows, side), F32)]
        + ends,
        2 * cells * 18 * width * width,
        smem=2,
        steps=faces,
        specs={
            2: one(x2.shape),
            9: one(y1.shape),
            20: pl.BlockSpec((OUT_VARS, 1, rows, side), lambda i: (0, i, 0, 0)),
            21: one(land_sea.shape),
        },
        out_specs={0: one((OUT_VARS, faces, rows, side), 1)},
        name="decode",
    )
    arrived = lax.all_to_all(outgoing, "tile", split_axis=0, concat_axis=0, tiled=True)

    held = jnp.transpose(ocean_state[0, 0].reshape(tiles, cap, OCEAN_CH, side), (0, 2, 1, 3))
    state = jnp.pad(held, ((0, 0), (0, 0), (0, 8 - cap), (0, 0))).reshape(tiles, OCEAN_CH * 8, side)
    hidden = ocean_in.shape[0]
    high = ocean_in.astype(BF)
    rest = (ocean_in - high.astype(F32)).astype(BF)
    flux_pad = (-flux_ch * cap) % 16
    each = jnp.eye(cap, dtype=BF)
    slot8 = jnp.eye(cap, 8, dtype=BF)

    def flux_part(weights):
        part = each[:, None, None, :] * weights[None, :, OCEAN_CH:, None]
        return jnp.pad(part.reshape(cap * hidden, flux_ch * cap), ((0, 0), (0, flux_pad)))

    def state_part(weights):
        part = slot8[:, None, None, :] * weights[None, :, :OCEAN_CH, None]
        return part.reshape(cap * hidden, OCEAN_CH * 8)

    into = jnp.concatenate(
        [flux_part(high), flux_part(rest), state_part(high), state_part(rest), state_part(high)], axis=1
    )
    out_weight = jnp.broadcast_to(ocean_out[None, :, None], (cap, hidden, LANES)).reshape(-1, LANES)
    sea, back = call(
        functools.partial(ocean_kernel, cap),
        [jax.ShapeDtypeStruct((tiles, 8, side), F32), jax.ShapeDtypeStruct((tiles, 8, side), BF)],
        (arrived, state, into, out_weight),
        [],
        2 * slot_count * side * hidden * 8,
        name="ocean",
    )
    returned = lax.all_to_all(back, "tile", split_axis=0, concat_axis=0, tiled=True)
    key = (owner_ids * 8 + rank)[:, None]
    first = pl.BlockSpec((1, faces, rows, side), lambda i: (0, 0, 0, 0))
    (atmos_next,) = call(
        surface_kernel,
        [jax.ShapeDtypeStruct(pred.shape, BF)],
        (returned, key, land_sea, pred),
        [],
        2 * count * tiles * 8 * side,
        specs={3: first},
        out_specs={0: first},
        aliases={3: 0},
        name="surface",
    )
    renewed = jnp.stack([sea[:, :cap], held[:, 0]], axis=2)
    return atmos_next, renewed.reshape(1, 1, slot_count, OCEAN_CH, side)


def fits(mesh):
    return mesh.shape["face"] == 1


def solution(mesh):
    in_specs = (
        P(None, "face", "tile", None),
        P("face", "tile", None),
        P(("face", "tile"), None),
        P(),
        P("face", "tile", None, None, None),
        P(),
        P(),
        P(),
        P(),
        P(),
        P(),
        P(),
    )
    out_specs = (P(None, "face", "tile", None), P("face", "tile", None, None, None))
    return jax.shard_map(
        on_one_group if fits(mesh) else on_device,
        mesh=mesh,
        in_specs=in_specs,
        out_specs=out_specs,
        check_vma=False,
    )
```

```python
import functools

import jax
import jax.numpy as jnp
import numpy as np
from jax import lax
from jax.experimental import pallas as pl
from jax.experimental.pallas import tpu as pltpu
from jax.sharding import PartitionSpec as P

OUT_VARS = 8
FLUX_CH = 4
OCEAN_CH = 2


def extended(shard, sides, width):
    for axis, dim in sides:
        size, length = (lax.axis_size(axis), shard.shape[dim])
        up = [(i, (i + 1) % size) for i in range(size)]
        down = [(j, i) for i, j in up]
        last = lax.slice_in_dim(shard, length - width, length, axis=dim)
        initial = lax.slice_in_dim(shard, 0, width, axis=dim)
        before = lax.ppermute(last, axis, up)
        after = lax.ppermute(initial, axis, down)
        shard = jnp.concatenate([before, shard, after], axis=dim)
    return shard


def pad_field(values, seam_table):
    channels, faces_dev, stripe_rows, face_side = values.shape
    tile_count = lax.axis_size("tile")
    stripe = lax.axis_index("tile")
    face_group = lax.axis_index("face")
    rimmed = extended(values, (("tile", 2),), 1)
    edge_rows = jnp.stack([values[:, :, 0, :], rimmed[:, :, 0, :]], axis=2)
    edge_pieces = edge_rows.reshape(channels, faces_dev, 2, tile_count, stripe_rows)
    received = lax.all_to_all(edge_pieces, "tile", split_axis=3, concat_axis=3, tiled=True)
    row_part = received[:, :, :, 0, :]
    row_start = stripe * stripe_rows
    col_part = jnp.stack([values[:, :, :, 0], values[:, :, :, face_side - 1]], axis=2)
    seam_piece = jnp.concatenate([row_part, col_part], axis=2)
    seam_piece = jnp.transpose(seam_piece, (1, 2, 0, 3)).reshape(
        1, faces_dev, 4, channels * stripe_rows
    )
    own_sides = lax.dynamic_slice_in_dim(seam_table, face_group * (faces_dev * 4), faces_dev * 4, 0)
    gathered = lax.all_gather(seam_piece, ("face", "tile"), axis=0, tiled=True)
    group_count = gathered.shape[0] // tile_count
    strip_table = gathered.reshape(group_count, tile_count, faces_dev, 4, channels, stripe_rows)
    strip_table = jnp.transpose(strip_table, (0, 2, 3, 4, 1, 5)).reshape(
        group_count * faces_dev * 4, channels, face_side
    )
    strips = jnp.take(strip_table, own_sides[:, 0], axis=0)
    strips = jnp.where(own_sides[:, 1][:, None, None] == 1, strips[:, :, ::-1], strips)
    strips = jnp.transpose(strips.reshape(faces_dev, 4, channels, face_side), (2, 0, 1, 3))
    upper_row = jnp.where(stripe == 0, strips[:, :, 0, :], rimmed[:, :, 0, :])
    bottom = jnp.where(
        stripe == tile_count - 1, strips[:, :, 1, :], rimmed[:, :, stripe_rows + 1, :]
    )
    middle = jnp.concatenate([upper_row[:, :, None, :], values, bottom[:, :, None, :]], axis=2)
    zero_cells = jnp.zeros((channels, faces_dev, 2, 1), values.dtype)
    columns = jnp.concatenate([zero_cells, strips[:, :, 2:, :], zero_cells], axis=3)
    columns = lax.dynamic_slice_in_dim(columns, row_start, stripe_rows + 2, 3)
    return jnp.concatenate([columns[:, :, 0, :, None], middle, columns[:, :, 1, :, None]], axis=3)


def convolve(padded, weight):
    channels, faces_dev, rows_two, side_two = padded.shape
    stripe_rows = rows_two - 2
    face_side = side_two - 2
    planes = []
    for face_index in range(faces_dev):
        summed = jnp.zeros((weight.shape[1], stripe_rows * face_side), jnp.float32)
        for row_shift in range(3):
            tap_rows = jnp.concatenate(
                [
                    padded[
                        :,
                        face_index,
                        row_shift : row_shift + stripe_rows,
                        col_shift : col_shift + face_side,
                    ]
                    for col_shift in range(3)
                ],
                axis=0,
            )
            summed = summed + jnp.dot(
                weight[row_shift],
                tap_rows.reshape(3 * channels, stripe_rows * face_side),
                preferred_element_type=jnp.float32,
            )
        planes.append(jax.nn.gelu(summed).astype(jnp.bfloat16).reshape(-1, stripe_rows, face_side))
    return jnp.stack(planes, axis=1)


def upsample(values):
    return jnp.repeat(jnp.repeat(values, 2, axis=2), 2, axis=3)


def ocean_update(held_state, arrived_flux, ocean_in, ocean_out):
    stacked = jnp.concatenate([held_state, arrived_flux.astype(jnp.float32)], axis=1)
    hidden = jax.nn.gelu(
        jnp.einsum("hc,ncs->nhs", ocean_in, stacked, precision=lax.Precision.HIGHEST)
    )
    sea_now = held_state[:, 0] + jnp.einsum(
        "h,nhs->ns", ocean_out, hidden, precision=lax.Precision.HIGHEST
    )
    return jnp.stack([sea_now, held_state[:, 0]], axis=1)


def ocean_blocks(held_state, arrived_flux, ocean_in, ocean_out, block_count):
    slot_count, state_ch, face_side = held_state.shape
    capacity = slot_count // block_count
    held_split = held_state.reshape(block_count, capacity, state_ch, face_side)
    flux_split = arrived_flux.reshape(block_count, capacity, arrived_flux.shape[1], face_side)
    stepped = lax.map(
        lambda pair: ocean_update(pair[0], pair[1], ocean_in, ocean_out), (held_split, flux_split)
    )
    return stepped.reshape(slot_count, state_ch, face_side)


def on_device(
    atmos_state,
    land_sea,
    owners,
    seam_table,
    ocean_state,
    conv_input,
    conv_encode,
    conv_coarse,
    conv_decode,
    output_head,
    ocean_in,
    ocean_out,
):
    encoded = convolve(pad_field(atmos_state, seam_table), conv_input)
    skip_level = convolve(pad_field(encoded, seam_table), conv_encode)
    channels, faces_dev, stripe_rows, face_side = skip_level.shape
    pooled = (
        skip_level.astype(jnp.float32)
        .reshape(channels, faces_dev, stripe_rows // 2, 2, face_side // 2, 2)
        .mean(axis=(3, 5))
        .astype(jnp.bfloat16)
    )
    coarse_out = convolve(pad_field(pooled, seam_table), conv_coarse)
    coarse_pad = upsample(pad_field(coarse_out, seam_table))[
        :, :, 1 : stripe_rows + 3, 1 : face_side + 3
    ]
    padded = jnp.concatenate([pad_field(skip_level, seam_table), coarse_pad], axis=0)
    decoded = convolve(padded, conv_decode)
    head_out = jnp.dot(
        output_head, decoded.reshape(channels, -1), preferred_element_type=jnp.float32
    )
    head_out = head_out.reshape(-1, faces_dev, stripe_rows, face_side)
    predicted = atmos_state[:OUT_VARS].astype(jnp.float32) + head_out[:OUT_VARS]
    is_ocean = land_sea == 1
    fluxes = jnp.where(is_ocean[None], head_out[OUT_VARS:], 0.0).astype(jnp.bfloat16)
    flux_tiles = jnp.transpose(fluxes, (1, 2, 0, 3)).reshape(
        faces_dev * stripe_rows, FLUX_CH * face_side
    )
    tile_count = lax.axis_size("tile")
    owner_ids = owners[:, 0]
    owner_hits = (owner_ids[:, None] == jnp.arange(tile_count)[None, :]).astype(jnp.int32)
    slot_rank = jnp.sum((jnp.cumsum(owner_hits, axis=0) - 1) * owner_hits, axis=1)
    slot_count = ocean_state.shape[2]
    capacity = slot_count // tile_count
    slot_index = owner_ids * capacity + slot_rank
    selector = (jnp.arange(slot_count)[:, None] == slot_index[None, :]).astype(jnp.bfloat16)
    outgoing = jnp.dot(selector, flux_tiles, preferred_element_type=jnp.float32).astype(
        jnp.bfloat16
    )
    outgoing = outgoing.reshape(tile_count, capacity, FLUX_CH, face_side)
    held_state = ocean_state[0, 0]
    arrived = lax.all_to_all(outgoing, "tile", split_axis=0, concat_axis=0, tiled=True)
    renewed = ocean_blocks(
        held_state, arrived.reshape(slot_count, FLUX_CH, face_side), ocean_in, ocean_out, tile_count
    )
    sea_back = renewed[:, 0].astype(jnp.bfloat16).reshape(tile_count, capacity, face_side)
    sea_slots = lax.all_to_all(sea_back, "tile", split_axis=0, concat_axis=0, tiled=True)
    sea_tiles = jnp.dot(
        selector.T, sea_slots.reshape(slot_count, face_side), preferred_element_type=jnp.float32
    )
    sea_temp = sea_tiles.reshape(faces_dev, stripe_rows, face_side)
    surface = jnp.where(is_ocean, sea_temp, predicted[0])
    atmos_next = jnp.concatenate([surface[None], predicted[1:]], axis=0).astype(jnp.bfloat16)
    return (atmos_next, renewed.reshape(1, 1, slot_count, OCEAN_CH, face_side))


GROUP = 16
LANES = 128
VMEM = pltpu.VMEM
BF = jnp.bfloat16
F32 = jnp.float32
NT = (((1,), (1,)), ((), ()))


def mm(a, b):
    return jnp.dot(a, b, preferred_element_type=F32)


def mm_nt(a, b):
    return lax.dot_general(a, b, NT, preferred_element_type=F32)


def iota(shape, dim):
    return lax.broadcasted_iota(jnp.int32, shape, dim)


def smooth(x):
    inner = x * (0.7978845608028654 + 0.03567740813636141 * (x * x))
    half = 0.5 * x
    return half * jnp.tanh(inner) + half


class Field:
    def __init__(self, faces, rows, chans, side, tiles):
        self.faces, self.rows, self.chans, self.side, self.tiles = faces, rows, chans, side, tiles
        self.per = LANES // chans
        self.groups = faces // self.per
        self.span = rows + 2
        self.extra = self.groups * self.span
        used = max(self.extra + 2 * self.groups, 2 * self.groups * rows)
        self.chunk = used + (-used) % 16

    def main(self):
        return jax.ShapeDtypeStruct((self.faces, self.rows, self.chans, self.side), BF)

    def edges(self, more=0):
        edge = jax.ShapeDtypeStruct((self.faces, self.chans, self.side + more), BF)
        return [edge, edge]

    def sends(self):
        return [
            jax.ShapeDtypeStruct((2 * self.faces * 8, self.chans), BF),
            jax.ShapeDtypeStruct((self.tiles, self.chunk, LANES), BF),
        ]

    def send_scratch(self):
        return [
            pltpu.VMEM((2, self.faces, 8, self.chans), F32),
            pltpu.VMEM((self.tiles, self.chunk, LANES), F32),
            pltpu.VMEM((self.side + 8, LANES), F32),
            pltpu.VMEM((16, self.rows * self.side), BF),
        ]

    def halo_scratch(self):
        return [
            pltpu.VMEM((6, self.faces, GROUP, self.chans), F32),
            pltpu.VMEM((2, GROUP * GROUP, self.chans), F32),
            pltpu.VMEM((self.faces, self.chans, self.side), BF),
            pltpu.VMEM((self.faces, self.chans, self.side), BF),
            pltpu.VMEM((2, self.faces, self.chans, self.side), BF),
            pltpu.VMEM((self.tiles, self.chunk, LANES), F32),
            pltpu.VMEM((2, self.faces, 8, self.chans), F32),
        ]


def flip_matrix(size, flag):
    row, col = iota((size, size), 0), iota((size, size), 1)
    return (row == jnp.where(flag == 1, size - 1 - col, col)).astype(F32).astype(BF)


def end_picker(side):
    row, col = iota((16, side), 0), iota((16, side), 1)
    return (((row == 0) & (col == 0)) | ((row == 1) & (col == side - 1))).astype(F32).astype(BF)


def column_picker(fld):
    length = fld.rows * fld.side
    row, col = iota((16, length), 0), iota((16, length), 1)
    want = (row & 7) * fld.side + (row >> 3) * (fld.side - 1)
    return (col == want).astype(F32).astype(BF)


def keep_columns(picker, face_rows, f, cols):
    picked = mm_nt(picker, jnp.concatenate(face_rows, axis=1))
    cols[0, f] = picked[:8]
    cols[1, f] = picked[8:]


def pack_sends(fld, stripe, tab, top, bot, off, ec_out, send_out, cols, stage, strip, picker):
    last, rows, chans, groups, per = fld.tiles - 1, fld.rows, fld.chans, fld.groups, fld.per
    held = cols[...]
    ec_out[...] = held.reshape(2 * fld.faces * 8, chans).astype(BF)
    paired = held.reshape(2, groups, per, 8, chans)
    packed = jnp.concatenate([paired[:, :, j] for j in range(per)], axis=3)
    across = packed[:, :, :rows].reshape(2 * groups * rows, LANES)
    initial = packed[:, :, 0].reshape(2 * groups, LANES)
    final = packed[:, :, rows - 1].reshape(2 * groups, LANES)
    pieces = []
    for q in range(2):
        for g in range(fld.faces):
            p = tab[4 * g + q, 0]
            pieces.append(cols[jnp.maximum((p & 3) - 2, 0), p >> 2][:rows])
    merged = [jnp.concatenate(pieces[n : n + per], axis=1) for n in range(0, len(pieces), per)]
    stage[...] = jnp.zeros_like(stage)
    for q in range(2):
        for i in range(groups):
            stage[q * last, i * fld.span + 1 : i * fld.span + 1 + rows, :] = merged[q * groups + i]

    def lanes(h):
        return slice((h % per) * chans, (h % per + 1) * chans)

    @pl.when((stripe == 0) | (stripe == last))
    def _():
        q = jnp.where(stripe == 0, 0, 1)
        for i in range(groups):
            turned = []
            for h in range(i * per, (i + 1) * per):
                upper = top[h, :, off : off + fld.side].astype(F32)
                lower = bot[h, :, off : off + fld.side].astype(F32)
                cells = jnp.where(q == 0, upper, lower).astype(BF)
                turned.append(mm_nt(flip_matrix(fld.side, tab[4 * h + q, 1]), cells))
            strip[0:8] = jnp.zeros((8, LANES), F32)
            strip[fld.side : fld.side + 8] = jnp.zeros((8, LANES), F32)
            strip[1 : fld.side + 1, :] = jnp.concatenate(turned, axis=1)
            for d in range(1, last, 10):
                here = range(d, min(d + 10, last))
                taken = [strip[e * rows : e * rows + fld.span, :] for e in here]
                for e, piece in zip(here, taken):
                    stage[e, i * fld.span : (i + 1) * fld.span, :] = piece

    stage[last - stripe, : 2 * groups * rows, :] = across

    @pl.when(stripe < last)
    def _():
        stage[last - 1 - stripe, fld.extra : fld.extra + 2 * groups, :] = final

    @pl.when(stripe > 0)
    def _():
        stage[last + 1 - stripe, fld.extra : fld.extra + 2 * groups, :] = initial

    send_out[...] = stage[...].astype(BF)


def gather_halos(fld, stripe, tab, top, bot, up, dn, off, ec, recv, cand, cols, above, below, pair, got, mirror):
    faces, rows, chans, side, tiles = fld.faces, fld.rows, fld.chans, fld.side, fld.tiles
    last = tiles - 1
    groups = fld.groups
    got[...] = recv[...].astype(F32)
    own = ec[...].astype(F32).reshape(2, faces, 8, chans)
    row, col = iota((groups * rows, groups * rows), 0), iota((groups * rows, groups * rows), 1)
    turn = ((row // rows == col // rows) & (row % rows + col % rows == rows - 1)).astype(F32).astype(BF)
    prow, pcol = iota((16, side), 0), iota((16, side), 1)

    def lanes(h):
        return slice((h % fld.per) * chans, (h % fld.per + 1) * chans)

    here = slice(off, off + side)
    above[...] = up[:, :, here]
    below[...] = dn[:, :, here]
    over = mm_nt(end_picker(side), above[...].reshape(faces * chans, side))
    under = mm_nt(end_picker(side), below[...].reshape(faces * chans, side))
    heads = [got[q * last, : fld.extra, :] for q in range(2)]
    before = got[jnp.minimum(last + 1 - stripe, last), fld.extra : fld.extra + 2 * groups, :]
    after = got[jnp.maximum(last - 1 - stripe, 0), fld.extra : fld.extra + 2 * groups, :]
    for s in range(2):
        across = got[last - stripe, s * groups * rows : (s + 1) * groups * rows, :]
        turned = mm(turn, across.astype(BF))
        for h in range(faces):
            i = h // fld.per
            cand[2 + s, h, 0:1] = over[s : s + 1, h * chans : (h + 1) * chans]
            cand[2 + s, h, rows + 1 : rows + 2] = under[s : s + 1, h * chans : (h + 1) * chans]
            cand[2 + s, h, 1 : rows + 1] = own[s, h, :rows]
            mirror[s, h, :rows] = across[i * rows : (i + 1) * rows, lanes(h)]
            cand[4 + s, h, 0:1] = before[s * groups + i : s * groups + i + 1, lanes(h)]
            cand[4 + s, h, rows + 1 : rows + 2] = after[s * groups + i : s * groups + i + 1, lanes(h)]
            cand[4 + s, h, 1 : rows + 1] = turned[i * rows : (i + 1) * rows, lanes(h)]
    at_edge = (stripe == 0) | (stripe == last)

    @pl.when(jnp.logical_not(at_edge))
    def _():
        for q in range(2):
            for h in range(faces):
                i = h // fld.per
                cand[q, h, 0 : fld.span] = heads[q][i * fld.span : (i + 1) * fld.span, lanes(h)]

    @pl.when(at_edge)
    def _():
        q = jnp.where(stripe == 0, 0, 1)
        for h in range(faces):
            pair[0, h] = jnp.where(q == 0, top[h, :, here].astype(F32), below[h].astype(F32)).astype(BF)
            pair[1, h] = jnp.where(q == 0, above[h].astype(F32), bot[h, :, here].astype(F32)).astype(BF)
        place = stripe * rows - 1 + prow
        inside = (place >= 0) & (place < side)
        windows = []
        for s in range(2):
            for h in range(faces):
                want = jnp.where(tab[4 * h + s, 1] == 1, side - 1 - place, place)
                window = ((pcol == want) & inside).astype(F32).astype(BF)
                windows.append(mm_nt(window, pair[s, h]))
        pieces = []
        for g in range(faces):
            p = tab[4 * g + q, 0]
            pieces.append(mirror[jnp.maximum((p & 3) - 2, 0), p >> 2][:rows])
        for s in range(2):
            for h in range(faces):
                cand[s, h] = windows[s * faces + h]
        for i in range(groups):
            merged = jnp.concatenate(pieces[i * fld.per : (i + 1) * fld.per], axis=1)
            got[last - stripe, i * fld.span + 1 : i * fld.span + 1 + rows, :] = merged
        for i in range(groups):
            lined = jnp.concatenate(
                [got[d, i * fld.span + 1 : i * fld.span + 1 + rows, :] for d in range(tiles)], axis=0
            )
            lined = jnp.transpose(lined)
            for j in range(fld.per):
                g = i * fld.per + j
                p = tab[4 * g + q, 0]
                kind, h = p & 3, p >> 2
                near = pair[jnp.minimum(kind, 1), h].astype(F32)
                far = lined[j * chans : (j + 1) * chans]
                cells = jnp.where(kind < 2, near, far).astype(BF)
                placed = mm(cells, flip_matrix(side, tab[4 * g + q, 1])).astype(BF)

                @pl.when(q == 0)
                def _():
                    above[g] = placed

                @pl.when(q == 1)
                def _():
                    below[g] = placed

    slot = iota((GROUP, chans), 0)
    live = (slot < fld.span) & jnp.logical_not(
        ((slot == 0) & (stripe == 0)) | ((slot == rows + 1) & (stripe == last))
    )
    for s in range(2):
        taken = []
        for g in range(faces):
            p = tab[4 * g + 2 + s, 0]
            kind, h = p & 3, p >> 2
            which = jnp.where((kind >= 2) & (tab[4 * g + 2 + s, 1] == 1), kind + 2, kind)
            taken.append(jnp.where(live, cand[which, h], 0.0))
        taken.append(jnp.zeros(((GROUP - faces) * GROUP, chans), F32))
        cols[s] = jnp.concatenate(taken, axis=0)


def column_terms(side_weight, cols, out_ch):
    terms = []
    for s in range(2):
        part = mm_nt(side_weight[s], cols[s])
        size = part.shape[1]
        terms.append(
            part[out_ch : 2 * out_ch]
            + pltpu.roll(part[:out_ch], 1, 1)
            + pltpu.roll(part[2 * out_ch :], size - 1, 1)
        )
    return terms


def face_terms(terms, face_index):
    size = terms[0].shape[1]
    shift = lax.rem(2 * size - GROUP * face_index - 1, size)
    return [pltpu.roll(term, shift, 1)[:, :LANES] for term in terms]


def conv_row(weight, stacked, terms, r, out_ch):
    z = mm(weight, stacked)
    side = z.shape[1]
    left, right = pltpu.roll(z[:out_ch], 1, 1), pltpu.roll(z[2 * out_ch :], side - 1, 1)
    lane = iota((out_ch, LANES), 1)
    first = terms[0] if r == 0 else pltpu.roll(terms[0], LANES - r, 1)
    final = pltpu.roll(terms[1], LANES - 1 - r, 1)
    head = jnp.where(lane == 0, first, left[:, :LANES])
    tail = jnp.where(lane == LANES - 1, final, right[:, side - LANES :])
    if side > LANES:
        left = jnp.concatenate([head, left[:, LANES:]], axis=1)
        right = jnp.concatenate([right[:, : side - LANES], tail], axis=1)
    else:
        left, right = head, tail
    return smooth(z[out_ch : 2 * out_ch] + left + right).astype(BF)


def row_stack(x, above, below, k, f, rows):
    lines = [above[f]] + [x[k, r] for r in range(rows)] + [below[f]]
    return lambda r: lines[r : r + 3]


def prep_kernel(fld, stripe_ref, tab, atmos, perm, x_out, top, bot, ec_out, send_out, *sends):
    stripe, step = stripe_ref[0], pl.program_id(0)
    batch = x_out.shape[0]

    @pl.when(step == 0)
    def _():
        sends[3][...] = column_picker(fld)

    def one_face(k, carry):
        f = step * batch + k
        block = atmos[:, k].astype(F32).reshape(fld.chans * fld.rows, fld.side).astype(BF)
        moved = mm(perm[...], block).astype(BF)
        lines = [moved[r * fld.chans : (r + 1) * fld.chans] for r in range(fld.rows)]
        for r in range(fld.rows):
            x_out[k, r] = lines[r]
        top[f] = lines[0]
        bot[f] = lines[-1]
        keep_columns(sends[3][...], lines, f, sends[0])
        return carry

    lax.fori_loop(0, batch, one_face, 0)

    @pl.when(step == fld.faces // batch - 1)
    def _():
        pack_sends(fld, stripe, tab, top, bot, 0, ec_out, send_out, *sends)


def level_kernel(fld, out_fld, low, off, stripe_ref, tab, x, old_top, old_bot, up, dn, ec, recv, weight, side_weight, *refs):
    stripe, step = stripe_ref[0], pl.program_id(0)
    if low is None:
        outs, sends, halos = refs[:5], refs[5:9], refs[9:]
        x_out, top, bot, ec_out, send_out = outs
    else:
        pool, outs, sends, low_sends, halos = refs[0], refs[1:9], refs[9:13], refs[13:17], refs[17:]
        x_out, y_out, top, bot, ec_out, send_out, low_ec, low_send = outs
    *halos, ends_ref = halos
    batch = x_out.shape[0]
    _, cols, above, below = halos[:4]
    side = fld.side

    @pl.when(step == 0)
    def _():
        gather_halos(fld, stripe, tab, old_top, old_bot, up, dn, off, ec, recv, *halos)
        terms = column_terms(side_weight, [cols[0].astype(BF), cols[1].astype(BF)], out_fld.chans)
        ends_ref[0], ends_ref[1] = terms
        sends[3][...] = column_picker(out_fld)
        if low is not None:
            low_sends[3][...] = column_picker(low)

    def one_face(k, carry):
        f = step * batch + k
        lines = row_stack(x, above, below, k, f, fld.rows)
        ends = face_terms([ends_ref[0], ends_ref[1]], f)
        made, pooled = [], []
        for r in range(fld.rows):
            cells = conv_row(weight[...], jnp.concatenate(lines(r), axis=0), ends, r, out_fld.chans)
            x_out[k, r] = cells
            made.append(cells)
            if low is not None and r % 2 == 1:
                mean = (mm(made[r - 1], pool[...]) + mm(cells, pool[...])).astype(BF)
                y_out[k, r // 2] = mean
                pooled.append(mean)
        top[f, :, :side] = made[0]
        bot[f, :, :side] = made[-1]
        keep_columns(sends[3][...], made, f, sends[0])
        if low is not None:
            top[f, :, side:] = pooled[0]
            bot[f, :, side:] = pooled[-1]
            keep_columns(low_sends[3][...], pooled, f, low_sends[0])
        return carry

    lax.fori_loop(0, batch, one_face, 0)

    @pl.when(step == fld.faces // batch - 1)
    def _():
        if low is not None:
            pack_sends(low, stripe, tab, top, bot, side, low_ec, low_send, *low_sends)
        pack_sends(out_fld, stripe, tab, top, bot, 0, ec_out, send_out, *sends)


def decode_kernel(fld, low, out_ch, vars_out, stripe_ref, tab, x, top, bot, up, dn, ec, recv, y, low_top, low_bot, yup, ydn, yec, yrecv, weight, side_weight, spread, head, atmos, land, row_key, col_key, pred_out, flux_out, *refs):
    halos, low_halos, flux, ends_ref = refs[:7], refs[7:14], refs[14], refs[15]
    stripe, step = stripe_ref[0], pl.program_id(0)
    _, cols, above, below = halos[:4]
    _, low_cols, low_above, low_below = low_halos[:4]
    batch = x.shape[0]

    @pl.when(step == 0)
    def _():
        gather_halos(low, stripe, tab, low_top, low_bot, yup, ydn, 0, yec, yrecv, *low_halos)
        gather_halos(fld, stripe, tab, top, bot, up, dn, 0, ec, recv, *halos)
        size = GROUP * GROUP
        row, col = iota((size, size), 0), iota((size, size), 1)
        widen = (col == (row // GROUP) * GROUP + (row % GROUP + 1) // 2).astype(F32).astype(BF)
        joined = []
        for s in range(2):
            wide = mm(widen, low_cols[s].astype(BF))
            joined.append(jnp.concatenate([cols[s], wide], axis=1).astype(BF))
        ends_ref[0], ends_ref[1] = column_terms(side_weight, joined, out_ch)

    def one_face(k, carry):
        f = step * batch + k
        lines = row_stack(x, above, below, k, f, fld.rows)
        ends = face_terms([ends_ref[0], ends_ref[1]], f)
        low_lines = [low_above[f]] + [y[k, r] for r in range(low.rows)] + [low_below[f]]
        wide = [mm(cells, spread[...]).astype(BF) for cells in low_lines]
        made = []
        for r in range(fld.rows):
            picked = [wide[(r + a + 1) // 2] for a in range(3)]
            made.append(
                conv_row(weight[...], jnp.concatenate(lines(r) + picked, axis=0), ends, r, out_ch)
            )
        result = mm(head[...], jnp.concatenate(made, axis=0)).reshape(-1, fld.rows, fld.side)
        pred_out[:, k] = (atmos[:, k].astype(F32) + result[:vars_out]).astype(BF)
        flux[:, f] = jnp.where((land[k] == 1)[None], result[vars_out:], 0.0)
        return carry

    lax.fori_loop(0, batch, one_face, 0)

    @pl.when(step == fld.faces // batch - 1)
    def _():
        chosen = (row_key[...] == col_key[...]).astype(F32).astype(BF)
        tiles = flux[...].reshape(-1, fld.side).astype(BF)
        flux_out[...] = mm(chosen, tiles).astype(BF).reshape(flux_out.shape)


def ocean_kernel(cap, recv, state, into, out_weight, sea_out, back_out):
    tiles, _, side = recv.shape

    def one_source(t, carry):
        flux = recv[t].astype(F32)
        pad = (-flux.shape[0]) % 16
        flux = jnp.concatenate([flux, jnp.zeros((pad, side), F32)], axis=0).astype(BF)
        held = state[t]
        high = held.astype(BF)
        low = (held - high.astype(F32)).astype(BF)
        hidden = smooth(mm(into[...], jnp.concatenate([flux, flux, high, high, low], axis=0)))
        width = out_weight[...]
        wide = jnp.concatenate([width] * (side // LANES), axis=1)
        drift = (hidden * wide).reshape(cap, -1, side).sum(axis=1)
        drift = jnp.concatenate([drift, jnp.zeros((8 - cap, side), F32)], axis=0)
        sea = held[:8] + drift
        sea_out[t] = sea
        back_out[t] = sea.astype(BF)
        return carry

    lax.fori_loop(0, tiles, one_source, 0)


def surface_kernel(back, key, land, pred, out):
    faces, rows, side = land.shape
    slots = back[...].astype(F32).reshape(-1, side).astype(BF)
    chosen = (key[...] == iota((faces * rows, slots.shape[0]), 1)).astype(F32).astype(BF)
    sea = mm(chosen, slots).reshape(faces, rows, side)
    out[0] = jnp.where(land[...] == 1, sea, pred[0].astype(F32)).astype(BF)


def call(kernel, outs, ins, scratch, flops, smem=0, steps=1, specs=None, aliases=None, out_specs=None, name=None):
    whole = pl.BlockSpec(memory_space=pltpu.VMEM)
    in_specs = [pl.BlockSpec(memory_space=pltpu.SMEM)] * smem + [whole] * (len(ins) - smem)
    for position, spec in (specs or {}).items():
        in_specs[position] = spec
    grid = {"grid": (steps,)} if specs else {}
    moved = sum(int(np.prod(a.shape)) * a.dtype.itemsize for a in list(ins) + list(outs))
    return pl.pallas_call(
        kernel,
        out_shape=outs,
        **grid,
        in_specs=in_specs,
        out_specs=[(out_specs or {}).get(n, whole) for n in range(len(outs))],
        scratch_shapes=scratch,
        input_output_aliases=aliases or {},
        compiler_params=pltpu.CompilerParams(vmem_limit_bytes=56 * 1024 * 1024),
        cost_estimate=pl.CostEstimate(flops=int(flops), bytes_accessed=int(moved), transcendentals=0),
        name=name,
    )(*ins)


def swap_rows(top, bot):
    tiles = lax.axis_size("tile")
    ring = [(i, (i + 1) % tiles) for i in range(tiles)]
    up = lax.ppermute(bot, "tile", ring)
    return up, lax.ppermute(top, "tile", [(j, i) for i, j in ring])


def swap_chunks(chunks):
    return lax.all_to_all(chunks, "tile", split_axis=0, concat_axis=0, tiled=True)


def packed_weight(weight, chans):
    taps, out_ch, _ = weight.shape
    split = weight.reshape(taps, out_ch, taps, chans)
    body = jnp.transpose(split, (2, 1, 0, 3)).reshape(taps * out_ch, taps * chans)
    sides = jnp.stack([split[:, :, 0], split[:, :, 2]]).reshape(2, taps * out_ch, chans)
    return body, sides


def on_one_group(
    atmos_state,
    land_sea,
    owners,
    seam_table,
    ocean_state,
    conv_input,
    conv_encode,
    conv_coarse,
    conv_decode,
    output_head,
    ocean_in,
    ocean_out,
):
    in_ch, faces, rows, side = atmos_state.shape
    tiles = lax.axis_size("tile")
    width = conv_input.shape[1]
    stripe = lax.axis_index("tile").astype(jnp.int32).reshape(1)
    entry = Field(faces, rows, in_ch, side, tiles)
    full = Field(faces, rows, width, side, tiles)
    low = Field(faces, rows // 2, width, side // 2, tiles)
    cells = faces * rows * side

    order = np.arange(in_ch * rows)
    perm = np.zeros((in_ch * rows, in_ch * rows), np.float32)
    perm[order, (order % in_ch) * rows + order // in_ch] = 1.0
    spread = np.zeros((side // 2, side), np.float32)
    spread[np.arange(side) // 2, np.arange(side)] = 1.0
    perm, pool = jnp.asarray(perm, BF), jnp.asarray(0.25 * spread.T, BF)
    spread = jnp.asarray(spread, BF)

    def some(batch, shape, dim=0):
        block = tuple(batch if n == dim else size for n, size in enumerate(shape))
        return pl.BlockSpec(block, lambda i: tuple(i if n == dim else 0 for n in range(len(shape))))

    few, many = (3 if faces % 3 == 0 else 1), faces
    half = many // 2 if many % 2 == 0 else many
    ends = [pltpu.VMEM((2, width, GROUP * GROUP), F32)]
    x0, top, bot, ec, send = call(
        functools.partial(prep_kernel, entry),
        [entry.main()] + entry.edges() + entry.sends(),
        (stripe, seam_table, atmos_state, perm),
        entry.send_scratch(),
        2 * cells * in_ch * in_ch * rows,
        smem=2,
        steps=faces // half,
        specs={2: some(half, atmos_state.shape, 1)},
        out_specs={0: some(half, entry.main().shape)},
        name="prep",
    )
    got = swap_chunks(send)
    up, dn = swap_rows(top, bot)
    x1, top, bot, ec, send = call(
        functools.partial(level_kernel, entry, full, None, 0),
        [full.main()] + full.edges() + full.sends(),
        (stripe, seam_table, x0, top, bot, up, dn, ec, got) + packed_weight(conv_input, in_ch),
        full.send_scratch() + entry.halo_scratch() + ends,
        2 * cells * 9 * in_ch * width,
        smem=2,
        steps=faces // few,
        specs={2: some(few, x0.shape)},
        out_specs={0: some(few, full.main().shape)},
        name="conv_in",
    )
    got = swap_chunks(send)
    up, dn = swap_rows(top, bot)
    x2, y0, top, bot, ec, send, low_ec, low_send = call(
        functools.partial(level_kernel, full, full, low, 0),
        [full.main(), low.main()] + full.edges(side // 2) + full.sends() + low.sends(),
        (stripe, seam_table, x1, top, bot, up, dn, ec, got) + packed_weight(conv_encode, width) + (pool,),
        full.send_scratch() + low.send_scratch() + full.halo_scratch() + ends,
        2 * cells * 9 * width * width,
        smem=2,
        steps=faces // few,
        specs={2: some(few, x1.shape)},
        out_specs={0: some(few, full.main().shape), 1: some(few, low.main().shape)},
        name="encode",
    )
    low_got = swap_chunks(low_send)
    up, dn = swap_rows(top, bot)
    y1, low_top, low_bot, low_ec, low_send = call(
        functools.partial(level_kernel, low, low, None, side),
        [low.main()] + low.edges() + low.sends(),
        (stripe, seam_table, y0, top, bot, up, dn, low_ec, low_got) + packed_weight(conv_coarse, width),
        low.send_scratch() + low.halo_scratch() + ends,
        10e9,
        smem=2,
        steps=faces // many,
        specs={2: some(many, y0.shape)},
        out_specs={0: some(many, low.main().shape)},
        name="coarse",
    )
    low_send, got = lax.optimization_barrier((low_send, swap_chunks(send)))
    low_got = swap_chunks(low_send)
    low_up, low_dn = swap_rows(low_top, low_bot)

    taps = conv_decode.shape[0]
    split = conv_decode.reshape(taps, width, taps, 2, width)
    body = jnp.transpose(split, (2, 1, 3, 0, 4)).reshape(taps * width, 2 * taps * width)
    sides = jnp.stack([split[:, :, 0], split[:, :, 2]]).reshape(2, taps * width, 2 * width)
    heads = output_head.shape[0]
    flux_ch = heads - OUT_VARS
    eye = jnp.eye(rows, dtype=output_head.dtype)
    head = (output_head[:, None, None, :] * eye[None, :, :, None]).reshape(heads * rows, rows * width)

    slot_count = ocean_state.shape[2]
    cap = slot_count // tiles
    owner_ids = owners[:, 0]
    count = owner_ids.shape[0]
    earlier = np.tril(np.ones((count, count), bool), -1)
    rank = jnp.sum((owner_ids[:, None] == owner_ids[None, :]) & earlier, axis=1).astype(jnp.int32)
    slot_index = owner_ids * cap + rank
    col_key = (np.arange(flux_ch, dtype=np.int32)[:, None] * slot_count + slot_index[None, :]).reshape(1, -1)
    row_key = (
        np.arange(flux_ch, dtype=np.int32)[None, :, None] * slot_count
        + np.arange(slot_count, dtype=np.int32).reshape(tiles, 1, cap)
    ).reshape(-1, 1)
    row_key = jnp.asarray(row_key)
    pred, outgoing = call(
        functools.partial(decode_kernel, full, low, width, OUT_VARS),
        [
            jax.ShapeDtypeStruct((OUT_VARS, faces, rows, side), BF),
            jax.ShapeDtypeStruct((tiles, flux_ch * cap, side), BF),
        ],
        (stripe, seam_table, x2, top, bot, up, dn, ec, got)
        + (y1, low_top, low_bot, low_up, low_dn, low_ec, low_got)
        + (body, sides, spread, head, atmos_state, land_sea, row_key, col_key),
        full.halo_scratch()
        + low.halo_scratch()
        + [pltpu.VMEM((flux_ch, faces, rows, side), F32)]
        + ends,
        2 * cells * 18 * width * width,
        smem=2,
        steps=faces // few,
        specs={
            2: some(few, x2.shape),
            9: some(few, y1.shape),
            20: pl.BlockSpec((OUT_VARS, few, rows, side), lambda i: (0, i, 0, 0)),
            21: some(few, land_sea.shape),
        },
        out_specs={0: some(few, (OUT_VARS, faces, rows, side), 1)},
        name="decode",
    )
    arrived = lax.all_to_all(outgoing, "tile", split_axis=0, concat_axis=0, tiled=True)

    held = jnp.transpose(ocean_state[0, 0].reshape(tiles, cap, OCEAN_CH, side), (0, 2, 1, 3))
    state = jnp.pad(held, ((0, 0), (0, 0), (0, 8 - cap), (0, 0))).reshape(tiles, OCEAN_CH * 8, side)
    hidden = ocean_in.shape[0]
    high = ocean_in.astype(BF)
    rest = (ocean_in - high.astype(F32)).astype(BF)
    flux_pad = (-flux_ch * cap) % 16
    each = jnp.eye(cap, dtype=BF)
    slot8 = jnp.eye(cap, 8, dtype=BF)

    def flux_part(weights):
        part = each[:, None, None, :] * weights[None, :, OCEAN_CH:, None]
        return jnp.pad(part.reshape(cap * hidden, flux_ch * cap), ((0, 0), (0, flux_pad)))

    def state_part(weights):
        part = slot8[:, None, None, :] * weights[None, :, :OCEAN_CH, None]
        return part.reshape(cap * hidden, OCEAN_CH * 8)

    into = jnp.concatenate(
        [flux_part(high), flux_part(rest), state_part(high), state_part(rest), state_part(high)], axis=1
    )
    out_weight = jnp.broadcast_to(ocean_out[None, :, None], (cap, hidden, LANES)).reshape(-1, LANES)
    sea, back = call(
        functools.partial(ocean_kernel, cap),
        [jax.ShapeDtypeStruct((tiles, 8, side), F32), jax.ShapeDtypeStruct((tiles, 8, side), BF)],
        (arrived, state, into, out_weight),
        [],
        2 * slot_count * side * hidden * 8,
        name="ocean",
    )
    returned = lax.all_to_all(back, "tile", split_axis=0, concat_axis=0, tiled=True)
    key = (owner_ids * 8 + rank)[:, None]
    first = pl.BlockSpec((1, faces, rows, side), lambda i: (0, 0, 0, 0))
    (atmos_next,) = call(
        surface_kernel,
        [jax.ShapeDtypeStruct(pred.shape, BF)],
        (returned, key, land_sea, pred),
        [],
        2 * count * tiles * 8 * side,
        specs={3: first},
        out_specs={0: first},
        aliases={3: 0},
        name="surface",
    )
    renewed = jnp.stack([sea[:, :cap], held[:, 0]], axis=2)
    return atmos_next, renewed.reshape(1, 1, slot_count, OCEAN_CH, side)


def fits(mesh):
    return mesh.shape["face"] == 1


def solution(mesh):
    in_specs = (
        P(None, "face", "tile", None),
        P("face", "tile", None),
        P(("face", "tile"), None),
        P(),
        P("face", "tile", None, None, None),
        P(),
        P(),
        P(),
        P(),
        P(),
        P(),
        P(),
    )
    out_specs = (P(None, "face", "tile", None), P("face", "tile", None, None, None))
    return jax.shard_map(
        on_one_group if fits(mesh) else on_device,
        mesh=mesh,
        in_specs=in_specs,
        out_specs=out_specs,
        check_vma=False,
    )
```

```python
import functools

import jax
import jax.numpy as jnp
import numpy as np
from jax import lax
from jax.experimental import pallas as pl
from jax.experimental.pallas import tpu as pltpu
from jax.sharding import PartitionSpec as P

OUT_VARS = 8
FLUX_CH = 4
OCEAN_CH = 2


def extended(shard, sides, width):
    for axis, dim in sides:
        size, length = (lax.axis_size(axis), shard.shape[dim])
        up = [(i, (i + 1) % size) for i in range(size)]
        down = [(j, i) for i, j in up]
        last = lax.slice_in_dim(shard, length - width, length, axis=dim)
        initial = lax.slice_in_dim(shard, 0, width, axis=dim)
        before = lax.ppermute(last, axis, up)
        after = lax.ppermute(initial, axis, down)
        shard = jnp.concatenate([before, shard, after], axis=dim)
    return shard


def pad_field(values, seam_table):
    channels, faces_dev, stripe_rows, face_side = values.shape
    tile_count = lax.axis_size("tile")
    stripe = lax.axis_index("tile")
    face_group = lax.axis_index("face")
    rimmed = extended(values, (("tile", 2),), 1)
    edge_rows = jnp.stack([values[:, :, 0, :], rimmed[:, :, 0, :]], axis=2)
    edge_pieces = edge_rows.reshape(channels, faces_dev, 2, tile_count, stripe_rows)
    received = lax.all_to_all(edge_pieces, "tile", split_axis=3, concat_axis=3, tiled=True)
    row_part = received[:, :, :, 0, :]
    row_start = stripe * stripe_rows
    col_part = jnp.stack([values[:, :, :, 0], values[:, :, :, face_side - 1]], axis=2)
    seam_piece = jnp.concatenate([row_part, col_part], axis=2)
    seam_piece = jnp.transpose(seam_piece, (1, 2, 0, 3)).reshape(
        1, faces_dev, 4, channels * stripe_rows
    )
    own_sides = lax.dynamic_slice_in_dim(seam_table, face_group * (faces_dev * 4), faces_dev * 4, 0)
    gathered = lax.all_gather(seam_piece, ("face", "tile"), axis=0, tiled=True)
    group_count = gathered.shape[0] // tile_count
    strip_table = gathered.reshape(group_count, tile_count, faces_dev, 4, channels, stripe_rows)
    strip_table = jnp.transpose(strip_table, (0, 2, 3, 4, 1, 5)).reshape(
        group_count * faces_dev * 4, channels, face_side
    )
    strips = jnp.take(strip_table, own_sides[:, 0], axis=0)
    strips = jnp.where(own_sides[:, 1][:, None, None] == 1, strips[:, :, ::-1], strips)
    strips = jnp.transpose(strips.reshape(faces_dev, 4, channels, face_side), (2, 0, 1, 3))
    upper_row = jnp.where(stripe == 0, strips[:, :, 0, :], rimmed[:, :, 0, :])
    bottom = jnp.where(
        stripe == tile_count - 1, strips[:, :, 1, :], rimmed[:, :, stripe_rows + 1, :]
    )
    middle = jnp.concatenate([upper_row[:, :, None, :], values, bottom[:, :, None, :]], axis=2)
    zero_cells = jnp.zeros((channels, faces_dev, 2, 1), values.dtype)
    columns = jnp.concatenate([zero_cells, strips[:, :, 2:, :], zero_cells], axis=3)
    columns = lax.dynamic_slice_in_dim(columns, row_start, stripe_rows + 2, 3)
    return jnp.concatenate([columns[:, :, 0, :, None], middle, columns[:, :, 1, :, None]], axis=3)


def convolve(padded, weight):
    channels, faces_dev, rows_two, side_two = padded.shape
    stripe_rows = rows_two - 2
    face_side = side_two - 2
    planes = []
    for face_index in range(faces_dev):
        summed = jnp.zeros((weight.shape[1], stripe_rows * face_side), jnp.float32)
        for row_shift in range(3):
            tap_rows = jnp.concatenate(
                [
                    padded[
                        :,
                        face_index,
                        row_shift : row_shift + stripe_rows,
                        col_shift : col_shift + face_side,
                    ]
                    for col_shift in range(3)
                ],
                axis=0,
            )
            summed = summed + jnp.dot(
                weight[row_shift],
                tap_rows.reshape(3 * channels, stripe_rows * face_side),
                preferred_element_type=jnp.float32,
            )
        planes.append(jax.nn.gelu(summed).astype(jnp.bfloat16).reshape(-1, stripe_rows, face_side))
    return jnp.stack(planes, axis=1)


def upsample(values):
    return jnp.repeat(jnp.repeat(values, 2, axis=2), 2, axis=3)


def ocean_update(held_state, arrived_flux, ocean_in, ocean_out):
    stacked = jnp.concatenate([held_state, arrived_flux.astype(jnp.float32)], axis=1)
    hidden = jax.nn.gelu(
        jnp.einsum("hc,ncs->nhs", ocean_in, stacked, precision=lax.Precision.HIGHEST)
    )
    sea_now = held_state[:, 0] + jnp.einsum(
        "h,nhs->ns", ocean_out, hidden, precision=lax.Precision.HIGHEST
    )
    return jnp.stack([sea_now, held_state[:, 0]], axis=1)


def ocean_blocks(held_state, arrived_flux, ocean_in, ocean_out, block_count):
    slot_count, state_ch, face_side = held_state.shape
    capacity = slot_count // block_count
    held_split = held_state.reshape(block_count, capacity, state_ch, face_side)
    flux_split = arrived_flux.reshape(block_count, capacity, arrived_flux.shape[1], face_side)
    stepped = lax.map(
        lambda pair: ocean_update(pair[0], pair[1], ocean_in, ocean_out), (held_split, flux_split)
    )
    return stepped.reshape(slot_count, state_ch, face_side)


def on_device(
    atmos_state,
    land_sea,
    owners,
    seam_table,
    ocean_state,
    conv_input,
    conv_encode,
    conv_coarse,
    conv_decode,
    output_head,
    ocean_in,
    ocean_out,
):
    encoded = convolve(pad_field(atmos_state, seam_table), conv_input)
    skip_level = convolve(pad_field(encoded, seam_table), conv_encode)
    channels, faces_dev, stripe_rows, face_side = skip_level.shape
    pooled = (
        skip_level.astype(jnp.float32)
        .reshape(channels, faces_dev, stripe_rows // 2, 2, face_side // 2, 2)
        .mean(axis=(3, 5))
        .astype(jnp.bfloat16)
    )
    coarse_out = convolve(pad_field(pooled, seam_table), conv_coarse)
    coarse_pad = upsample(pad_field(coarse_out, seam_table))[
        :, :, 1 : stripe_rows + 3, 1 : face_side + 3
    ]
    padded = jnp.concatenate([pad_field(skip_level, seam_table), coarse_pad], axis=0)
    decoded = convolve(padded, conv_decode)
    head_out = jnp.dot(
        output_head, decoded.reshape(channels, -1), preferred_element_type=jnp.float32
    )
    head_out = head_out.reshape(-1, faces_dev, stripe_rows, face_side)
    predicted = atmos_state[:OUT_VARS].astype(jnp.float32) + head_out[:OUT_VARS]
    is_ocean = land_sea == 1
    fluxes = jnp.where(is_ocean[None], head_out[OUT_VARS:], 0.0).astype(jnp.bfloat16)
    flux_tiles = jnp.transpose(fluxes, (1, 2, 0, 3)).reshape(
        faces_dev * stripe_rows, FLUX_CH * face_side
    )
    tile_count = lax.axis_size("tile")
    owner_ids = owners[:, 0]
    owner_hits = (owner_ids[:, None] == jnp.arange(tile_count)[None, :]).astype(jnp.int32)
    slot_rank = jnp.sum((jnp.cumsum(owner_hits, axis=0) - 1) * owner_hits, axis=1)
    slot_count = ocean_state.shape[2]
    capacity = slot_count // tile_count
    slot_index = owner_ids * capacity + slot_rank
    selector = (jnp.arange(slot_count)[:, None] == slot_index[None, :]).astype(jnp.bfloat16)
    outgoing = jnp.dot(selector, flux_tiles, preferred_element_type=jnp.float32).astype(
        jnp.bfloat16
    )
    outgoing = outgoing.reshape(tile_count, capacity, FLUX_CH, face_side)
    held_state = ocean_state[0, 0]
    arrived = lax.all_to_all(outgoing, "tile", split_axis=0, concat_axis=0, tiled=True)
    renewed = ocean_blocks(
        held_state, arrived.reshape(slot_count, FLUX_CH, face_side), ocean_in, ocean_out, tile_count
    )
    sea_back = renewed[:, 0].astype(jnp.bfloat16).reshape(tile_count, capacity, face_side)
    sea_slots = lax.all_to_all(sea_back, "tile", split_axis=0, concat_axis=0, tiled=True)
    sea_tiles = jnp.dot(
        selector.T, sea_slots.reshape(slot_count, face_side), preferred_element_type=jnp.float32
    )
    sea_temp = sea_tiles.reshape(faces_dev, stripe_rows, face_side)
    surface = jnp.where(is_ocean, sea_temp, predicted[0])
    atmos_next = jnp.concatenate([surface[None], predicted[1:]], axis=0).astype(jnp.bfloat16)
    return (atmos_next, renewed.reshape(1, 1, slot_count, OCEAN_CH, face_side))


GROUP = 16
LANES = 128
VMEM = pltpu.VMEM
BF = jnp.bfloat16
F32 = jnp.float32
NT = (((1,), (1,)), ((), ()))


def mm(a, b):
    return jnp.dot(a, b, preferred_element_type=F32)


def mm_nt(a, b):
    return lax.dot_general(a, b, NT, preferred_element_type=F32)


def iota(shape, dim):
    return lax.broadcasted_iota(jnp.int32, shape, dim)


def smooth(x):
    inner = x * (0.7978845608028654 + 0.03567740813636141 * (x * x))
    half = 0.5 * x
    return half * jnp.tanh(inner) + half


class Field:
    def __init__(self, faces, rows, chans, side, tiles):
        self.faces, self.rows, self.chans, self.side, self.tiles = faces, rows, chans, side, tiles
        self.per = LANES // chans
        self.groups = faces // self.per
        self.span = rows + 2
        self.extra = self.groups * self.span
        used = max(self.extra + 2 * self.groups, 2 * self.groups * rows)
        self.chunk = used + (-used) % 16

    def main(self):
        return jax.ShapeDtypeStruct((self.faces, self.rows, self.chans, self.side), BF)

    def edges(self, more=0):
        edge = jax.ShapeDtypeStruct((self.faces, self.chans, self.side + more), BF)
        return [edge, edge]

    def sends(self):
        return [
            jax.ShapeDtypeStruct((2 * self.faces * 8, self.chans), BF),
            jax.ShapeDtypeStruct((self.tiles, self.chunk, LANES), BF),
        ]

    def send_scratch(self):
        return [
            pltpu.VMEM((2, self.faces, 8, self.chans), F32),
            pltpu.VMEM((self.tiles, self.chunk, LANES), F32),
            pltpu.VMEM((self.side + 8, LANES), F32),
            pltpu.VMEM((16, self.rows * self.side), BF),
            pltpu.VMEM((2, self.side, self.side), BF),
        ]

    def halo_scratch(self):
        return [
            pltpu.VMEM((6, self.faces, GROUP, self.chans), F32),
            pltpu.VMEM((2, GROUP * GROUP, self.chans), F32),
            pltpu.VMEM((self.faces, self.chans, self.side), BF),
            pltpu.VMEM((self.faces, self.chans, self.side), BF),
            pltpu.VMEM((2, self.faces, self.chans, self.side), BF),
            pltpu.VMEM((self.tiles, self.chunk, LANES), F32),
            pltpu.VMEM((2, self.faces, 8, self.chans), F32),
            pltpu.VMEM((2, self.side, self.side), BF),
        ]


def fill_flips(flips):
    size = flips.shape[1]
    row, col = iota((size, size), 0), iota((size, size), 1)
    flips[0] = (row == col).astype(F32).astype(BF)
    flips[1] = (row + col == size - 1).astype(F32).astype(BF)


def end_picker(side):
    row, col = iota((16, side), 0), iota((16, side), 1)
    return (((row == 0) & (col == 0)) | ((row == 1) & (col == side - 1))).astype(F32).astype(BF)


def column_picker(fld):
    length = fld.rows * fld.side
    row, col = iota((16, length), 0), iota((16, length), 1)
    want = (row & 7) * fld.side + (row >> 3) * (fld.side - 1)
    return (col == want).astype(F32).astype(BF)


def keep_columns(picker, face_rows, f, cols):
    picked = mm_nt(picker, jnp.concatenate(face_rows, axis=1))
    cols[0, f] = picked[:8]
    cols[1, f] = picked[8:]


def pack_sends(fld, stripe, tab, top, bot, off, ec_out, send_out, cols, stage, strip, picker, flips):
    last, rows, chans, groups, per = fld.tiles - 1, fld.rows, fld.chans, fld.groups, fld.per
    held = cols[...]
    ec_out[...] = held.reshape(2 * fld.faces * 8, chans).astype(BF)
    paired = held.reshape(2, groups, per, 8, chans)
    packed = jnp.concatenate([paired[:, :, j] for j in range(per)], axis=3)
    across = packed[:, :, :rows].reshape(2 * groups * rows, LANES)
    initial = packed[:, :, 0].reshape(2 * groups, LANES)
    final = packed[:, :, rows - 1].reshape(2 * groups, LANES)
    pieces = []
    for q in range(2):
        for g in range(fld.faces):
            p = tab[4 * g + q, 0]
            pieces.append(cols[jnp.maximum((p & 3) - 2, 0), p >> 2][:rows])
    merged = [jnp.concatenate(pieces[n : n + per], axis=1) for n in range(0, len(pieces), per)]
    stage[...] = jnp.zeros_like(stage)
    for q in range(2):
        for i in range(groups):
            stage[q * last, i * fld.span + 1 : i * fld.span + 1 + rows, :] = merged[q * groups + i]

    def lanes(h):
        return slice((h % per) * chans, (h % per + 1) * chans)

    @pl.when((stripe == 0) | (stripe == last))
    def _():
        q = jnp.where(stripe == 0, 0, 1)
        fill_flips(flips)
        for i in range(groups):
            turned = []
            for h in range(i * per, (i + 1) * per):
                upper = top[h, :, off : off + fld.side].astype(F32)
                lower = bot[h, :, off : off + fld.side].astype(F32)
                cells = jnp.where(q == 0, upper, lower).astype(BF)
                turned.append(mm_nt(flips[tab[4 * h + q, 1]], cells))
            strip[0:8] = jnp.zeros((8, LANES), F32)
            strip[fld.side : fld.side + 8] = jnp.zeros((8, LANES), F32)
            strip[1 : fld.side + 1, :] = jnp.concatenate(turned, axis=1)
            for d in range(1, last, 10):
                here = range(d, min(d + 10, last))
                taken = [strip[e * rows : e * rows + fld.span, :] for e in here]
                for e, piece in zip(here, taken):
                    stage[e, i * fld.span : (i + 1) * fld.span, :] = piece

    stage[last - stripe, : 2 * groups * rows, :] = across

    @pl.when(stripe < last)
    def _():
        stage[last - 1 - stripe, fld.extra : fld.extra + 2 * groups, :] = final

    @pl.when(stripe > 0)
    def _():
        stage[last + 1 - stripe, fld.extra : fld.extra + 2 * groups, :] = initial

    send_out[...] = stage[...].astype(BF)


def gather_halos(fld, stripe, tab, top, bot, up, dn, off, ec, recv, cand, cols, above, below, pair, got, mirror, flips):
    faces, rows, chans, side, tiles = fld.faces, fld.rows, fld.chans, fld.side, fld.tiles
    last = tiles - 1
    groups = fld.groups
    got[...] = recv[...].astype(F32)
    own = ec[...].astype(F32).reshape(2, faces, 8, chans)
    row, col = iota((groups * rows, groups * rows), 0), iota((groups * rows, groups * rows), 1)
    turn = ((row // rows == col // rows) & (row % rows + col % rows == rows - 1)).astype(F32).astype(BF)
    prow, pcol = iota((16, side), 0), iota((16, side), 1)

    def lanes(h):
        return slice((h % fld.per) * chans, (h % fld.per + 1) * chans)

    here = slice(off, off + side)
    above[...] = up[:, :, here]
    below[...] = dn[:, :, here]
    over = mm_nt(end_picker(side), above[...].reshape(faces * chans, side))
    under = mm_nt(end_picker(side), below[...].reshape(faces * chans, side))
    heads = [got[q * last, : fld.extra, :] for q in range(2)]
    before = got[jnp.minimum(last + 1 - stripe, last), fld.extra : fld.extra + 2 * groups, :]
    after = got[jnp.maximum(last - 1 - stripe, 0), fld.extra : fld.extra + 2 * groups, :]
    for s in range(2):
        across = got[last - stripe, s * groups * rows : (s + 1) * groups * rows, :]
        turned = mm(turn, across.astype(BF))
        for h in range(faces):
            i = h // fld.per
            cand[2 + s, h, 0:1] = over[s : s + 1, h * chans : (h + 1) * chans]
            cand[2 + s, h, rows + 1 : rows + 2] = under[s : s + 1, h * chans : (h + 1) * chans]
            cand[2 + s, h, 1 : rows + 1] = own[s, h, :rows]
            mirror[s, h, :rows] = across[i * rows : (i + 1) * rows, lanes(h)]
            cand[4 + s, h, 0:1] = before[s * groups + i : s * groups + i + 1, lanes(h)]
            cand[4 + s, h, rows + 1 : rows + 2] = after[s * groups + i : s * groups + i + 1, lanes(h)]
            cand[4 + s, h, 1 : rows + 1] = turned[i * rows : (i + 1) * rows, lanes(h)]
    at_edge = (stripe == 0) | (stripe == last)

    @pl.when(jnp.logical_not(at_edge))
    def _():
        for q in range(2):
            for h in range(faces):
                i = h // fld.per
                cand[q, h, 0 : fld.span] = heads[q][i * fld.span : (i + 1) * fld.span, lanes(h)]

    @pl.when(at_edge)
    def _():
        q = jnp.where(stripe == 0, 0, 1)
        fill_flips(flips)
        for h in range(faces):
            pair[0, h] = jnp.where(q == 0, top[h, :, here].astype(F32), below[h].astype(F32)).astype(BF)
            pair[1, h] = jnp.where(q == 0, above[h].astype(F32), bot[h, :, here].astype(F32)).astype(BF)
        place = stripe * rows - 1 + prow
        inside = (place >= 0) & (place < side)
        windows = []
        for s in range(2):
            for h in range(faces):
                want = jnp.where(tab[4 * h + s, 1] == 1, side - 1 - place, place)
                window = ((pcol == want) & inside).astype(F32).astype(BF)
                windows.append(mm_nt(window, pair[s, h]))
        pieces = []
        for g in range(faces):
            p = tab[4 * g + q, 0]
            pieces.append(mirror[jnp.maximum((p & 3) - 2, 0), p >> 2][:rows])
        for s in range(2):
            for h in range(faces):
                cand[s, h] = windows[s * faces + h]
        for i in range(groups):
            merged = jnp.concatenate(pieces[i * fld.per : (i + 1) * fld.per], axis=1)
            got[last - stripe, i * fld.span + 1 : i * fld.span + 1 + rows, :] = merged
        for i in range(groups):
            lined = jnp.concatenate(
                [got[d, i * fld.span + 1 : i * fld.span + 1 + rows, :] for d in range(tiles)], axis=0
            )
            lined = jnp.transpose(lined)
            for j in range(fld.per):
                g = i * fld.per + j
                p = tab[4 * g + q, 0]
                kind, h = p & 3, p >> 2
                near = pair[jnp.minimum(kind, 1), h].astype(F32)
                far = lined[j * chans : (j + 1) * chans]
                cells = jnp.where(kind < 2, near, far).astype(BF)
                placed = mm(cells, flips[tab[4 * g + q, 1]]).astype(BF)

                @pl.when(q == 0)
                def _():
                    above[g] = placed

                @pl.when(q == 1)
                def _():
                    below[g] = placed

    slot = iota((GROUP, chans), 0)
    live = (slot < fld.span) & jnp.logical_not(
        ((slot == 0) & (stripe == 0)) | ((slot == rows + 1) & (stripe == last))
    )
    for s in range(2):
        taken = []
        for g in range(faces):
            p = tab[4 * g + 2 + s, 0]
            kind, h = p & 3, p >> 2
            which = jnp.where((kind >= 2) & (tab[4 * g + 2 + s, 1] == 1), kind + 2, kind)
            taken.append(jnp.where(live, cand[which, h], 0.0))
        taken.append(jnp.zeros(((GROUP - faces) * GROUP, chans), F32))
        cols[s] = jnp.concatenate(taken, axis=0)


def column_terms(side_weight, cols, out_ch):
    terms = []
    for s in range(2):
        part = mm_nt(side_weight[s], cols[s])
        size = part.shape[1]
        terms.append(
            part[out_ch : 2 * out_ch]
            + pltpu.roll(part[:out_ch], 1, 1)
            + pltpu.roll(part[2 * out_ch :], size - 1, 1)
        )
    return terms


def face_terms(terms, face_index):
    size = terms[0].shape[1]
    shift = lax.rem(2 * size - GROUP * face_index - 1, size)
    return [pltpu.roll(term, shift, 1)[:, :LANES] for term in terms]


def conv_row(weight, stacked, terms, r, out_ch):
    z = mm(weight, stacked)
    side = z.shape[1]
    left, right = pltpu.roll(z[:out_ch], 1, 1), pltpu.roll(z[2 * out_ch :], side - 1, 1)
    lane = iota((out_ch, LANES), 1)
    first = terms[0] if r == 0 else pltpu.roll(terms[0], LANES - r, 1)
    final = pltpu.roll(terms[1], LANES - 1 - r, 1)
    head = jnp.where(lane == 0, first, left[:, :LANES])
    tail = jnp.where(lane == LANES - 1, final, right[:, side - LANES :])
    if side > LANES:
        left = jnp.concatenate([head, left[:, LANES:]], axis=1)
        right = jnp.concatenate([right[:, : side - LANES], tail], axis=1)
    else:
        left, right = head, tail
    return smooth(z[out_ch : 2 * out_ch] + left + right).astype(BF)


def row_stack(x, above, below, k, f, rows):
    lines = [above[f]] + [x[k, r] for r in range(rows)] + [below[f]]
    return lambda r: lines[r : r + 3]


def prep_kernel(fld, stripe_ref, tab, atmos, perm, x_out, top, bot, ec_out, send_out, *sends):
    stripe, step = stripe_ref[0], pl.program_id(0)
    batch = x_out.shape[0]

    @pl.when(step == 0)
    def _():
        sends[3][...] = column_picker(fld)

    def one_face(k, carry):
        f = step * batch + k
        block = atmos[:, k].astype(F32).reshape(fld.chans * fld.rows, fld.side).astype(BF)
        moved = mm(perm[...], block).astype(BF)
        lines = [moved[r * fld.chans : (r + 1) * fld.chans] for r in range(fld.rows)]
        for r in range(fld.rows):
            x_out[k, r] = lines[r]
        top[f] = lines[0]
        bot[f] = lines[-1]
        keep_columns(sends[3][...], lines, f, sends[0])
        return carry

    lax.fori_loop(0, batch, one_face, 0)

    @pl.when(step == fld.faces // batch - 1)
    def _():
        pack_sends(fld, stripe, tab, top, bot, 0, ec_out, send_out, *sends)


def level_kernel(fld, out_fld, low, off, stripe_ref, tab, x, old_top, old_bot, up, dn, ec, recv, weight, side_weight, *refs):
    stripe, step = stripe_ref[0], pl.program_id(0)
    if low is None:
        outs, sends, halos = refs[:5], refs[5:10], refs[10:]
        x_out, top, bot, ec_out, send_out = outs
    else:
        pool, outs, sends, low_sends, halos = refs[0], refs[1:9], refs[9:14], refs[14:19], refs[19:]
        x_out, y_out, top, bot, ec_out, send_out, low_ec, low_send = outs
    *halos, ends_ref = halos
    batch = x_out.shape[0]
    _, cols, above, below = halos[:4]
    side = fld.side

    @pl.when(step == 0)
    def _():
        gather_halos(fld, stripe, tab, old_top, old_bot, up, dn, off, ec, recv, *halos)
        terms = column_terms(side_weight, [cols[0].astype(BF), cols[1].astype(BF)], out_fld.chans)
        ends_ref[0], ends_ref[1] = terms
        sends[3][...] = column_picker(out_fld)
        if low is not None:
            low_sends[3][...] = column_picker(low)

    def one_face(k, carry):
        f = step * batch + k
        lines = row_stack(x, above, below, k, f, fld.rows)
        ends = face_terms([ends_ref[0], ends_ref[1]], f)
        made, pooled = [], []
        for r in range(fld.rows):
            cells = conv_row(weight[...], jnp.concatenate(lines(r), axis=0), ends, r, out_fld.chans)
            x_out[k, r] = cells
            made.append(cells)
            if low is not None and r % 2 == 1:
                mean = (mm(made[r - 1], pool[...]) + mm(cells, pool[...])).astype(BF)
                y_out[k, r // 2] = mean
                pooled.append(mean)
        top[f, :, :side] = made[0]
        bot[f, :, :side] = made[-1]
        keep_columns(sends[3][...], made, f, sends[0])
        if low is not None:
            top[f, :, side:] = pooled[0]
            bot[f, :, side:] = pooled[-1]
            keep_columns(low_sends[3][...], pooled, f, low_sends[0])
        return carry

    lax.fori_loop(0, batch, one_face, 0)

    @pl.when(step == fld.faces // batch - 1)
    def _():
        if low is not None:
            pack_sends(low, stripe, tab, top, bot, side, low_ec, low_send, *low_sends)
        pack_sends(out_fld, stripe, tab, top, bot, 0, ec_out, send_out, *sends)


def decode_kernel(fld, low, out_ch, vars_out, stripe_ref, tab, x, top, bot, up, dn, ec, recv, y, low_top, low_bot, yup, ydn, yec, yrecv, weight, side_weight, spread, head, atmos, land, row_key, col_key, pred_out, flux_out, *refs):
    halos, low_halos, flux, ends_ref = refs[:8], refs[8:16], refs[16], refs[17]
    stripe, step = stripe_ref[0], pl.program_id(0)
    _, cols, above, below = halos[:4]
    _, low_cols, low_above, low_below = low_halos[:4]
    batch = x.shape[0]

    @pl.when(step == 0)
    def _():
        gather_halos(low, stripe, tab, low_top, low_bot, yup, ydn, 0, yec, yrecv, *low_halos)
        gather_halos(fld, stripe, tab, top, bot, up, dn, 0, ec, recv, *halos)
        size = GROUP * GROUP
        row, col = iota((size, size), 0), iota((size, size), 1)
        widen = (col == (row // GROUP) * GROUP + (row % GROUP + 1) // 2).astype(F32).astype(BF)
        joined = []
        for s in range(2):
            wide = mm(widen, low_cols[s].astype(BF))
            joined.append(jnp.concatenate([cols[s], wide], axis=1).astype(BF))
        ends_ref[0], ends_ref[1] = column_terms(side_weight, joined, out_ch)

    def one_face(k, carry):
        f = step * batch + k
        lines = row_stack(x, above, below, k, f, fld.rows)
        ends = face_terms([ends_ref[0], ends_ref[1]], f)
        low_lines = [low_above[f]] + [y[k, r] for r in range(low.rows)] + [low_below[f]]
        wide = [mm(cells, spread[...]).astype(BF) for cells in low_lines]
        made = []
        for r in range(fld.rows):
            picked = [wide[(r + a + 1) // 2] for a in range(3)]
            made.append(
                conv_row(weight[...], jnp.concatenate(lines(r) + picked, axis=0), ends, r, out_ch)
            )
        result = mm(head[...], jnp.concatenate(made, axis=0)).reshape(-1, fld.rows, fld.side)
        pred_out[:, k] = (atmos[:, k].astype(F32) + result[:vars_out]).astype(BF)
        flux[:, f] = jnp.where((land[k] == 1)[None], result[vars_out:], 0.0)
        return carry

    lax.fori_loop(0, batch, one_face, 0)

    @pl.when(step == fld.faces // batch - 1)
    def _():
        chosen = (row_key[...] == col_key[...]).astype(F32).astype(BF)
        tiles = flux[...].reshape(-1, fld.side).astype(BF)
        flux_out[...] = mm(chosen, tiles).astype(BF).reshape(flux_out.shape)


def ocean_kernel(cap, recv, state, into, out_weight, sea_out, back_out):
    tiles, _, side = recv.shape

    hidden = into.shape[0] // cap
    unit = 2 if tiles % 2 == 0 else 1

    def one_source(t):
        flux = recv[t].astype(F32)
        pad = (-flux.shape[0]) % 16
        flux = jnp.concatenate([flux, jnp.zeros((pad, side), F32)], axis=0).astype(BF)
        held = state[t]
        high = held.astype(BF)
        low = (held - high.astype(F32)).astype(BF)
        stacked = jnp.concatenate([flux, flux, high, high, low], axis=0)
        width = jnp.concatenate([out_weight[...]] * (side // LANES), axis=1)
        drift = []
        for k in range(cap):
            grown = smooth(mm(into[k * hidden : (k + 1) * hidden, :], stacked)) * width
            drift.append(grown.sum(axis=0, keepdims=True))
        drift.append(jnp.zeros((8 - cap, side), F32))
        return held[:8] + jnp.concatenate(drift, axis=0)

    def some_sources(n, carry):
        made = [one_source(n * unit + u) for u in range(unit)]
        for u, sea in enumerate(made):
            sea_out[n * unit + u] = sea
            back_out[n * unit + u] = sea.astype(BF)
        return carry

    lax.fori_loop(0, tiles // unit, some_sources, 0)


def surface_kernel(back, key, land, pred, out):
    faces, rows, side = land.shape
    slots = back[...].astype(F32).reshape(-1, side).astype(BF)
    chosen = (key[...] == iota((faces * rows, slots.shape[0]), 1)).astype(F32).astype(BF)
    sea = mm(chosen, slots).reshape(faces, rows, side)
    out[0] = jnp.where(land[...] == 1, sea, pred[0].astype(F32)).astype(BF)


def call(kernel, outs, ins, scratch, flops, smem=0, steps=1, specs=None, aliases=None, out_specs=None, name=None):
    whole = pl.BlockSpec(memory_space=pltpu.VMEM)
    in_specs = [pl.BlockSpec(memory_space=pltpu.SMEM)] * smem + [whole] * (len(ins) - smem)
    for position, spec in (specs or {}).items():
        in_specs[position] = spec
    grid = {"grid": (steps,)} if specs else {}
    moved = sum(int(np.prod(a.shape)) * a.dtype.itemsize for a in list(ins) + list(outs))
    return pl.pallas_call(
        kernel,
        out_shape=outs,
        **grid,
        in_specs=in_specs,
        out_specs=[(out_specs or {}).get(n, whole) for n in range(len(outs))],
        scratch_shapes=scratch,
        input_output_aliases=aliases or {},
        compiler_params=pltpu.CompilerParams(vmem_limit_bytes=56 * 1024 * 1024),
        cost_estimate=pl.CostEstimate(flops=int(flops), bytes_accessed=int(moved), transcendentals=0),
        name=name,
    )(*ins)


def swap_rows(top, bot):
    tiles = lax.axis_size("tile")
    ring = [(i, (i + 1) % tiles) for i in range(tiles)]
    up = lax.ppermute(bot, "tile", ring)
    return up, lax.ppermute(top, "tile", [(j, i) for i, j in ring])


def swap_chunks(chunks):
    return lax.all_to_all(chunks, "tile", split_axis=0, concat_axis=0, tiled=True)


def packed_weight(weight, chans):
    taps, out_ch, _ = weight.shape
    split = weight.reshape(taps, out_ch, taps, chans)
    body = jnp.transpose(split, (2, 1, 0, 3)).reshape(taps * out_ch, taps * chans)
    sides = jnp.stack([split[:, :, 0], split[:, :, 2]]).reshape(2, taps * out_ch, chans)
    return body, sides


def on_one_group(
    atmos_state,
    land_sea,
    owners,
    seam_table,
    ocean_state,
    conv_input,
    conv_encode,
    conv_coarse,
    conv_decode,
    output_head,
    ocean_in,
    ocean_out,
):
    in_ch, faces, rows, side = atmos_state.shape
    tiles = lax.axis_size("tile")
    width = conv_input.shape[1]
    stripe = lax.axis_index("tile").astype(jnp.int32).reshape(1)
    entry = Field(faces, rows, in_ch, side, tiles)
    full = Field(faces, rows, width, side, tiles)
    low = Field(faces, rows // 2, width, side // 2, tiles)
    cells = faces * rows * side

    order = np.arange(in_ch * rows)
    perm = np.zeros((in_ch * rows, in_ch * rows), np.float32)
    perm[order, (order % in_ch) * rows + order // in_ch] = 1.0
    spread = np.zeros((side // 2, side), np.float32)
    spread[np.arange(side) // 2, np.arange(side)] = 1.0
    perm, pool = jnp.asarray(perm, BF), jnp.asarray(0.25 * spread.T, BF)
    spread = jnp.asarray(spread, BF)

    def some(batch, shape, dim=0):
        block = tuple(batch if n == dim else size for n, size in enumerate(shape))
        return pl.BlockSpec(block, lambda i: tuple(i if n == dim else 0 for n in range(len(shape))))

    few, many = (3 if faces % 3 == 0 else 1), faces
    half = many // 2 if many % 2 == 0 else many
    ends = [pltpu.VMEM((2, width, GROUP * GROUP), F32)]
    x0, top, bot, ec, send = call(
        functools.partial(prep_kernel, entry),
        [entry.main()] + entry.edges() + entry.sends(),
        (stripe, seam_table, atmos_state, perm),
        entry.send_scratch(),
        2 * cells * in_ch * in_ch * rows,
        smem=2,
        steps=faces // half,
        specs={2: some(half, atmos_state.shape, 1)},
        out_specs={0: some(half, entry.main().shape)},
        name="prep",
    )
    got = swap_chunks(send)
    up, dn = swap_rows(top, bot)
    x1, top, bot, ec, send = call(
        functools.partial(level_kernel, entry, full, None, 0),
        [full.main()] + full.edges() + full.sends(),
        (stripe, seam_table, x0, top, bot, up, dn, ec, got) + packed_weight(conv_input, in_ch),
        full.send_scratch() + entry.halo_scratch() + ends,
        2 * cells * 9 * in_ch * width,
        smem=2,
        steps=faces // few,
        specs={2: some(few, x0.shape)},
        out_specs={0: some(few, full.main().shape)},
        name="conv_in",
    )
    got = swap_chunks(send)
    up, dn = swap_rows(top, bot)
    x2, y0, top, bot, ec, send, low_ec, low_send = call(
        functools.partial(level_kernel, full, full, low, 0),
        [full.main(), low.main()] + full.edges(side // 2) + full.sends() + low.sends(),
        (stripe, seam_table, x1, top, bot, up, dn, ec, got) + packed_weight(conv_encode, width) + (pool,),
        full.send_scratch() + low.send_scratch() + full.halo_scratch() + ends,
        2 * cells * 9 * width * width,
        smem=2,
        steps=faces // few,
        specs={2: some(few, x1.shape)},
        out_specs={0: some(few, full.main().shape), 1: some(few, low.main().shape)},
        name="encode",
    )
    low_got = swap_chunks(low_send)
    up, dn = swap_rows(top, bot)
    y1, low_top, low_bot, low_ec, low_send = call(
        functools.partial(level_kernel, low, low, None, side),
        [low.main()] + low.edges() + low.sends(),
        (stripe, seam_table, y0, top, bot, up, dn, low_ec, low_got) + packed_weight(conv_coarse, width),
        low.send_scratch() + low.halo_scratch() + ends,
        10e9,
        smem=2,
        steps=faces // many,
        specs={2: some(many, y0.shape)},
        out_specs={0: some(many, low.main().shape)},
        name="coarse",
    )
    low_send, got = lax.optimization_barrier((low_send, swap_chunks(send)))
    low_got = swap_chunks(low_send)
    low_up, low_dn = swap_rows(low_top, low_bot)

    taps = conv_decode.shape[0]
    split = conv_decode.reshape(taps, width, taps, 2, width)
    body = jnp.transpose(split, (2, 1, 3, 0, 4)).reshape(taps * width, 2 * taps * width)
    sides = jnp.stack([split[:, :, 0], split[:, :, 2]]).reshape(2, taps * width, 2 * width)
    heads = output_head.shape[0]
    flux_ch = heads - OUT_VARS
    eye = jnp.eye(rows, dtype=output_head.dtype)
    head = (output_head[:, None, None, :] * eye[None, :, :, None]).reshape(heads * rows, rows * width)

    slot_count = ocean_state.shape[2]
    cap = slot_count // tiles
    owner_ids = owners[:, 0]
    count = owner_ids.shape[0]
    earlier = np.tril(np.ones((count, count), bool), -1)
    rank = jnp.sum((owner_ids[:, None] == owner_ids[None, :]) & earlier, axis=1).astype(jnp.int32)
    slot_index = owner_ids * cap + rank
    col_key = (np.arange(flux_ch, dtype=np.int32)[:, None] * slot_count + slot_index[None, :]).reshape(1, -1)
    row_key = (
        np.arange(flux_ch, dtype=np.int32)[None, :, None] * slot_count
        + np.arange(slot_count, dtype=np.int32).reshape(tiles, 1, cap)
    ).reshape(-1, 1)
    row_key = jnp.asarray(row_key)
    pred, outgoing = call(
        functools.partial(decode_kernel, full, low, width, OUT_VARS),
        [
            jax.ShapeDtypeStruct((OUT_VARS, faces, rows, side), BF),
            jax.ShapeDtypeStruct((tiles, flux_ch * cap, side), BF),
        ],
        (stripe, seam_table, x2, top, bot, up, dn, ec, got)
        + (y1, low_top, low_bot, low_up, low_dn, low_ec, low_got)
        + (body, sides, spread, head, atmos_state, land_sea, row_key, col_key),
        full.halo_scratch()
        + low.halo_scratch()
        + [pltpu.VMEM((flux_ch, faces, rows, side), F32)]
        + ends,
        2 * cells * 18 * width * width,
        smem=2,
        steps=faces // few,
        specs={
            2: some(few, x2.shape),
            9: some(few, y1.shape),
            20: pl.BlockSpec((OUT_VARS, few, rows, side), lambda i: (0, i, 0, 0)),
            21: some(few, land_sea.shape),
        },
        out_specs={0: some(few, (OUT_VARS, faces, rows, side), 1)},
        name="decode",
    )
    arrived = lax.all_to_all(outgoing, "tile", split_axis=0, concat_axis=0, tiled=True)

    held = jnp.transpose(ocean_state[0, 0].reshape(tiles, cap, OCEAN_CH, side), (0, 2, 1, 3))
    state = jnp.pad(held, ((0, 0), (0, 0), (0, 8 - cap), (0, 0))).reshape(tiles, OCEAN_CH * 8, side)
    hidden = ocean_in.shape[0]
    high = ocean_in.astype(BF)
    rest = (ocean_in - high.astype(F32)).astype(BF)
    flux_pad = (-flux_ch * cap) % 16
    each = jnp.eye(cap, dtype=BF)
    slot8 = jnp.eye(cap, 8, dtype=BF)

    def flux_part(weights):
        part = each[:, None, None, :] * weights[None, :, OCEAN_CH:, None]
        return jnp.pad(part.reshape(cap * hidden, flux_ch * cap), ((0, 0), (0, flux_pad)))

    def state_part(weights):
        part = slot8[:, None, None, :] * weights[None, :, :OCEAN_CH, None]
        return part.reshape(cap * hidden, OCEAN_CH * 8)

    into = jnp.concatenate(
        [flux_part(high), flux_part(rest), state_part(high), state_part(rest), state_part(high)], axis=1
    )
    out_weight = jnp.broadcast_to(ocean_out[:, None], (hidden, LANES))
    sea, back = call(
        functools.partial(ocean_kernel, cap),
        [jax.ShapeDtypeStruct((tiles, 8, side), F32), jax.ShapeDtypeStruct((tiles, 8, side), BF)],
        (arrived, state, into, out_weight),
        [],
        2 * slot_count * side * hidden * 8,
        name="ocean",
    )
    returned = lax.all_to_all(back, "tile", split_axis=0, concat_axis=0, tiled=True)
    key = (owner_ids * 8 + rank)[:, None]
    first = pl.BlockSpec((1, faces, rows, side), lambda i: (0, 0, 0, 0))
    (atmos_next,) = call(
        surface_kernel,
        [jax.ShapeDtypeStruct(pred.shape, BF)],
        (returned, key, land_sea, pred),
        [],
        2 * count * tiles * 8 * side,
        specs={3: first},
        out_specs={0: first},
        aliases={3: 0},
        name="surface",
    )
    renewed = jnp.stack([sea[:, :cap], held[:, 0]], axis=2)
    return atmos_next, renewed.reshape(1, 1, slot_count, OCEAN_CH, side)


def fits(mesh):
    return mesh.shape["face"] == 1


def solution(mesh):
    in_specs = (
        P(None, "face", "tile", None),
        P("face", "tile", None),
        P(("face", "tile"), None),
        P(),
        P("face", "tile", None, None, None),
        P(),
        P(),
        P(),
        P(),
        P(),
        P(),
        P(),
    )
    out_specs = (P(None, "face", "tile", None), P("face", "tile", None, None, None))
    return jax.shard_map(
        on_one_group if fits(mesh) else on_device,
        mesh=mesh,
        in_specs=in_specs,
        out_specs=out_specs,
        check_vma=False,
    )
```

```python
import functools

import jax
import jax.numpy as jnp
import numpy as np
from jax import lax
from jax.experimental import pallas as pl
from jax.experimental.pallas import tpu as pltpu
from jax.sharding import PartitionSpec as P

OUT_VARS = 8
FLUX_CH = 4
OCEAN_CH = 2


def extended(shard, sides, width):
    for axis, dim in sides:
        size, length = (lax.axis_size(axis), shard.shape[dim])
        up = [(i, (i + 1) % size) for i in range(size)]
        down = [(j, i) for i, j in up]
        last = lax.slice_in_dim(shard, length - width, length, axis=dim)
        initial = lax.slice_in_dim(shard, 0, width, axis=dim)
        before = lax.ppermute(last, axis, up)
        after = lax.ppermute(initial, axis, down)
        shard = jnp.concatenate([before, shard, after], axis=dim)
    return shard


def pad_field(values, seam_table):
    channels, faces_dev, stripe_rows, face_side = values.shape
    tile_count = lax.axis_size("tile")
    stripe = lax.axis_index("tile")
    face_group = lax.axis_index("face")
    rimmed = extended(values, (("tile", 2),), 1)
    edge_rows = jnp.stack([values[:, :, 0, :], rimmed[:, :, 0, :]], axis=2)
    edge_pieces = edge_rows.reshape(channels, faces_dev, 2, tile_count, stripe_rows)
    received = lax.all_to_all(edge_pieces, "tile", split_axis=3, concat_axis=3, tiled=True)
    row_part = received[:, :, :, 0, :]
    row_start = stripe * stripe_rows
    col_part = jnp.stack([values[:, :, :, 0], values[:, :, :, face_side - 1]], axis=2)
    seam_piece = jnp.concatenate([row_part, col_part], axis=2)
    seam_piece = jnp.transpose(seam_piece, (1, 2, 0, 3)).reshape(
        1, faces_dev, 4, channels * stripe_rows
    )
    own_sides = lax.dynamic_slice_in_dim(seam_table, face_group * (faces_dev * 4), faces_dev * 4, 0)
    gathered = lax.all_gather(seam_piece, ("face", "tile"), axis=0, tiled=True)
    group_count = gathered.shape[0] // tile_count
    strip_table = gathered.reshape(group_count, tile_count, faces_dev, 4, channels, stripe_rows)
    strip_table = jnp.transpose(strip_table, (0, 2, 3, 4, 1, 5)).reshape(
        group_count * faces_dev * 4, channels, face_side
    )
    strips = jnp.take(strip_table, own_sides[:, 0], axis=0)
    strips = jnp.where(own_sides[:, 1][:, None, None] == 1, strips[:, :, ::-1], strips)
    strips = jnp.transpose(strips.reshape(faces_dev, 4, channels, face_side), (2, 0, 1, 3))
    upper_row = jnp.where(stripe == 0, strips[:, :, 0, :], rimmed[:, :, 0, :])
    bottom = jnp.where(
        stripe == tile_count - 1, strips[:, :, 1, :], rimmed[:, :, stripe_rows + 1, :]
    )
    middle = jnp.concatenate([upper_row[:, :, None, :], values, bottom[:, :, None, :]], axis=2)
    zero_cells = jnp.zeros((channels, faces_dev, 2, 1), values.dtype)
    columns = jnp.concatenate([zero_cells, strips[:, :, 2:, :], zero_cells], axis=3)
    columns = lax.dynamic_slice_in_dim(columns, row_start, stripe_rows + 2, 3)
    return jnp.concatenate([columns[:, :, 0, :, None], middle, columns[:, :, 1, :, None]], axis=3)


def convolve(padded, weight):
    channels, faces_dev, rows_two, side_two = padded.shape
    stripe_rows = rows_two - 2
    face_side = side_two - 2
    planes = []
    for face_index in range(faces_dev):
        summed = jnp.zeros((weight.shape[1], stripe_rows * face_side), jnp.float32)
        for row_shift in range(3):
            tap_rows = jnp.concatenate(
                [
                    padded[
                        :,
                        face_index,
                        row_shift : row_shift + stripe_rows,
                        col_shift : col_shift + face_side,
                    ]
                    for col_shift in range(3)
                ],
                axis=0,
            )
            summed = summed + jnp.dot(
                weight[row_shift],
                tap_rows.reshape(3 * channels, stripe_rows * face_side),
                preferred_element_type=jnp.float32,
            )
        planes.append(jax.nn.gelu(summed).astype(jnp.bfloat16).reshape(-1, stripe_rows, face_side))
    return jnp.stack(planes, axis=1)


def upsample(values):
    return jnp.repeat(jnp.repeat(values, 2, axis=2), 2, axis=3)


def ocean_update(held_state, arrived_flux, ocean_in, ocean_out):
    stacked = jnp.concatenate([held_state, arrived_flux.astype(jnp.float32)], axis=1)
    hidden = jax.nn.gelu(
        jnp.einsum("hc,ncs->nhs", ocean_in, stacked, precision=lax.Precision.HIGHEST)
    )
    sea_now = held_state[:, 0] + jnp.einsum(
        "h,nhs->ns", ocean_out, hidden, precision=lax.Precision.HIGHEST
    )
    return jnp.stack([sea_now, held_state[:, 0]], axis=1)


def ocean_blocks(held_state, arrived_flux, ocean_in, ocean_out, block_count):
    slot_count, state_ch, face_side = held_state.shape
    capacity = slot_count // block_count
    held_split = held_state.reshape(block_count, capacity, state_ch, face_side)
    flux_split = arrived_flux.reshape(block_count, capacity, arrived_flux.shape[1], face_side)
    stepped = lax.map(
        lambda pair: ocean_update(pair[0], pair[1], ocean_in, ocean_out), (held_split, flux_split)
    )
    return stepped.reshape(slot_count, state_ch, face_side)


def on_device(
    atmos_state,
    land_sea,
    owners,
    seam_table,
    ocean_state,
    conv_input,
    conv_encode,
    conv_coarse,
    conv_decode,
    output_head,
    ocean_in,
    ocean_out,
):
    encoded = convolve(pad_field(atmos_state, seam_table), conv_input)
    skip_level = convolve(pad_field(encoded, seam_table), conv_encode)
    channels, faces_dev, stripe_rows, face_side = skip_level.shape
    pooled = (
        skip_level.astype(jnp.float32)
        .reshape(channels, faces_dev, stripe_rows // 2, 2, face_side // 2, 2)
        .mean(axis=(3, 5))
        .astype(jnp.bfloat16)
    )
    coarse_out = convolve(pad_field(pooled, seam_table), conv_coarse)
    coarse_pad = upsample(pad_field(coarse_out, seam_table))[
        :, :, 1 : stripe_rows + 3, 1 : face_side + 3
    ]
    padded = jnp.concatenate([pad_field(skip_level, seam_table), coarse_pad], axis=0)
    decoded = convolve(padded, conv_decode)
    head_out = jnp.dot(
        output_head, decoded.reshape(channels, -1), preferred_element_type=jnp.float32
    )
    head_out = head_out.reshape(-1, faces_dev, stripe_rows, face_side)
    predicted = atmos_state[:OUT_VARS].astype(jnp.float32) + head_out[:OUT_VARS]
    is_ocean = land_sea == 1
    fluxes = jnp.where(is_ocean[None], head_out[OUT_VARS:], 0.0).astype(jnp.bfloat16)
    flux_tiles = jnp.transpose(fluxes, (1, 2, 0, 3)).reshape(
        faces_dev * stripe_rows, FLUX_CH * face_side
    )
    tile_count = lax.axis_size("tile")
    owner_ids = owners[:, 0]
    owner_hits = (owner_ids[:, None] == jnp.arange(tile_count)[None, :]).astype(jnp.int32)
    slot_rank = jnp.sum((jnp.cumsum(owner_hits, axis=0) - 1) * owner_hits, axis=1)
    slot_count = ocean_state.shape[2]
    capacity = slot_count // tile_count
    slot_index = owner_ids * capacity + slot_rank
    selector = (jnp.arange(slot_count)[:, None] == slot_index[None, :]).astype(jnp.bfloat16)
    outgoing = jnp.dot(selector, flux_tiles, preferred_element_type=jnp.float32).astype(
        jnp.bfloat16
    )
    outgoing = outgoing.reshape(tile_count, capacity, FLUX_CH, face_side)
    held_state = ocean_state[0, 0]
    arrived = lax.all_to_all(outgoing, "tile", split_axis=0, concat_axis=0, tiled=True)
    renewed = ocean_blocks(
        held_state, arrived.reshape(slot_count, FLUX_CH, face_side), ocean_in, ocean_out, tile_count
    )
    sea_back = renewed[:, 0].astype(jnp.bfloat16).reshape(tile_count, capacity, face_side)
    sea_slots = lax.all_to_all(sea_back, "tile", split_axis=0, concat_axis=0, tiled=True)
    sea_tiles = jnp.dot(
        selector.T, sea_slots.reshape(slot_count, face_side), preferred_element_type=jnp.float32
    )
    sea_temp = sea_tiles.reshape(faces_dev, stripe_rows, face_side)
    surface = jnp.where(is_ocean, sea_temp, predicted[0])
    atmos_next = jnp.concatenate([surface[None], predicted[1:]], axis=0).astype(jnp.bfloat16)
    return (atmos_next, renewed.reshape(1, 1, slot_count, OCEAN_CH, face_side))


GROUP = 16
LANES = 128
VMEM = pltpu.VMEM
BF = jnp.bfloat16
F32 = jnp.float32
NT = (((1,), (1,)), ((), ()))


def mm(a, b):
    return jnp.dot(a, b, preferred_element_type=F32)


def mm_nt(a, b):
    return lax.dot_general(a, b, NT, preferred_element_type=F32)


def iota(shape, dim):
    return lax.broadcasted_iota(jnp.int32, shape, dim)


def smooth(x):
    inner = x * (0.7978845608028654 + 0.03567740813636141 * (x * x))
    half = 0.5 * x
    return half * jnp.tanh(inner) + half


class Field:
    def __init__(self, faces, rows, chans, side, tiles):
        self.faces, self.rows, self.chans, self.side, self.tiles = faces, rows, chans, side, tiles
        self.per = LANES // chans
        self.groups = faces // self.per
        self.span = rows + 2
        self.extra = self.groups * self.span
        used = max(self.extra + 2 * self.groups, 2 * self.groups * rows)
        self.chunk = used + (-used) % 16

    def main(self):
        return jax.ShapeDtypeStruct((self.faces, self.rows, self.chans, self.side), BF)

    def edges(self, more=0):
        edge = jax.ShapeDtypeStruct((self.faces, self.chans, self.side + more), BF)
        return [edge, edge]

    def sends(self):
        return [
            jax.ShapeDtypeStruct((2 * self.faces * 8, self.chans), BF),
            jax.ShapeDtypeStruct((self.tiles, self.chunk, LANES), BF),
        ]

    def send_scratch(self):
        return [
            pltpu.VMEM((2, self.faces, 8, self.chans), F32),
            pltpu.VMEM((self.tiles, self.chunk, LANES), F32),
            pltpu.VMEM((self.side + 8, LANES), F32),
            pltpu.VMEM((16, self.rows * LANES), BF),
            pltpu.VMEM((2, self.side, self.side), BF),
        ]

    def halo_scratch(self):
        return [
            pltpu.VMEM((6, self.faces, GROUP, self.chans), F32),
            pltpu.VMEM((2, GROUP * GROUP, self.chans), F32),
            pltpu.VMEM((self.faces, self.chans, self.side), BF),
            pltpu.VMEM((self.faces, self.chans, self.side), BF),
            pltpu.VMEM((2, self.faces, self.chans, self.side), BF),
            pltpu.VMEM((self.tiles, self.chunk, LANES), F32),
            pltpu.VMEM((2, self.faces, 8, self.chans), F32),
            pltpu.VMEM((2, self.side, self.side), BF),
        ]


def fill_flips(flips):
    size = flips.shape[1]
    row, col = iota((size, size), 0), iota((size, size), 1)
    flips[0] = (row == col).astype(F32).astype(BF)
    flips[1] = (row + col == size - 1).astype(F32).astype(BF)


def end_picker(side):
    row, col = iota((16, side), 0), iota((16, side), 1)
    return (((row == 0) & (col == 0)) | ((row == 1) & (col == side - 1))).astype(F32).astype(BF)


def column_picker(fld):
    length = fld.rows * LANES
    row, col = iota((16, length), 0), iota((16, length), 1)
    return (col == (row & 7) * LANES + (row >> 3) * (LANES - 1)).astype(F32).astype(BF)


def near_ends(cells):
    if cells.shape[1] > LANES:
        lane = iota((cells.shape[0], LANES), 1)
        cells = jnp.where(lane < LANES // 2, cells[:, :LANES], cells[:, cells.shape[1] - LANES :])
    return cells.astype(BF)


def keep_columns(picker, face_rows, f, cols):
    picked = mm_nt(picker, jnp.concatenate(face_rows, axis=1))
    cols[0, f] = picked[:8]
    cols[1, f] = picked[8:]


def pack_sends(fld, stripe, tab, top, bot, off, ec_out, send_out, cols, stage, strip, picker, flips):
    last, rows, chans, groups, per = fld.tiles - 1, fld.rows, fld.chans, fld.groups, fld.per
    held = cols[...]
    ec_out[...] = held.reshape(2 * fld.faces * 8, chans).astype(BF)
    paired = held.reshape(2, groups, per, 8, chans)
    packed = jnp.concatenate([paired[:, :, j] for j in range(per)], axis=3)
    across = packed[:, :, :rows].reshape(2 * groups * rows, LANES)
    initial = packed[:, :, 0].reshape(2 * groups, LANES)
    final = packed[:, :, rows - 1].reshape(2 * groups, LANES)
    pieces = []
    for q in range(2):
        for g in range(fld.faces):
            p = tab[4 * g + q, 0]
            pieces.append(cols[jnp.maximum((p & 3) - 2, 0), p >> 2][:rows])
    merged = [jnp.concatenate(pieces[n : n + per], axis=1) for n in range(0, len(pieces), per)]
    stage[...] = jnp.zeros_like(stage)
    for q in range(2):
        for i in range(groups):
            stage[q * last, i * fld.span + 1 : i * fld.span + 1 + rows, :] = merged[q * groups + i]

    def lanes(h):
        return slice((h % per) * chans, (h % per + 1) * chans)

    @pl.when((stripe == 0) | (stripe == last))
    def _():
        q = jnp.where(stripe == 0, 0, 1)
        fill_flips(flips)
        for i in range(groups):
            turned = []
            for h in range(i * per, (i + 1) * per):
                upper = top[h, :, off : off + fld.side].astype(F32)
                lower = bot[h, :, off : off + fld.side].astype(F32)
                cells = jnp.where(q == 0, upper, lower).astype(BF)
                turned.append(mm_nt(flips[tab[4 * h + q, 1]], cells))
            strip[0:8] = jnp.zeros((8, LANES), F32)
            strip[fld.side : fld.side + 8] = jnp.zeros((8, LANES), F32)
            strip[1 : fld.side + 1, :] = jnp.concatenate(turned, axis=1)
            for d in range(1, last, 10):
                here = range(d, min(d + 10, last))
                taken = [strip[e * rows : e * rows + fld.span, :] for e in here]
                for e, piece in zip(here, taken):
                    stage[e, i * fld.span : (i + 1) * fld.span, :] = piece

    stage[last - stripe, : 2 * groups * rows, :] = across

    @pl.when(stripe < last)
    def _():
        stage[last - 1 - stripe, fld.extra : fld.extra + 2 * groups, :] = final

    @pl.when(stripe > 0)
    def _():
        stage[last + 1 - stripe, fld.extra : fld.extra + 2 * groups, :] = initial

    send_out[...] = stage[...].astype(BF)


def gather_halos(fld, stripe, tab, top, bot, up, dn, off, ec, recv, cand, cols, above, below, pair, got, mirror, flips):
    faces, rows, chans, side, tiles = fld.faces, fld.rows, fld.chans, fld.side, fld.tiles
    last = tiles - 1
    groups = fld.groups
    got[...] = recv[...].astype(F32)
    own = ec[...].astype(F32).reshape(2, faces, 8, chans)
    row, col = iota((groups * rows, groups * rows), 0), iota((groups * rows, groups * rows), 1)
    turn = ((row // rows == col // rows) & (row % rows + col % rows == rows - 1)).astype(F32).astype(BF)
    prow, pcol = iota((16, side), 0), iota((16, side), 1)

    def lanes(h):
        return slice((h % fld.per) * chans, (h % fld.per + 1) * chans)

    here = slice(off, off + side)
    above[...] = up[:, :, here]
    below[...] = dn[:, :, here]
    over = mm_nt(end_picker(LANES), near_ends(above[...].reshape(faces * chans, side).astype(F32)))
    under = mm_nt(end_picker(LANES), near_ends(below[...].reshape(faces * chans, side).astype(F32)))
    heads = [got[q * last, : fld.extra, :] for q in range(2)]
    before = got[jnp.minimum(last + 1 - stripe, last), fld.extra : fld.extra + 2 * groups, :]
    after = got[jnp.maximum(last - 1 - stripe, 0), fld.extra : fld.extra + 2 * groups, :]
    for s in range(2):
        across = got[last - stripe, s * groups * rows : (s + 1) * groups * rows, :]
        turned = mm(turn, across.astype(BF))
        for h in range(faces):
            i = h // fld.per
            cand[2 + s, h, 0:1] = over[s : s + 1, h * chans : (h + 1) * chans]
            cand[2 + s, h, rows + 1 : rows + 2] = under[s : s + 1, h * chans : (h + 1) * chans]
            cand[2 + s, h, 1 : rows + 1] = own[s, h, :rows]
            mirror[s, h, :rows] = across[i * rows : (i + 1) * rows, lanes(h)]
            cand[4 + s, h, 0:1] = before[s * groups + i : s * groups + i + 1, lanes(h)]
            cand[4 + s, h, rows + 1 : rows + 2] = after[s * groups + i : s * groups + i + 1, lanes(h)]
            cand[4 + s, h, 1 : rows + 1] = turned[i * rows : (i + 1) * rows, lanes(h)]
    at_edge = (stripe == 0) | (stripe == last)

    @pl.when(jnp.logical_not(at_edge))
    def _():
        for q in range(2):
            for h in range(faces):
                i = h // fld.per
                cand[q, h, 0 : fld.span] = heads[q][i * fld.span : (i + 1) * fld.span, lanes(h)]

    @pl.when(at_edge)
    def _():
        q = jnp.where(stripe == 0, 0, 1)
        fill_flips(flips)
        for h in range(faces):
            pair[0, h] = jnp.where(q == 0, top[h, :, here].astype(F32), below[h].astype(F32)).astype(BF)
            pair[1, h] = jnp.where(q == 0, above[h].astype(F32), bot[h, :, here].astype(F32)).astype(BF)
        place = stripe * rows - 1 + prow
        inside = (place >= 0) & (place < side)
        windows = []
        for s in range(2):
            for h in range(faces):
                want = jnp.where(tab[4 * h + s, 1] == 1, side - 1 - place, place)
                window = ((pcol == want) & inside).astype(F32).astype(BF)
                windows.append(mm_nt(window, pair[s, h]))
        pieces = []
        for g in range(faces):
            p = tab[4 * g + q, 0]
            pieces.append(mirror[jnp.maximum((p & 3) - 2, 0), p >> 2][:rows])
        for s in range(2):
            for h in range(faces):
                cand[s, h] = windows[s * faces + h]
        for i in range(groups):
            merged = jnp.concatenate(pieces[i * fld.per : (i + 1) * fld.per], axis=1)
            got[last - stripe, i * fld.span + 1 : i * fld.span + 1 + rows, :] = merged
        for i in range(groups):
            lined = jnp.concatenate(
                [got[d, i * fld.span + 1 : i * fld.span + 1 + rows, :] for d in range(tiles)], axis=0
            )
            lined = jnp.transpose(lined)
            for j in range(fld.per):
                g = i * fld.per + j
                p = tab[4 * g + q, 0]
                kind, h = p & 3, p >> 2
                near = pair[jnp.minimum(kind, 1), h].astype(F32)
                far = lined[j * chans : (j + 1) * chans]
                cells = jnp.where(kind < 2, near, far).astype(BF)
                placed = mm(cells, flips[tab[4 * g + q, 1]]).astype(BF)

                @pl.when(q == 0)
                def _():
                    above[g] = placed

                @pl.when(q == 1)
                def _():
                    below[g] = placed

    slot = iota((GROUP, chans), 0)
    live = (slot < fld.span) & jnp.logical_not(
        ((slot == 0) & (stripe == 0)) | ((slot == rows + 1) & (stripe == last))
    )
    for s in range(2):
        taken = []
        for g in range(faces):
            p = tab[4 * g + 2 + s, 0]
            kind, h = p & 3, p >> 2
            which = jnp.where((kind >= 2) & (tab[4 * g + 2 + s, 1] == 1), kind + 2, kind)
            taken.append(jnp.where(live, cand[which, h], 0.0))
        taken.append(jnp.zeros(((GROUP - faces) * GROUP, chans), F32))
        cols[s] = jnp.concatenate(taken, axis=0)


def column_terms(side_weight, cols, out_ch):
    terms = []
    for s in range(2):
        part = mm_nt(side_weight[s], cols[s])
        size = part.shape[1]
        terms.append(
            part[out_ch : 2 * out_ch]
            + pltpu.roll(part[:out_ch], 1, 1)
            + pltpu.roll(part[2 * out_ch :], size - 1, 1)
        )
    return terms


def face_terms(terms, face_index):
    size = terms[0].shape[1]
    shift = lax.rem(2 * size - GROUP * face_index - 1, size)
    return [pltpu.roll(term, shift, 1)[:, :LANES] for term in terms]


def conv_row(weight, stacked, terms, r, out_ch):
    z = mm(weight, stacked)
    side = z.shape[1]
    left, right = pltpu.roll(z[:out_ch], 1, 1), pltpu.roll(z[2 * out_ch :], side - 1, 1)
    lane = iota((out_ch, LANES), 1)
    first = terms[0] if r == 0 else pltpu.roll(terms[0], LANES - r, 1)
    final = pltpu.roll(terms[1], LANES - 1 - r, 1)
    head = jnp.where(lane == 0, first, left[:, :LANES])
    tail = jnp.where(lane == LANES - 1, final, right[:, side - LANES :])
    if side > LANES:
        left = jnp.concatenate([head, left[:, LANES:]], axis=1)
        right = jnp.concatenate([right[:, : side - LANES], tail], axis=1)
    else:
        left, right = head, tail
    return smooth(z[out_ch : 2 * out_ch] + left + right)


def row_stack(x, above, below, k, f, rows):
    lines = [above[f]] + [x[k, r] for r in range(rows)] + [below[f]]
    return lambda r: lines[r : r + 3]


def prep_kernel(fld, stripe_ref, tab, atmos, perm, x_out, top, bot, ec_out, send_out, *sends):
    stripe, step = stripe_ref[0], pl.program_id(0)
    batch = x_out.shape[0]

    @pl.when(step == 0)
    def _():
        sends[3][...] = column_picker(fld)

    def one_face(k, carry):
        f = step * batch + k
        block = atmos[:, k].astype(F32).reshape(fld.chans * fld.rows, fld.side).astype(BF)
        moved = mm(perm[...], block)
        lines = [moved[r * fld.chans : (r + 1) * fld.chans] for r in range(fld.rows)]
        for r in range(fld.rows):
            x_out[k, r] = lines[r].astype(BF)
        top[f] = lines[0].astype(BF)
        bot[f] = lines[-1].astype(BF)
        keep_columns(sends[3][...], [near_ends(cells) for cells in lines], f, sends[0])
        return carry

    lax.fori_loop(0, batch, one_face, 0)

    @pl.when(step == fld.faces // batch - 1)
    def _():
        pack_sends(fld, stripe, tab, top, bot, 0, ec_out, send_out, *sends)


def level_kernel(fld, out_fld, low, off, stripe_ref, tab, x, old_top, old_bot, up, dn, ec, recv, weight, side_weight, *refs):
    stripe, step = stripe_ref[0], pl.program_id(0)
    if low is None:
        outs, sends, halos = refs[:5], refs[5:10], refs[10:]
        x_out, top, bot, ec_out, send_out = outs
    else:
        pool, outs, sends, low_sends, halos = refs[0], refs[1:9], refs[9:14], refs[14:19], refs[19:]
        x_out, y_out, top, bot, ec_out, send_out, low_ec, low_send = outs
    *halos, ends_ref = halos
    batch = x_out.shape[0]
    _, cols, above, below = halos[:4]
    side = fld.side

    @pl.when(step == 0)
    def _():
        gather_halos(fld, stripe, tab, old_top, old_bot, up, dn, off, ec, recv, *halos)
        terms = column_terms(side_weight, [cols[0].astype(BF), cols[1].astype(BF)], out_fld.chans)
        ends_ref[0], ends_ref[1] = terms
        sends[3][...] = column_picker(out_fld)
        if low is not None:
            low_sends[3][...] = column_picker(low)

    def one_face(k, carry):
        f = step * batch + k
        lines = row_stack(x, above, below, k, f, fld.rows)
        ends = face_terms([ends_ref[0], ends_ref[1]], f)
        made, pooled, near = [], [], []
        for r in range(fld.rows):
            cells = conv_row(weight[...], jnp.concatenate(lines(r), axis=0), ends, r, out_fld.chans)
            near.append(near_ends(cells))
            cells = cells.astype(BF)
            x_out[k, r] = cells
            made.append(cells)
            if low is not None and r % 2 == 1:
                mean = (mm(made[r - 1], pool[...]) + mm(cells, pool[...])).astype(BF)
                y_out[k, r // 2] = mean
                pooled.append(mean)
        top[f, :, :side] = made[0]
        bot[f, :, :side] = made[-1]
        keep_columns(sends[3][...], near, f, sends[0])
        if low is not None:
            top[f, :, side:] = pooled[0]
            bot[f, :, side:] = pooled[-1]
            keep_columns(low_sends[3][...], pooled, f, low_sends[0])
        return carry

    lax.fori_loop(0, batch, one_face, 0)

    @pl.when(step == fld.faces // batch - 1)
    def _():
        if low is not None:
            pack_sends(low, stripe, tab, top, bot, side, low_ec, low_send, *low_sends)
        pack_sends(out_fld, stripe, tab, top, bot, 0, ec_out, send_out, *sends)


def decode_kernel(fld, low, out_ch, vars_out, stripe_ref, tab, x, top, bot, up, dn, ec, recv, y, low_top, low_bot, yup, ydn, yec, yrecv, weight, side_weight, spread, head, atmos, land, row_key, col_key, pred_out, flux_out, *refs):
    halos, low_halos, flux, ends_ref = refs[:8], refs[8:16], refs[16], refs[17]
    stripe, step = stripe_ref[0], pl.program_id(0)
    _, cols, above, below = halos[:4]
    _, low_cols, low_above, low_below = low_halos[:4]
    batch = x.shape[0]

    @pl.when(step == 0)
    def _():
        gather_halos(low, stripe, tab, low_top, low_bot, yup, ydn, 0, yec, yrecv, *low_halos)
        gather_halos(fld, stripe, tab, top, bot, up, dn, 0, ec, recv, *halos)
        size = GROUP * GROUP
        row, col = iota((size, size), 0), iota((size, size), 1)
        widen = (col == (row // GROUP) * GROUP + (row % GROUP + 1) // 2).astype(F32).astype(BF)
        joined = []
        for s in range(2):
            wide = mm(widen, low_cols[s].astype(BF))
            joined.append(jnp.concatenate([cols[s], wide], axis=1).astype(BF))
        ends_ref[0], ends_ref[1] = column_terms(side_weight, joined, out_ch)

    def one_face(k, carry):
        f = step * batch + k
        lines = row_stack(x, above, below, k, f, fld.rows)
        ends = face_terms([ends_ref[0], ends_ref[1]], f)
        low_lines = [low_above[f]] + [y[k, r] for r in range(low.rows)] + [low_below[f]]
        wide = [mm(cells, spread[...]).astype(BF) for cells in low_lines]
        made = []
        for r in range(fld.rows):
            picked = [wide[(r + a + 1) // 2] for a in range(3)]
            made.append(
                conv_row(weight[...], jnp.concatenate(lines(r) + picked, axis=0), ends, r, out_ch).astype(BF)
            )
        result = mm(head[...], jnp.concatenate(made, axis=0)).reshape(-1, fld.rows, fld.side)
        pred_out[:, k] = (atmos[:, k].astype(F32) + result[:vars_out]).astype(BF)
        flux[:, f] = jnp.where((land[k] == 1)[None], result[vars_out:], 0.0)
        return carry

    lax.fori_loop(0, batch, one_face, 0)

    @pl.when(step == fld.faces // batch - 1)
    def _():
        chosen = (row_key[...] == col_key[...]).astype(F32).astype(BF)
        tiles = flux[...].reshape(-1, fld.side).astype(BF)
        flux_out[...] = mm(chosen, tiles).astype(BF).reshape(flux_out.shape)


def ocean_kernel(cap, recv, state, into, out_weight, sea_out, back_out):
    tiles, _, side = recv.shape

    hidden = into.shape[0] // cap
    unit = 2 if tiles % 2 == 0 else 1

    def one_source(t):
        flux = recv[t].astype(F32)
        pad = (-flux.shape[0]) % 16
        flux = jnp.concatenate([flux, jnp.zeros((pad, side), F32)], axis=0).astype(BF)
        held = state[t]
        high = held.astype(BF)
        low = (held - high.astype(F32)).astype(BF)
        stacked = jnp.concatenate([flux, flux, high, high, low], axis=0)
        width = jnp.concatenate([out_weight[...]] * (side // LANES), axis=1)
        drift = []
        for k in range(cap):
            grown = smooth(mm(into[k * hidden : (k + 1) * hidden, :], stacked)) * width
            drift.append(grown.sum(axis=0, keepdims=True))
        drift.append(jnp.zeros((8 - cap, side), F32))
        return held[:8] + jnp.concatenate(drift, axis=0)

    def some_sources(n, carry):
        made = [one_source(n * unit + u) for u in range(unit)]
        for u, sea in enumerate(made):
            sea_out[n * unit + u] = sea
            back_out[n * unit + u] = sea.astype(BF)
        return carry

    lax.fori_loop(0, tiles // unit, some_sources, 0)


def surface_kernel(back, key, land, pred, out):
    faces, rows, side = land.shape
    slots = back[...].astype(F32).reshape(-1, side).astype(BF)
    chosen = (key[...] == iota((faces * rows, slots.shape[0]), 1)).astype(F32).astype(BF)
    sea = mm(chosen, slots).reshape(faces, rows, side)
    out[0] = jnp.where(land[...] == 1, sea, pred[0].astype(F32)).astype(BF)


def call(kernel, outs, ins, scratch, flops, smem=0, steps=1, specs=None, aliases=None, out_specs=None, name=None):
    whole = pl.BlockSpec(memory_space=pltpu.VMEM)
    in_specs = [pl.BlockSpec(memory_space=pltpu.SMEM)] * smem + [whole] * (len(ins) - smem)
    for position, spec in (specs or {}).items():
        in_specs[position] = spec
    grid = {"grid": (steps,)} if specs else {}
    moved = sum(int(np.prod(a.shape)) * a.dtype.itemsize for a in list(ins) + list(outs))
    return pl.pallas_call(
        kernel,
        out_shape=outs,
        **grid,
        in_specs=in_specs,
        out_specs=[(out_specs or {}).get(n, whole) for n in range(len(outs))],
        scratch_shapes=scratch,
        input_output_aliases=aliases or {},
        compiler_params=pltpu.CompilerParams(vmem_limit_bytes=56 * 1024 * 1024),
        cost_estimate=pl.CostEstimate(flops=int(flops), bytes_accessed=int(moved), transcendentals=0),
        name=name,
    )(*ins)


def swap_rows(top, bot):
    tiles = lax.axis_size("tile")
    ring = [(i, (i + 1) % tiles) for i in range(tiles)]
    up = lax.ppermute(bot, "tile", ring)
    return up, lax.ppermute(top, "tile", [(j, i) for i, j in ring])


def swap_chunks(chunks):
    return lax.all_to_all(chunks, "tile", split_axis=0, concat_axis=0, tiled=True)


def packed_weight(weight, chans):
    taps, out_ch, _ = weight.shape
    split = weight.reshape(taps, out_ch, taps, chans)
    body = jnp.transpose(split, (2, 1, 0, 3)).reshape(taps * out_ch, taps * chans)
    sides = jnp.stack([split[:, :, 0], split[:, :, 2]]).reshape(2, taps * out_ch, chans)
    return body, sides


def on_one_group(
    atmos_state,
    land_sea,
    owners,
    seam_table,
    ocean_state,
    conv_input,
    conv_encode,
    conv_coarse,
    conv_decode,
    output_head,
    ocean_in,
    ocean_out,
):
    in_ch, faces, rows, side = atmos_state.shape
    tiles = lax.axis_size("tile")
    width = conv_input.shape[1]
    stripe = lax.axis_index("tile").astype(jnp.int32).reshape(1)
    entry = Field(faces, rows, in_ch, side, tiles)
    full = Field(faces, rows, width, side, tiles)
    low = Field(faces, rows // 2, width, side // 2, tiles)
    cells = faces * rows * side

    order = np.arange(in_ch * rows)
    perm = np.zeros((in_ch * rows, in_ch * rows), np.float32)
    perm[order, (order % in_ch) * rows + order // in_ch] = 1.0
    spread = np.zeros((side // 2, side), np.float32)
    spread[np.arange(side) // 2, np.arange(side)] = 1.0
    perm, pool = jnp.asarray(perm, BF), jnp.asarray(0.25 * spread.T, BF)
    spread = jnp.asarray(spread, BF)

    def some(batch, shape, dim=0):
        block = tuple(batch if n == dim else size for n, size in enumerate(shape))
        return pl.BlockSpec(block, lambda i: tuple(i if n == dim else 0 for n in range(len(shape))))

    few, many = (3 if faces % 3 == 0 else 1), faces
    half = many // 2 if many % 2 == 0 else many
    ends = [pltpu.VMEM((2, width, GROUP * GROUP), F32)]
    x0, top, bot, ec, send = call(
        functools.partial(prep_kernel, entry),
        [entry.main()] + entry.edges() + entry.sends(),
        (stripe, seam_table, atmos_state, perm),
        entry.send_scratch(),
        2 * cells * in_ch * in_ch * rows,
        smem=2,
        steps=faces // half,
        specs={2: some(half, atmos_state.shape, 1)},
        out_specs={0: some(half, entry.main().shape)},
        name="prep",
    )
    got = swap_chunks(send)
    up, dn = swap_rows(top, bot)
    x1, top, bot, ec, send = call(
        functools.partial(level_kernel, entry, full, None, 0),
        [full.main()] + full.edges() + full.sends(),
        (stripe, seam_table, x0, top, bot, up, dn, ec, got) + packed_weight(conv_input, in_ch),
        full.send_scratch() + entry.halo_scratch() + ends,
        2 * cells * 9 * in_ch * width,
        smem=2,
        steps=faces // few,
        specs={2: some(few, x0.shape)},
        out_specs={0: some(few, full.main().shape)},
        name="conv_in",
    )
    got = swap_chunks(send)
    up, dn = swap_rows(top, bot)
    x2, y0, top, bot, ec, send, low_ec, low_send = call(
        functools.partial(level_kernel, full, full, low, 0),
        [full.main(), low.main()] + full.edges(side // 2) + full.sends() + low.sends(),
        (stripe, seam_table, x1, top, bot, up, dn, ec, got) + packed_weight(conv_encode, width) + (pool,),
        full.send_scratch() + low.send_scratch() + full.halo_scratch() + ends,
        2 * cells * 9 * width * width,
        smem=2,
        steps=faces // few,
        specs={2: some(few, x1.shape)},
        out_specs={0: some(few, full.main().shape), 1: some(few, low.main().shape)},
        name="encode",
    )
    low_got = swap_chunks(low_send)
    up, dn = swap_rows(top, bot)
    y1, low_top, low_bot, low_ec, low_send = call(
        functools.partial(level_kernel, low, low, None, side),
        [low.main()] + low.edges() + low.sends(),
        (stripe, seam_table, y0, top, bot, up, dn, low_ec, low_got) + packed_weight(conv_coarse, width),
        low.send_scratch() + low.halo_scratch() + ends,
        10e9,
        smem=2,
        steps=faces // many,
        specs={2: some(many, y0.shape)},
        out_specs={0: some(many, low.main().shape)},
        name="coarse",
    )
    low_send, got = lax.optimization_barrier((low_send, swap_chunks(send)))
    low_got = swap_chunks(low_send)
    low_up, low_dn = swap_rows(low_top, low_bot)

    taps = conv_decode.shape[0]
    split = conv_decode.reshape(taps, width, taps, 2, width)
    body = jnp.transpose(split, (2, 1, 3, 0, 4)).reshape(taps * width, 2 * taps * width)
    sides = jnp.stack([split[:, :, 0], split[:, :, 2]]).reshape(2, taps * width, 2 * width)
    heads = output_head.shape[0]
    flux_ch = heads - OUT_VARS
    eye = jnp.eye(rows, dtype=output_head.dtype)
    head = (output_head[:, None, None, :] * eye[None, :, :, None]).reshape(heads * rows, rows * width)

    slot_count = ocean_state.shape[2]
    cap = slot_count // tiles
    owner_ids = owners[:, 0]
    count = owner_ids.shape[0]
    earlier = np.tril(np.ones((count, count), bool), -1)
    rank = jnp.sum((owner_ids[:, None] == owner_ids[None, :]) & earlier, axis=1).astype(jnp.int32)
    slot_index = owner_ids * cap + rank
    col_key = (np.arange(flux_ch, dtype=np.int32)[:, None] * slot_count + slot_index[None, :]).reshape(1, -1)
    row_key = (
        np.arange(flux_ch, dtype=np.int32)[None, :, None] * slot_count
        + np.arange(slot_count, dtype=np.int32).reshape(tiles, 1, cap)
    ).reshape(-1, 1)
    row_key = jnp.asarray(row_key)
    pred, outgoing = call(
        functools.partial(decode_kernel, full, low, width, OUT_VARS),
        [
            jax.ShapeDtypeStruct((OUT_VARS, faces, rows, side), BF),
            jax.ShapeDtypeStruct((tiles, flux_ch * cap, side), BF),
        ],
        (stripe, seam_table, x2, top, bot, up, dn, ec, got)
        + (y1, low_top, low_bot, low_up, low_dn, low_ec, low_got)
        + (body, sides, spread, head, atmos_state, land_sea, row_key, col_key),
        full.halo_scratch()
        + low.halo_scratch()
        + [pltpu.VMEM((flux_ch, faces, rows, side), F32)]
        + ends,
        2 * cells * 18 * width * width,
        smem=2,
        steps=faces // few,
        specs={
            2: some(few, x2.shape),
            9: some(few, y1.shape),
            20: pl.BlockSpec((OUT_VARS, few, rows, side), lambda i: (0, i, 0, 0)),
            21: some(few, land_sea.shape),
        },
        out_specs={0: some(few, (OUT_VARS, faces, rows, side), 1)},
        name="decode",
    )
    arrived = lax.all_to_all(outgoing, "tile", split_axis=0, concat_axis=0, tiled=True)

    held = jnp.transpose(ocean_state[0, 0].reshape(tiles, cap, OCEAN_CH, side), (0, 2, 1, 3))
    state = jnp.pad(held, ((0, 0), (0, 0), (0, 8 - cap), (0, 0))).reshape(tiles, OCEAN_CH * 8, side)
    hidden = ocean_in.shape[0]
    high = ocean_in.astype(BF)
    rest = (ocean_in - high.astype(F32)).astype(BF)
    flux_pad = (-flux_ch * cap) % 16
    each = jnp.eye(cap, dtype=BF)
    slot8 = jnp.eye(cap, 8, dtype=BF)

    def flux_part(weights):
        part = each[:, None, None, :] * weights[None, :, OCEAN_CH:, None]
        return jnp.pad(part.reshape(cap * hidden, flux_ch * cap), ((0, 0), (0, flux_pad)))

    def state_part(weights):
        part = slot8[:, None, None, :] * weights[None, :, :OCEAN_CH, None]
        return part.reshape(cap * hidden, OCEAN_CH * 8)

    into = jnp.concatenate(
        [flux_part(high), flux_part(rest), state_part(high), state_part(rest), state_part(high)], axis=1
    )
    out_weight = jnp.broadcast_to(ocean_out[:, None], (hidden, LANES))
    sea, back = call(
        functools.partial(ocean_kernel, cap),
        [jax.ShapeDtypeStruct((tiles, 8, side), F32), jax.ShapeDtypeStruct((tiles, 8, side), BF)],
        (arrived, state, into, out_weight),
        [],
        2 * slot_count * side * hidden * 8,
        name="ocean",
    )
    returned = lax.all_to_all(back, "tile", split_axis=0, concat_axis=0, tiled=True)
    key = (owner_ids * 8 + rank)[:, None]
    first = pl.BlockSpec((1, faces, rows, side), lambda i: (0, 0, 0, 0))
    (atmos_next,) = call(
        surface_kernel,
        [jax.ShapeDtypeStruct(pred.shape, BF)],
        (returned, key, land_sea, pred),
        [],
        2 * count * tiles * 8 * side,
        specs={3: first},
        out_specs={0: first},
        aliases={3: 0},
        name="surface",
    )
    renewed = jnp.stack([sea[:, :cap], held[:, 0]], axis=2)
    return atmos_next, renewed.reshape(1, 1, slot_count, OCEAN_CH, side)


def fits(mesh):
    return mesh.shape["face"] == 1


def solution(mesh):
    in_specs = (
        P(None, "face", "tile", None),
        P("face", "tile", None),
        P(("face", "tile"), None),
        P(),
        P("face", "tile", None, None, None),
        P(),
        P(),
        P(),
        P(),
        P(),
        P(),
        P(),
    )
    out_specs = (P(None, "face", "tile", None), P("face", "tile", None, None, None))
    return jax.shard_map(
        on_one_group if fits(mesh) else on_device,
        mesh=mesh,
        in_specs=in_specs,
        out_specs=out_specs,
        check_vma=False,
    )
```
